32 devices in a mesh: dp: 8 (over z, y), tensor: 4 (over x, core).
Axes of the slice: x: 2, y: 2, z: 4, core: 2. Of those that a mesh axis runs over, the one named last changes fastest.
Arguments:
- inputs: bfloat16 [4096, 1024], P('dp'), may hold values from -6 to 6
- teacher: bfloat16 [4096, 1024], P('dp'), may hold values from -6 to 6
- lengths: int32 [8], P('dp'), may hold values from 128 to 512, as said below
- expert_ids: int32 [4096, 2], P('dp'), may hold values from 0 to 15, as said below
- route_slots: int32 [4096, 2], P('dp'), may hold values from 0 to 80, as said below
- gain_attn: float32 [1024], replicated, may hold values from 0.5 to 1.5
- w_qkv: bfloat16 [3, 1024, 1024], P(None, None, 'tensor'), may hold values from -0.09375 to 0.09375
- w_out: bfloat16 [1024, 1024], P('tensor'), may hold values from -0.5 to 0.5
- rel_table: float32 [32, 16], P(None, 'tensor'), may hold values from -4 to 4
- gain_moe: float32 [1024], replicated, may hold values from 0.5 to 1.5
- w_router: bfloat16 [1024, 16], replicated, may hold values from -0.09375 to 0.09375
- w_gate_up: bfloat16 [16, 2, 1024, 2816], P('dp', None, None, 'tensor'), may hold values from -0.1875 to 0.1875
- w_down: bfloat16 [16, 2816, 1024], P('dp', 'tensor'), may hold values from -0.21875 to 0.21875
Outputs:
- block_out: float32 [4096, 1024], P('dp', 'tensor')
- loss: float32 [], replicated
- input_grad: float32 [4096, 1024], P('dp', 'tensor')
- gain_attn_grad: float32 [1024], replicated
- qkv_grad: float32 [3, 1024, 1024], P(None, None, 'tensor')
- out_proj_grad: float32 [1024, 1024], P('tensor')
- table_grad: float32 [32, 16], P(None, 'tensor')
- gain_moe_grad: float32 [1024], replicated
- router_grad: float32 [1024, 16], replicated
- gate_up_grad: float32 [16, 2, 1024, 2816], P('dp', None, None, 'tensor')
- down_grad: float32 [16, 2816, 1024], P('dp', 'tensor')
The draws below stay inside these ranges and needn't reach their ends.
Inputs may be any that keep to these rules, and one draw needn't show every extreme that they name: The first sequence has 128 valid tokens and the last 512; between them lengths grow with the sequence's index, each shortened at random. `expert_ids`: a token's two experts differ. `route_slots`: within the tokens of one index of dp, first routes take slots in token order before second routes, and each expert's slots are 0, 1, 2 and so on; 80 marks a route that is dropped or whose token is padding; some expert receives 80 routes from every index of dp.
All inputs are finite; a program needn't handle non-finite values.
Results may differ from the reference program's by a relative error of at most 0.018.
The reference program's roundings to bfloat16 on the way count: a program that leaves them out, or rounds other values in their place, can miss the bound.
Values may be sent and summed in bfloat16 or wider, within the bound.
A program may use at most 320 MiB of HBM per device.

```python
import jax
import jax.numpy as jnp
from jax import lax

D = 1024
HEADS = 16
HEAD_DIM = 64
FF = 2816
BUCKETS = 32
SEQ_LEN = 512
SEQ_DEV = 1
MIN_LEN = 128
EXPERTS = 16
TOK_DEV = 512
TOKENS = 4096
SEQS = 8
CAP = 80
N_DP = 8
N_TENSOR = 4


def routing_tables(key):
    group_count = TOKENS // TOK_DEV
    seq_index = jnp.arange(SEQS, dtype=jnp.int32)
    base_length = MIN_LEN + (SEQ_LEN - MIN_LEN) * seq_index // max(SEQS - 1, 1)
    shorten = jax.random.randint(jax.random.fold_in(key, 11), (SEQS,), 0, (SEQ_LEN - MIN_LEN) // 4 + 1)
    interior = ((seq_index > 0) & (seq_index < SEQS - 1)).astype(jnp.int32)
    seq_lengths = jnp.maximum(base_length - shorten * interior, MIN_LEN).astype(jnp.int32)
    token_index = jnp.arange(TOKENS, dtype=jnp.int32)
    position = token_index % SEQ_LEN
    favored = jax.random.randint(jax.random.fold_in(key, 12), (), 0, EXPERTS)
    forced = position < (CAP + SEQ_DEV - 1) // SEQ_DEV
    coin_flip = jax.random.randint(jax.random.fold_in(key, 13), (TOKENS,), 0, 4) == 0
    spread_pick = jax.random.randint(jax.random.fold_in(key, 14), (TOKENS,), 0, EXPERTS)
    first_pick = jnp.where(forced | coin_flip, favored, spread_pick)
    second = (first_pick + 1 + jax.random.randint(jax.random.fold_in(key, 15), (TOKENS,), 0, EXPERTS - 1)) % EXPERTS
    pair_ids = jnp.stack([first_pick, second], axis=1).astype(jnp.int32)
    token_alive = position < seq_lengths[token_index // SEQ_LEN]
    expert_range = jnp.arange(EXPERTS, dtype=jnp.int32)
    route_hits = ((pair_ids[:, :, None] == expert_range[None, None, :]) & token_alive[:, None, None]).astype(jnp.int32)
    route_hits = route_hits.reshape(group_count, TOK_DEV, 2, EXPERTS)
    first_hits = route_hits[:, :, 0]
    second_hits = route_hits[:, :, 1]
    first_rank = jnp.cumsum(first_hits, axis=1) - first_hits
    first_count = jnp.sum(first_hits, axis=1, keepdims=True)
    second_rank = jnp.cumsum(second_hits, axis=1) - second_hits + first_count
    queue_rank = jnp.stack([jnp.sum(first_rank * first_hits, axis=-1), jnp.sum(second_rank * second_hits, axis=-1)], axis=-1).reshape(TOKENS, 2)
    slot_index = jnp.where(token_alive[:, None] & (queue_rank < CAP), queue_rank, CAP)
    return (seq_lengths, pair_ids, slot_index.astype(jnp.int32))


def draw_lengths(key, part):
    return routing_tables(key)[0]


def draw_expert_ids(key, part):
    return routing_tables(key)[1]


def draw_route_slots(key, part):
    return routing_tables(key)[2]


def steps_of(rng, shape, shards, low, largest):
    factor_of = 1.0
    for dim, parts in shards:
        steps = jax.random.uniform(jax.random.fold_in(jax.random.fold_in(rng, 6), dim), (parts,), jnp.float32, low / len(shards), largest / len(shards))
        factor_of = factor_of * jnp.repeat(jnp.exp(steps), shape[dim] // parts).reshape((-1,) + (1,) * (len(shape) - 1 - dim))
    return factor_of


def scatter_about(key, dims, scale, reach, split=(), held_as=jnp.bfloat16):
    entries = jax.random.normal(key, dims, jnp.float32) * scale
    if len(split) > 0:
        entries = steps_of(key, dims, split, -0.22, 0.18) * entries
    return jnp.clip(entries, min=-reach, max=reach).astype(held_as)


def setup_inputs(seed: int = 0) -> dict:
    keys = jax.random.split(jax.random.key(seed), 14)
    inputs = scatter_about(keys[0], (TOKENS, D), 1.0, 6.0, ((0, 8),))
    teacher = scatter_about(keys[1], (TOKENS, D), 1.0, 6.0, ((0, 8),))
    lengths = draw_lengths(jax.random.fold_in(keys[13], 71), 0)
    expert_ids = draw_expert_ids(jax.random.fold_in(keys[13], 71), 0)
    route_slots = draw_route_slots(jax.random.fold_in(keys[13], 71), 0)
    gain_attn = jnp.clip(1.0 + 0.1 * jax.random.normal(keys[5], (D,), jnp.float32), 0.5, 1.5)
    w_qkv = scatter_about(keys[6], (3, D, HEADS * HEAD_DIM), (4 * D) ** -0.5, 0.09375, ((2, 4),))
    w_out = scatter_about(keys[7], (HEADS * HEAD_DIM, D), (D // 8) ** -0.5, 0.5, ((0, 4),))
    rel_table = scatter_about(keys[8], (BUCKETS, HEADS), 1.0, 4.0, ((1, 4),), jnp.float32)
    gain_moe = jnp.clip(1.0 + 0.1 * jax.random.normal(keys[9], (D,), jnp.float32), 0.5, 1.5)
    w_router = scatter_about(keys[10], (D, EXPERTS), (4 * D) ** -0.5, 0.09375)
    w_gate_up = scatter_about(keys[11], (EXPERTS, 2, D, FF), D ** -0.5, 0.1875, ((0, 8), (3, 4)))
    w_down = scatter_about(keys[12], (EXPERTS, FF, D), (FF // 4) ** -0.5, 0.21875, ((0, 8), (1, 4)))
    return dict(inputs=inputs, teacher=teacher, lengths=lengths, expert_ids=expert_ids, route_slots=route_slots, gain_attn=gain_attn, w_qkv=w_qkv, w_out=w_out, rel_table=rel_table, gain_moe=gain_moe, w_router=w_router, w_gate_up=w_gate_up, w_down=w_down)


EPSILON = 1e-06
FAR_STEPS = (12, 16, 23, 32, 46, 64, 91)
MASKED = -1000000000.0

@jax.custom_vjp
def low(v):
    return lax.optimization_barrier(v.astype(jnp.bfloat16)).astype(jnp.float32)

@jax.custom_vjp
def low_back(v):
    return v

def low_keep(v):
    return (low(v), None)

def low_pass(kept, grad):
    return (grad,)

def back_keep(v):
    return (v, None)

def back_low(kept, grad):
    return (low(grad),)
low.defvjp(low_keep, low_pass)
low_back.defvjp(back_keep, back_low)

def offset_bucket(offset):
    direction = jnp.where(offset > 0, 16, 0).astype(jnp.int32)
    distance = jnp.abs(offset)
    farther = jnp.full(offset.shape, 8, jnp.int32)
    for threshold in FAR_STEPS:
        farther = farther + (distance >= threshold).astype(jnp.int32)
    return direction + jnp.where(distance < 8, distance, farther)

def rms_norm(values, gain):
    return values * lax.rsqrt(lax.optimization_barrier(jnp.mean(values * values, axis=-1, keepdims=True)) + EPSILON) * gain

def route_gates(logits, picks):
    expert_probs = jax.nn.softmax(logits, axis=-1)
    chosen = lax.optimization_barrier(jnp.sum(expert_probs[:, None, :] * picks, axis=-1))
    return chosen / lax.optimization_barrier(jnp.sum(chosen, axis=-1, keepdims=True))

def reference(inputs, teacher, lengths, expert_ids, route_slots, gain_attn, w_qkv, w_out, rel_table, gain_moe, w_router, w_gate_up, w_down):
    highest = lax.Precision.HIGHEST
    token_index = jnp.arange(TOKENS, dtype=jnp.int32)
    row_len = lengths[token_index // SEQ_LEN]
    row_alive = (token_index % SEQ_LEN < row_len).astype(jnp.float32)[:, None]
    valid_total = jnp.sum(lengths).astype(jnp.float32)
    device_of = token_index // TOK_DEV
    kept_route = route_slots < CAP
    slot_total = EXPERTS * N_DP * CAP
    flat_slot = jnp.where(kept_route, (expert_ids * N_DP + device_of[:, None]) * CAP + route_slots, slot_total).astype(jnp.int32)
    source = jnp.full((slot_total + 1,), TOKENS, jnp.int32).at[flat_slot.reshape(-1)].set(jnp.repeat(token_index, 2))
    source = source[:slot_total]
    picks = (expert_ids[:, :, None] == jnp.arange(EXPERTS, dtype=jnp.int32)[None, None, :]).astype(jnp.float32)
    teacher_wide = teacher.astype(jnp.float32)
    key_range = jnp.arange(SEQ_LEN, dtype=jnp.int32)
    buckets = offset_bucket(key_range[None, :] - key_range[:, None])

    def forward(residual, gain_one, qkv_weight, out_weight, table, gain_two, router_weight, gate_up_weight, down_weight):
        normed_one = low(rms_norm(residual, gain_one))
        projected = low_back(low(jnp.einsum('td,jde->jte', normed_one, qkv_weight, precision=highest)))
        heads_split = projected.reshape(3, SEQS, SEQ_LEN, HEADS, HEAD_DIM)
        rel_bias = jnp.transpose(table[buckets], (2, 0, 1))

        def attend(carry, pieces):
            query_seq, key_seq, value_seq, length_here = pieces
            scores = low_back(jnp.einsum('qhe,khe->hqk', query_seq, key_seq, precision=highest)) + rel_bias
            scores = jnp.where(key_range[None, None, :] < length_here, scores, MASKED)
            probs = jax.nn.softmax(scores, axis=-1)
            mixture = jnp.einsum('hqk,khe->qhe', low(probs), value_seq, precision=highest)
            return (carry, mixture.reshape(SEQ_LEN, HEADS * HEAD_DIM))
        carry_out, mixtures = lax.scan(jax.checkpoint(attend), jnp.zeros((), jnp.float32), (heads_split[0], heads_split[1], heads_split[2], lengths))
        attended = low_back(low(mixtures.reshape(TOKENS, HEADS * HEAD_DIM)))
        after_attn = residual + low_back(jnp.dot(attended, out_weight, precision=highest))
        normed_two = low(rms_norm(after_attn, gain_two))
        logits = low_back(jnp.dot(normed_two, router_weight, precision=highest))
        gates = route_gates(logits, picks)
        padded = jnp.concatenate([normed_two, jnp.zeros((1, D), jnp.float32)], axis=0)
        slot_rows = padded[source].reshape(EXPERTS, N_DP * CAP, D)

        def expert(rows_here, gate_up_here, down_here):
            gate_pre = low_back(jnp.dot(rows_here, gate_up_here[0], precision=highest))
            up_pre = low_back(jnp.dot(rows_here, gate_up_here[1], precision=highest))
            hidden = low(jax.nn.gelu(gate_pre, approximate=True) * up_pre)
            partial_sums = jnp.einsum('rsf,sfd->srd', hidden.reshape(-1, N_TENSOR, FF // N_TENSOR), down_here.reshape(N_TENSOR, FF // N_TENSOR, D), precision=highest)
            return lax.optimization_barrier(jnp.sum(low_back(low(partial_sums)), axis=0))
        checked = jax.checkpoint(expert)
        outputs = lax.map(lambda packed: checked(packed[0], packed[1], packed[2]), (slot_rows, gate_up_weight, down_weight))
        flat_out = jnp.concatenate([outputs.reshape(slot_total, D), jnp.zeros((1, D), jnp.float32)], axis=0)
        routed = flat_out[flat_slot]
        expert_mix = gates[:, 0, None] * routed[:, 0] + gates[:, 1, None] * routed[:, 1]
        block_out = after_attn + expert_mix
        deviation = (block_out - teacher_wide) * row_alive
        squared = jnp.sum(deviation * deviation)
        return (squared * (TOKENS / (2.0 * valid_total)), (block_out, squared / (2.0 * valid_total * D)))
    params = (inputs.astype(jnp.float32), gain_attn, w_qkv.astype(jnp.float32), w_out.astype(jnp.float32), rel_table, gain_moe, w_router.astype(jnp.float32), w_gate_up.astype(jnp.float32), w_down.astype(jnp.float32))
    scaled, grad_pull, extras = jax.vjp(forward, *params, has_aux=True)
    gradients = grad_pull(jnp.ones_like(scaled))
    return (extras[0], extras[1], gradients[0], gradients[1], gradients[2], gradients[3], gradients[4], gradients[5], gradients[6], gradients[7], gradients[8])
```

```python
import functools
import math

import jax
import jax.numpy as jnp
from jax import lax
from jax.experimental import pallas as pl
from jax.experimental.pallas import tpu as pltpu
from jax.sharding import PartitionSpec as P

BUCKETS = 32
SEQ_LEN = 512
TILE = 128
SPAN = 2 * SEQ_LEN

EPSILON = 1e-06
FAR_STEPS = (12, 16, 23, 32, 46, 64, 91)
MASKED = -1000000000.0
F32 = jnp.float32
BF16 = jnp.bfloat16


def offset_bucket(offset):
    direction = jnp.where(offset > 0, 16, 0).astype(jnp.int32)
    distance = jnp.abs(offset)
    farther = jnp.full(offset.shape, 8, jnp.int32)
    for threshold in FAR_STEPS:
        farther = farther + (distance >= threshold).astype(jnp.int32)
    return direction + jnp.where(distance < 8, distance, farther)


def bucket_onehot(offsets):
    bucket_range = jnp.arange(BUCKETS, dtype=jnp.int32)
    return (offset_bucket(offsets)[:, None] == bucket_range[None, :]).astype(F32)


def route_gates(logits, picks):
    expert_probs = jax.nn.softmax(logits, axis=-1)
    chosen = jnp.sum(expert_probs[:, None, :] * picks, axis=-1)
    return chosen / jnp.sum(chosen, axis=-1, keepdims=True)


def dot(a, b, dims=((1,), (0,))):
    return lax.dot_general(a, b, (dims, ((), ())), preferred_element_type=F32)


def attention_forward(heads, width, len_ref, bias_ref, proj_ref, attended_ref, probs_ref):
    length = len_ref[0]
    alive = lax.broadcasted_iota(jnp.int32, (TILE, SEQ_LEN), 1) < length
    for h in range(heads):
        cols = slice(h * width, (h + 1) * width)
        keys = proj_ref[1, :, cols]
        values = proj_ref[2, :, cols]
        skew = pltpu.roll(
            jnp.broadcast_to(bias_ref[h : h + 1, :], (TILE, SPAN)), 0, 1, stride=1, stride_axis=0
        )
        for j in range(SEQ_LEN // TILE):
            rows = slice(j * TILE, (j + 1) * TILE)
            start = SEQ_LEN - j * TILE
            scores = dot(proj_ref[0, rows, cols], keys, ((1,), (1,)))
            scores = jnp.where(alive, scores + skew[:, start : start + SEQ_LEN], MASKED)
            exponent = jnp.exp(scores - jnp.max(scores, axis=1, keepdims=True))
            probs = exponent * (1.0 / jnp.sum(exponent, axis=1, keepdims=True))
            probs_ref[h, rows, :] = probs
            attended_ref[rows, cols] = dot(probs.astype(BF16), values).astype(BF16)


def attention_backward(heads, width, proj_ref, probs_ref, grad_ref, out_ref, diag_ref, acc, key_acc, value_acc):
    for h in range(heads):
        cols = slice(h * width, (h + 1) * width)
        keys = proj_ref[1, :, cols]
        values = proj_ref[2, :, cols]
        acc[...] = jnp.zeros_like(acc)
        for j in range(SEQ_LEN // TILE):
            rows = slice(j * TILE, (j + 1) * TILE)
            start = SEQ_LEN - j * TILE
            probs = probs_ref[h, rows, :]
            grad = grad_ref[rows, cols]
            prob_grad = dot(grad, values, ((1,), (1,)))
            score_grad = probs * (prob_grad - jnp.sum(probs * prob_grad, axis=1, keepdims=True))
            acc[:, start : start + SEQ_LEN] += score_grad
            low = score_grad.astype(BF16)
            out_ref[0, rows, cols] = dot(low, keys).astype(BF16)
            key_part = dot(low, proj_ref[0, rows, cols], ((0,), (0,)))
            value_part = dot(probs.astype(BF16), grad, ((0,), (0,)))
            if j == 0:
                key_acc[...] = key_part
                value_acc[...] = value_part
            else:
                key_acc[...] += key_part
                value_acc[...] += value_part
        out_ref[1, :, cols] = key_acc[...].astype(BF16)
        out_ref[2, :, cols] = value_acc[...].astype(BF16)
        total = acc[...]
        half = TILE // 2
        while half >= 1:
            total = total[:half] + pltpu.roll(total[half : 2 * half], SPAN - half, 1)
            half //= 2
        diag_ref[h : h + 1, :] = total


VMEM = pl.BlockSpec(memory_space=pltpu.VMEM)
SMEM = pl.BlockSpec(memory_space=pltpu.SMEM)


def rms_scale(values):
    return lax.rsqrt(jnp.mean(values * values, axis=-1, keepdims=True) + EPSILON)


def body(
    inputs,
    teacher,
    lengths,
    expert_ids,
    route_slots,
    gain_attn,
    w_qkv,
    w_out,
    rel_table,
    gain_moe,
    w_router,
    w_gate_up,
    w_down,
):
    highest = lax.Precision.HIGHEST
    tok_rows, model_width = inputs.shape
    groups = lax.axis_size("dp")
    shards = lax.axis_size("tensor")
    experts = w_router.shape[1]
    local_experts = w_gate_up.shape[0]
    capacity = 10 * tok_rows // (4 * experts)
    padded_cap = (capacity + 15) // 16 * 16
    slot_count = experts * padded_cap
    heads_here = rel_table.shape[1]
    width_here = w_qkv.shape[2]
    head_width = width_here // heads_here
    share = model_width // shards
    column_start = lax.axis_index("tensor") * share

    def mine(values):
        return lax.dynamic_slice_in_dim(values, column_start, share, values.ndim - 1)

    def gather_columns(values):
        return lax.all_gather(values, "tensor", axis=values.ndim - 1, tiled=True)

    def exchange(values):
        blocks = values.reshape(groups, slot_count // groups, share)
        return lax.all_to_all(blocks, "dp", split_axis=0, concat_axis=0, tiled=True)

    def scatter_columns(values):
        rows = values.shape[0]
        parts = lax.all_to_all(
            values.reshape(rows, shards, share), "tensor", split_axis=1, concat_axis=1, tiled=True
        )
        return jnp.sum(parts.astype(F32), axis=1)

    offsets = jnp.arange(SPAN, dtype=jnp.int32) - SEQ_LEN
    onehot_offsets = bucket_onehot(offsets)
    offset_bias = jnp.dot(onehot_offsets, rel_table, precision=highest).T

    residual = inputs.astype(F32)
    scale_one = rms_scale(residual)
    normed_low = (residual * scale_one * gain_attn).astype(BF16)
    projected = jnp.einsum("td,jde->jte", normed_low, w_qkv, preferred_element_type=F32).astype(BF16)

    attended, probs = pl.pallas_call(
        functools.partial(attention_forward, heads_here, head_width),
        out_shape=(
            jax.ShapeDtypeStruct((tok_rows, width_here), BF16),
            jax.ShapeDtypeStruct((heads_here, SEQ_LEN, SEQ_LEN), F32),
        ),
        in_specs=[SMEM, VMEM, VMEM],
        out_specs=(VMEM, VMEM),
        compiler_params=pltpu.CompilerParams(vmem_limit_bytes=32 * 1024 * 1024),
        name="attention_forward",
    )(lengths, offset_bias, projected)

    w_out_full = lax.all_gather(w_out, "tensor", axis=0, tiled=True)
    attended_full = gather_columns(attended)
    after_attn = residual + jnp.dot(attended_full, w_out_full, preferred_element_type=F32)
    scale_two = rms_scale(after_attn)
    normed_two_low = (after_attn * scale_two * gain_moe).astype(BF16)
    logits = jnp.dot(normed_two_low, w_router, preferred_element_type=F32)
    expert_range = jnp.arange(experts, dtype=jnp.int32)
    picks = (expert_ids[:, :, None] == expert_range[None, None, :]).astype(F32)
    gates, gate_pull = jax.vjp(lambda values: route_gates(values, picks), logits)
    kept_route = route_slots < capacity
    target = jnp.where(kept_route, expert_ids * padded_cap + route_slots, -1)
    slot_range = jnp.arange(slot_count, dtype=jnp.int32)
    route_of = (target[:, :, None] == slot_range[None, None, :]).astype(BF16)
    first_route, second_route = route_of[:, 0], route_of[:, 1]
    any_route = first_route + second_route

    after_mine = mine(after_attn)
    teacher_mine = mine(teacher).astype(F32)
    normed_mine = mine(normed_two_low)
    dispatched = dot(any_route, normed_mine, ((0,), (0,))).astype(BF16)
    expert_rows = gather_columns(exchange(dispatched)).reshape(
        groups, local_experts, padded_cap, model_width
    )
    gate_up = jnp.einsum("nxcd,xjdf->jnxcf", expert_rows, w_gate_up, preferred_element_type=F32)
    activated, gelu_pull = jax.vjp(lambda v: jax.nn.gelu(v, approximate=True), gate_up[0])
    hidden_low = (activated * gate_up[1]).astype(BF16)
    partial_out = jnp.einsum(
        "nxcf,xfd->nxcd", hidden_low, w_down, preferred_element_type=F32
    ).astype(BF16)
    summed = scatter_columns(partial_out.reshape(slot_count, model_width)).astype(BF16)
    returned = exchange(summed).reshape(slot_count, share)
    routed_first = dot(first_route, returned)
    routed_second = dot(second_route, returned)

    row_alive = (jnp.arange(tok_rows, dtype=jnp.int32) < lengths[0]).astype(F32)[:, None]
    valid_total = lax.psum(lengths[0].astype(F32), "dp")
    scale = groups * tok_rows / valid_total
    block_out = after_mine + gates[:, 0, None] * routed_first + gates[:, 1, None] * routed_second
    deviation = (block_out - teacher_mine) * row_alive
    out_grad = deviation * scale
    squared = lax.psum(jnp.sum(deviation * deviation), ("dp", "tensor"))
    loss = squared / (2.0 * valid_total * model_width)

    slot_grad = (
        dot(first_route, (gates[:, 0, None] * out_grad).astype(BF16), ((0,), (0,)))
        + dot(second_route, (gates[:, 1, None] * out_grad).astype(BF16), ((0,), (0,)))
    ).astype(BF16)
    gate_grad_part = jnp.stack(
        [jnp.sum(routed_first * out_grad, axis=-1), jnp.sum(routed_second * out_grad, axis=-1)],
        axis=1,
    )
    gate_grad = lax.psum(gate_grad_part, "tensor")
    expert_grad = gather_columns(exchange(slot_grad)).reshape(
        groups, local_experts, padded_cap, model_width
    )
    down_grad = jnp.einsum("nxcf,nxcd->xfd", hidden_low, expert_grad, preferred_element_type=F32)
    hidden_grad = jnp.einsum("nxcd,xfd->nxcf", expert_grad, w_down, preferred_element_type=F32)
    gate_side = gelu_pull(hidden_grad * gate_up[1])[0]
    up_side = hidden_grad * activated
    pre_grads = jnp.stack([gate_side, up_side], axis=0).astype(BF16)
    gate_up_grad = jnp.einsum(
        "nxcd,jnxcf->xjdf", expert_rows, pre_grads, preferred_element_type=F32
    )
    rows_grad = jnp.einsum("jnxcf,xjdf->nxcd", pre_grads, w_gate_up, preferred_element_type=F32)
    rows_mine = scatter_columns(rows_grad.astype(BF16).reshape(slot_count, model_width))
    back_grad = exchange(rows_mine.astype(BF16)).reshape(slot_count, share)

    logit_grad = gate_pull(gate_grad)[0].astype(BF16)
    router_grad = dot(normed_two_low, logit_grad, ((0,), (0,)))
    normed_two_grad = dot(any_route, back_grad) + mine(dot(logit_grad, w_router, ((1,), (1,))))
    gain_two_mine = mine(gain_moe)

    def rms_back(values, factor, gain, grad):
        projected_part = jnp.sum(grad * gain * values, axis=-1, keepdims=True)
        along = lax.psum(projected_part, "tensor")
        gain_grad = jnp.sum(grad * values * factor, axis=0)
        return factor * (grad * gain - values * (factor * factor * along / model_width)), gain_grad

    after_norm_grad, gain_moe_mine = rms_back(after_mine, scale_two, gain_two_mine, normed_two_grad)
    after_grad = out_grad + after_norm_grad
    branch_grad = gather_columns(after_grad.astype(BF16))
    out_proj_grad = dot(attended, branch_grad, ((0,), (0,)))
    attended_grad = dot(branch_grad, w_out, ((1,), (1,))).astype(BF16)

    projected_grad, diagonals = pl.pallas_call(
        functools.partial(attention_backward, heads_here, head_width),
        out_shape=(
            jax.ShapeDtypeStruct((3, tok_rows, width_here), BF16),
            jax.ShapeDtypeStruct((heads_here, SPAN), F32),
        ),
        in_specs=[VMEM, VMEM, VMEM],
        out_specs=(VMEM, VMEM),
        scratch_shapes=[
            pltpu.VMEM((TILE, SPAN), F32),
            pltpu.VMEM((SEQ_LEN, head_width), F32),
            pltpu.VMEM((SEQ_LEN, head_width), F32),
        ],
        compiler_params=pltpu.CompilerParams(vmem_limit_bytes=32 * 1024 * 1024),
        name="attention_backward",
    )(projected, probs, attended_grad)
    table_grad = jnp.dot(onehot_offsets.T, diagonals.T, precision=highest)

    qkv_grad = jnp.einsum("td,jte->jde", normed_low, projected_grad, preferred_element_type=F32)
    normed_one_part = jnp.einsum("jte,jde->td", projected_grad, w_qkv, preferred_element_type=F32)
    normed_one_grad = scatter_columns(normed_one_part.astype(BF16))
    input_norm_grad, gain_attn_mine = rms_back(
        mine(residual), scale_one, mine(gain_attn), normed_one_grad
    )
    input_grad = after_grad + input_norm_grad

    def place(part):
        whole = jnp.zeros((model_width,), F32)
        return lax.dynamic_update_slice_in_dim(whole, part, column_start, 0)

    gains = lax.psum(jnp.stack([place(gain_attn_mine), place(gain_moe_mine)]), ("dp", "tensor"))
    router_sum = lax.psum(router_grad.astype(BF16), "dp").astype(F32)
    qkv_sum = lax.psum(qkv_grad.astype(BF16), "dp").astype(F32)
    out_proj_sum = lax.psum(out_proj_grad.astype(BF16), "dp").astype(F32)
    table_sum = lax.psum(table_grad, "dp")
    return (
        block_out,
        loss,
        input_grad,
        gains[0],
        qkv_sum,
        out_proj_sum,
        table_sum,
        gains[1],
        router_sum,
        gate_up_grad,
        down_grad,
    )


def solution(mesh):
    placed = (
        P("dp", None),
        P("dp", None),
        P("dp"),
        P("dp", None),
        P("dp", None),
        P(),
        P(None, None, "tensor"),
        P("tensor", None),
        P(None, "tensor"),
        P(),
        P(),
        P("dp", None, None, "tensor"),
        P("dp", "tensor", None),
    )
    return jax.shard_map(
        body,
        mesh=mesh,
        in_specs=placed,
        out_specs=(
            P("dp", "tensor"),
            P(),
            P("dp", "tensor"),
            P(),
            P(None, None, "tensor"),
            P("tensor", None),
            P(None, "tensor"),
            P(),
            P(),
            P("dp", None, None, "tensor"),
            P("dp", "tensor", None),
        ),
        check_vma=False,
    )
```

```python
import functools
import math

import jax
import jax.numpy as jnp
from jax import lax
from jax.experimental import pallas as pl
from jax.experimental.pallas import tpu as pltpu
from jax.sharding import PartitionSpec as P

BUCKETS = 32
SEQ_LEN = 512
TILE = 128
SPAN = 2 * SEQ_LEN

EPSILON = 1e-06
FAR_STEPS = (12, 16, 23, 32, 46, 64, 91)
MASKED = -1000000000.0
F32 = jnp.float32
BF16 = jnp.bfloat16


def offset_bucket(offset):
    direction = jnp.where(offset > 0, 16, 0).astype(jnp.int32)
    distance = jnp.abs(offset)
    farther = jnp.full(offset.shape, 8, jnp.int32)
    for threshold in FAR_STEPS:
        farther = farther + (distance >= threshold).astype(jnp.int32)
    return direction + jnp.where(distance < 8, distance, farther)


def bucket_onehot(offsets):
    bucket_range = jnp.arange(BUCKETS, dtype=jnp.int32)
    return (offset_bucket(offsets)[:, None] == bucket_range[None, :]).astype(F32)


def route_gates(logits, picks):
    expert_probs = jax.nn.softmax(logits, axis=-1)
    chosen = jnp.sum(expert_probs[:, None, :] * picks, axis=-1)
    return chosen / jnp.sum(chosen, axis=-1, keepdims=True)


def dot(a, b, dims=((1,), (0,))):
    return lax.dot_general(a, b, (dims, ((), ())), preferred_element_type=F32)


def attention_forward(heads, width, len_ref, bias_ref, proj_ref, attended_ref, probs_ref):
    length = len_ref[0]
    alive = lax.broadcasted_iota(jnp.int32, (TILE, SEQ_LEN), 1) < length
    for h in range(heads):
        cols = slice(h * width, (h + 1) * width)
        keys = proj_ref[1, :, cols]
        values = proj_ref[2, :, cols]
        skew = pltpu.roll(
            jnp.broadcast_to(bias_ref[h : h + 1, :], (TILE, SPAN)), 0, 1, stride=1, stride_axis=0
        )
        for j in range(SEQ_LEN // TILE):
            rows = slice(j * TILE, (j + 1) * TILE)
            start = SEQ_LEN - j * TILE
            scores = dot(proj_ref[0, rows, cols], keys, ((1,), (1,)))
            scores = jnp.where(alive, scores + skew[:, start : start + SEQ_LEN], MASKED)
            exponent = jnp.exp(scores - jnp.max(scores, axis=1, keepdims=True))
            probs = exponent * (1.0 / jnp.sum(exponent, axis=1, keepdims=True))
            probs_ref[h, rows, :] = probs
            attended_ref[rows, cols] = dot(probs.astype(BF16), values).astype(BF16)


def attention_backward(heads, width, proj_ref, probs_ref, grad_ref, out_ref, diag_ref, acc, key_acc, value_acc):
    for h in range(heads):
        cols = slice(h * width, (h + 1) * width)
        keys = proj_ref[1, :, cols]
        values = proj_ref[2, :, cols]
        acc[...] = jnp.zeros_like(acc)
        for j in range(SEQ_LEN // TILE):
            rows = slice(j * TILE, (j + 1) * TILE)
            start = SEQ_LEN - j * TILE
            probs = probs_ref[h, rows, :]
            grad = grad_ref[rows, cols]
            prob_grad = dot(grad, values, ((1,), (1,)))
            score_grad = probs * (prob_grad - jnp.sum(probs * prob_grad, axis=1, keepdims=True))
            acc[:, start : start + SEQ_LEN] += score_grad
            low = score_grad.astype(BF16)
            out_ref[0, rows, cols] = dot(low, keys).astype(BF16)
            key_part = dot(low, proj_ref[0, rows, cols], ((0,), (0,)))
            value_part = dot(probs.astype(BF16), grad, ((0,), (0,)))
            if j == 0:
                key_acc[...] = key_part
                value_acc[...] = value_part
            else:
                key_acc[...] += key_part
                value_acc[...] += value_part
        out_ref[1, :, cols] = key_acc[...].astype(BF16)
        out_ref[2, :, cols] = value_acc[...].astype(BF16)
        total = acc[...]
        half = TILE // 2
        while half >= 1:
            total = total[:half] + pltpu.roll(total[half : 2 * half], SPAN - half, 1)
            half //= 2
        diag_ref[h : h + 1, :] = total


VMEM = pl.BlockSpec(memory_space=pltpu.VMEM)
SMEM = pl.BlockSpec(memory_space=pltpu.SMEM)


MESH_ID = pl.DeviceIdType.MESH
ANY = pl.BlockSpec(memory_space=pl.ANY)


class Mover:
    def __init__(self, groups, shards, cap, chunk, source, rows, part, back, scratch):
        self.groups, self.lines, self.cap, self.chunk = groups, shards // 2, cap, chunk
        self.source, self.rows, self.part, self.back = source, rows, part, back
        (self.mate_in, self.line_out, self.line_in, self.back_out, self.dp_sems, self.row_sems, self.sum_sems) = scratch
        self.me, self.place = lax.axis_index("dp"), lax.axis_index("tensor")
        self.line, self.core = lax.div(self.place, 2), lax.rem(self.place, 2)
        self.steps = groups // chunk

    def group(self, offset):
        return lax.rem(self.me + offset, self.groups)

    def shard(self, offset, core):
        return lax.rem(self.line + offset, self.lines) * 2 + core

    def greet(self):
        barrier = pltpu.get_barrier_semaphore()
        for i in range(1, self.groups):
            pl.semaphore_signal(barrier, inc=1, device_id={"dp": self.group(i)}, device_id_type=MESH_ID)
        for d in range(1, self.lines):
            pl.semaphore_signal(barrier, inc=1, device_id={"tensor": self.shard(d, self.core)}, device_id_type=MESH_ID)
        pl.semaphore_signal(barrier, inc=1, device_id={"tensor": self.shard(0, 1 - self.core)}, device_id_type=MESH_ID)
        pl.semaphore_wait(barrier, self.groups - 1 + self.lines)

    def remote(self, src, dst, sems, index, device):
        return pltpu.make_async_remote_copy(
            src_ref=src, dst_ref=dst, send_sem=sems.at[(0, *index)], recv_sem=sems.at[(1, *index)],
            device_id=device, device_id_type=MESH_ID,
        )

    def here(self, shard, i):
        return self.rows.at[shard, :, pl.ds(i * self.cap, self.cap), :]

    def send_out(self):
        pltpu.make_async_copy(self.source.at[self.me], self.here(self.place, 0), self.dp_sems.at[0, 1, 0]).start()
        for i in range(1, self.groups):
            self.out_copy(i).start()

    def out_copy(self, i):
        to = self.group(i)
        return self.remote(self.source.at[to], self.here(self.place, i), self.dp_sems.at[0], (i,), {"dp": to})

    def line_copy(self, d, i):
        return self.remote(
            self.here(self.place, i), self.here(self.place, i), self.row_sems.at[0], (d, i),
            {"tensor": self.shard(d, self.core)},
        )

    def mate_copy(self, d, i):
        shard = self.shard(self.lines - d, self.core)
        return self.remote(
            self.here(shard, i), self.here(shard, i), self.row_sems.at[1], (d, i),
            {"tensor": self.shard(0, 1 - self.core)},
        )

    def landed(self, where, sems, index):
        self.remote(where, where, sems, index, {"tensor": self.shard(0, 1 - self.core)}).wait_recv()

    def places(self, k):
        return range(k * self.chunk, (k + 1) * self.chunk)

    def spread(self, k):
        for i in self.places(k):
            where = self.here(self.place, i)
            if i == 0:
                pltpu.make_async_copy(self.source.at[self.me], where, self.dp_sems.at[0, 1, 0]).wait()
            else:
                self.landed(where, self.dp_sems.at[0], (i,))
            for d in range(1, self.lines):
                self.line_copy(d, i).start()
            self.mate_copy(0, i).start()

    def relay(self, k):
        for i in self.places(k):
            for d in range(1, self.lines):
                shard = self.shard(self.lines - d, self.core)
                self.landed(self.here(shard, i), self.row_sems.at[0], (d, i))
                self.mate_copy(d, i).start()

    def collect(self, k):
        for i in self.places(k):
            for d in range(self.lines):
                shard = self.shard(self.lines - d, 1 - self.core)
                self.landed(self.here(shard, i), self.row_sems.at[1], (d, i))

    def span(self, k):
        return pl.ds(k * self.chunk * self.cap, self.chunk * self.cap)

    def pair_copy(self, d, k):
        shard = self.shard(d, 1 - self.core)
        return self.remote(
            self.part.at[shard, :, self.span(k), :], self.mate_in.at[d, :, self.span(k), :], self.sum_sems.at[0], (d, k),
            {"tensor": self.shard(0, 1 - self.core)},
        )

    def sum_copy(self, d, k):
        return self.remote(
            self.line_out.at[d, :, self.span(k), :], self.line_in.at[d, :, self.span(k), :], self.sum_sems.at[1], (d, k),
            {"tensor": self.shard(d, self.core)},
        )

    def back_copy(self, i):
        return self.remote(
            self.back_out.at[:, pl.ds(i * self.cap, self.cap), :], self.back.at[self.me], self.dp_sems.at[1], (i,),
            {"dp": self.group(self.groups - i)},
        )

    def pair(self, k):
        for d in range(self.lines):
            self.pair_copy(d, k).start()

    def pair_sum(self, d, k):
        shard = self.shard(d, self.core)
        return self.part[shard, :, self.span(k), :].astype(F32) + self.mate_in[d, :, self.span(k), :].astype(F32)

    def along(self, k):
        for d in range(self.lines):
            self.landed(self.mate_in.at[d, :, self.span(k), :], self.sum_sems.at[0], (d, k))
        for d in range(1, self.lines):
            self.line_out[d, :, self.span(k), :] = self.pair_sum(d, k).astype(BF16)
            self.sum_copy(d, k).start()

    def give(self, k):
        total = self.pair_sum(0, k)
        for d in range(1, self.lines):
            self.landed(self.line_in.at[d, :, self.span(k), :], self.sum_sems.at[1], (d, k))
            total = total + self.line_in[d, :, self.span(k), :].astype(F32)
        self.back_out[:, self.span(k), :] = total.astype(BF16)
        for i in self.places(k):
            if i == 0:
                self.own_back().start()
            else:
                self.back_copy(i).start()

    def own_back(self):
        return pltpu.make_async_copy(
            self.back_out.at[:, pl.ds(0, self.cap), :], self.back.at[self.me], self.dp_sems.at[1, 1, 0]
        )

    def run(self, compute):
        self.greet()
        self.send_out()
        for step in range(self.steps + 4):
            for lag, work in enumerate((self.spread, self.relay, compute, self.along, self.give)):
                k = step - lag
                if 0 <= k < self.steps:
                    if lag == 2:
                        self.collect(k)
                    work(k)
                    if lag == 2:
                        self.pair(k)

    def finish(self):
        self.own_back().wait()
        for i in range(1, self.groups):
            where = self.back.at[self.group(i)]
            self.landed(where, self.dp_sems.at[1], (i,))
            self.out_copy(i).wait_send()
            self.back_copy(i).wait_send()
        for i in range(self.groups):
            for d in range(self.lines):
                if d:
                    self.line_copy(d, i).wait_send()
                self.mate_copy(d, i).wait_send()
        for k in range(self.steps):
            for d in range(self.lines):
                if d:
                    self.sum_copy(d, k).wait_send()
                self.pair_copy(d, k).wait_send()


def mover_scratch(groups, shards, local, cap, share, chunk):
    lines, slots, steps = shards // 2, groups * cap, groups // chunk
    return [
        pltpu.VMEM((lines, local, slots, share), BF16),
        pltpu.VMEM((lines, local, slots, share), BF16),
        pltpu.VMEM((lines, local, slots, share), BF16),
        pltpu.VMEM((local, slots, share), BF16),
        pltpu.SemaphoreType.DMA((2, 2, groups)),
        pltpu.SemaphoreType.DMA((2, 2, lines, groups)),
        pltpu.SemaphoreType.DMA((2, 2, lines, steps)),
    ]


ROOT = math.sqrt(2.0 / math.pi)


def gelu_parts(v):
    inner = jnp.tanh(ROOT * (v + 0.044715 * (v * v * v)))
    half = 0.5 * (1.0 + inner)
    slope = half + 0.5 * v * (1.0 - inner * inner) * (ROOT * (1.0 + 3.0 * 0.044715 * v * v))
    return v * half, slope


def expert_forward(
    groups, shards, local, cap, chunk,
    source, gate_up_hbm, down_hbm,
    back, rows_hbm, pre_hbm, hidden_hbm,
    rows, part, gate_up, down, pre, hidden, load_sems, save_sems, *scratch,
):
    mover = Mover(groups, shards, cap, chunk, source, rows, part, back, scratch)
    share = rows.shape[-1]
    loads = [pltpu.make_async_copy(gate_up_hbm, gate_up, load_sems.at[0]), pltpu.make_async_copy(down_hbm, down, load_sems.at[1])]
    for load in loads:
        load.start()

    def saves(k):
        span = mover.span(k)
        return [
            pltpu.make_async_copy(rows.at[:, :, span, :], rows_hbm.at[:, :, span, :], save_sems.at[0, k]),
            pltpu.make_async_copy(pre.at[:, :, span, :], pre_hbm.at[:, :, span, :], save_sems.at[1, k]),
            pltpu.make_async_copy(hidden.at[:, span, :], hidden_hbm.at[:, span, :], save_sems.at[2, k]),
        ]

    def compute(k):
        span = mover.span(k)
        if k == 0:
            for load in loads:
                load.wait()
        for e in range(local):
            lhs = jnp.concatenate([rows[s, e, span, :] for s in range(shards)], axis=1)
            gate = dot(lhs, gate_up[e, 0])
            up = dot(lhs, gate_up[e, 1])
            pre[0, e, span, :] = gate
            pre[1, e, span, :] = up
            low = (gelu_parts(gate)[0] * up).astype(BF16)
            hidden[e, span, :] = low
            result = dot(low, down[e]).astype(BF16)
            for s in range(shards):
                part[s, e, span, :] = result[:, s * share : (s + 1) * share]
        for save in saves(k):
            save.start()

    mover.run(compute)
    mover.finish()
    for k in range(mover.steps):
        for save in saves(k):
            save.wait()


def expert_backward(
    groups, shards, local, cap, chunk,
    source, gate_up_hbm, down_hbm, pre_hbm,
    back, rows_hbm, side_hbm,
    rows, part, gate_up, down, pre, side, load_sems, save_sems, *scratch,
):
    mover = Mover(groups, shards, cap, chunk, source, rows, part, back, scratch)
    share = rows.shape[-1]
    loads = [
        pltpu.make_async_copy(gate_up_hbm, gate_up, load_sems.at[0]),
        pltpu.make_async_copy(down_hbm, down, load_sems.at[1]),
        pltpu.make_async_copy(pre_hbm, pre, load_sems.at[2]),
    ]
    for load in loads:
        load.start()

    def saves(k):
        span = mover.span(k)
        return [
            pltpu.make_async_copy(rows.at[:, :, span, :], rows_hbm.at[:, :, span, :], save_sems.at[0, k]),
            pltpu.make_async_copy(side.at[:, :, span, :], side_hbm.at[:, :, span, :], save_sems.at[1, k]),
        ]

    def compute(k):
        span = mover.span(k)
        if k == 0:
            for load in loads:
                load.wait()
        for e in range(local):
            lhs = jnp.concatenate([rows[s, e, span, :] for s in range(shards)], axis=1)
            hidden_grad = dot(lhs, down[e], ((1,), (1,)))
            activated, slope = gelu_parts(pre[0, e, span, :])
            gate_side = (hidden_grad * pre[1, e, span, :] * slope).astype(BF16)
            up_side = (hidden_grad * activated).astype(BF16)
            side[0, e, span, :] = gate_side
            side[1, e, span, :] = up_side
            result = dot(gate_side, gate_up[e, 0], ((1,), (1,))) + dot(up_side, gate_up[e, 1], ((1,), (1,)))
            result = result.astype(BF16)
            for s in range(shards):
                part[s, e, span, :] = result[:, s * share : (s + 1) * share]
        for save in saves(k):
            save.start()

    mover.run(compute)
    mover.finish()
    for k in range(mover.steps):
        for save in saves(k):
            save.wait()


def rms_scale(values):
    return lax.rsqrt(jnp.mean(values * values, axis=-1, keepdims=True) + EPSILON)


def body(
    inputs,
    teacher,
    lengths,
    expert_ids,
    route_slots,
    gain_attn,
    w_qkv,
    w_out,
    rel_table,
    gain_moe,
    w_router,
    w_gate_up,
    w_down,
):
    highest = lax.Precision.HIGHEST
    tok_rows, model_width = inputs.shape
    groups = lax.axis_size("dp")
    shards = lax.axis_size("tensor")
    experts = w_router.shape[1]
    local_experts = w_gate_up.shape[0]
    capacity = 10 * tok_rows // (4 * experts)
    padded_cap = (capacity + 15) // 16 * 16
    slot_count = experts * padded_cap
    heads_here = rel_table.shape[1]
    width_here = w_qkv.shape[2]
    head_width = width_here // heads_here
    share = model_width // shards
    column_start = lax.axis_index("tensor") * share

    def mine(values):
        return lax.dynamic_slice_in_dim(values, column_start, share, values.ndim - 1)

    def gather_columns(values):
        return lax.all_gather(values, "tensor", axis=values.ndim - 1, tiled=True)

    def scatter_columns(values):
        rows = values.shape[0]
        parts = lax.all_to_all(
            values.reshape(rows, shards, share), "tensor", split_axis=1, concat_axis=1, tiled=True
        )
        return jnp.sum(parts.astype(F32), axis=1)

    offsets = jnp.arange(SPAN, dtype=jnp.int32) - SEQ_LEN
    onehot_offsets = bucket_onehot(offsets)
    offset_bias = jnp.dot(onehot_offsets, rel_table, precision=highest).T

    residual = inputs.astype(F32)
    scale_one = rms_scale(residual)
    normed_low = (residual * scale_one * gain_attn).astype(BF16)
    projected = jnp.einsum("td,jde->jte", normed_low, w_qkv, preferred_element_type=F32).astype(BF16)

    attended, probs = pl.pallas_call(
        functools.partial(attention_forward, heads_here, head_width),
        out_shape=(
            jax.ShapeDtypeStruct((tok_rows, width_here), BF16),
            jax.ShapeDtypeStruct((heads_here, SEQ_LEN, SEQ_LEN), F32),
        ),
        in_specs=[SMEM, VMEM, VMEM],
        out_specs=(VMEM, VMEM),
        compiler_params=pltpu.CompilerParams(vmem_limit_bytes=32 * 1024 * 1024),
        name="attention_forward",
    )(lengths, offset_bias, projected)

    w_out_full = lax.all_gather(w_out, "tensor", axis=0, tiled=True)
    attended_full = gather_columns(attended)
    after_attn = residual + jnp.dot(attended_full, w_out_full, preferred_element_type=F32)
    scale_two = rms_scale(after_attn)
    normed_two_low = (after_attn * scale_two * gain_moe).astype(BF16)
    logits = jnp.dot(normed_two_low, w_router, preferred_element_type=F32)
    expert_range = jnp.arange(experts, dtype=jnp.int32)
    picks = (expert_ids[:, :, None] == expert_range[None, None, :]).astype(F32)
    gates, gate_pull = jax.vjp(lambda values: route_gates(values, picks), logits)
    kept_route = route_slots < capacity
    target = jnp.where(kept_route, expert_ids * padded_cap + route_slots, -1)
    slot_range = jnp.arange(slot_count, dtype=jnp.int32)
    route_of = (target[:, :, None] == slot_range[None, None, :]).astype(BF16)
    first_route, second_route = route_of[:, 0], route_of[:, 1]
    any_route = first_route + second_route

    after_mine = mine(after_attn)
    teacher_mine = mine(teacher).astype(F32)
    normed_mine = mine(normed_two_low)
    dispatched = dot(any_route, normed_mine, ((0,), (0,))).astype(BF16)
    chunk = max(groups // 4, 1)
    slots = groups * padded_cap
    block_shape = (groups, local_experts, padded_cap, share)
    rows_type = jax.ShapeDtypeStruct((shards, local_experts, slots, share), BF16)
    back_type = jax.ShapeDtypeStruct(block_shape, BF16)
    ff_here = w_down.shape[1]
    sizes = (groups, shards, local_experts, padded_cap)
    rows_scratch = [
        pltpu.VMEM((shards, local_experts, slots, share), BF16),
        pltpu.VMEM((shards, local_experts, slots, share), BF16),
        pltpu.VMEM(w_gate_up.shape, BF16),
        pltpu.VMEM(w_down.shape, BF16),
        pltpu.VMEM((2, local_experts, slots, ff_here), F32),
    ]
    returned, expert_rows, pre_acts, hidden_low = pl.pallas_call(
        functools.partial(expert_forward, *sizes, chunk),
        out_shape=(
            back_type,
            rows_type,
            jax.ShapeDtypeStruct((2, local_experts, slots, ff_here), F32),
            jax.ShapeDtypeStruct((local_experts, slots, ff_here), BF16),
        ),
        in_specs=[ANY] * 3,
        out_specs=(ANY,) * 4,
        scratch_shapes=rows_scratch
        + [
            pltpu.VMEM((local_experts, slots, ff_here), BF16),
            pltpu.SemaphoreType.DMA((2,)),
            pltpu.SemaphoreType.DMA((3, groups // chunk)),
        ]
        + mover_scratch(*sizes, share, chunk),
        compiler_params=pltpu.CompilerParams(
            vmem_limit_bytes=50 * 1024 * 1024, collective_id=1, has_side_effects=True
        ),
        name="expert_forward",
    )(dispatched.reshape(block_shape), w_gate_up, w_down)
    returned = returned.reshape(slot_count, share)
    routed_first = dot(first_route, returned)
    routed_second = dot(second_route, returned)

    row_alive = (jnp.arange(tok_rows, dtype=jnp.int32) < lengths[0]).astype(F32)[:, None]
    valid_total = lax.psum(lengths[0].astype(F32), "dp")
    scale = groups * tok_rows / valid_total
    block_out = after_mine + gates[:, 0, None] * routed_first + gates[:, 1, None] * routed_second
    deviation = (block_out - teacher_mine) * row_alive
    out_grad = deviation * scale
    squared = lax.psum(jnp.sum(deviation * deviation), ("dp", "tensor"))
    loss = squared / (2.0 * valid_total * model_width)

    slot_grad = (
        dot(first_route, (gates[:, 0, None] * out_grad).astype(BF16), ((0,), (0,)))
        + dot(second_route, (gates[:, 1, None] * out_grad).astype(BF16), ((0,), (0,)))
    ).astype(BF16)
    gate_grad_part = jnp.stack(
        [jnp.sum(routed_first * out_grad, axis=-1), jnp.sum(routed_second * out_grad, axis=-1)],
        axis=1,
    )
    gate_grad = lax.psum(gate_grad_part, "tensor")
    back_grad, expert_grad, pre_grads = pl.pallas_call(
        functools.partial(expert_backward, *sizes, chunk),
        out_shape=(
            back_type,
            rows_type,
            jax.ShapeDtypeStruct((2, local_experts, slots, ff_here), BF16),
        ),
        in_specs=[ANY] * 4,
        out_specs=(ANY,) * 3,
        scratch_shapes=rows_scratch
        + [
            pltpu.VMEM((2, local_experts, slots, ff_here), BF16),
            pltpu.SemaphoreType.DMA((3,)),
            pltpu.SemaphoreType.DMA((2, groups // chunk)),
        ]
        + mover_scratch(*sizes, share, chunk),
        compiler_params=pltpu.CompilerParams(
            vmem_limit_bytes=50 * 1024 * 1024, collective_id=2, has_side_effects=True
        ),
        name="expert_backward",
    )(slot_grad.reshape(block_shape), w_gate_up, w_down, pre_acts)
    back_grad = back_grad.reshape(slot_count, share)
    down_grad = jnp.einsum("xmf,sxmc->xfsc", hidden_low, expert_grad, preferred_element_type=F32)
    down_grad = down_grad.reshape(w_down.shape)
    gate_up_grad = jnp.einsum("sxmc,jxmf->xjscf", expert_rows, pre_grads, preferred_element_type=F32)
    gate_up_grad = gate_up_grad.reshape(w_gate_up.shape)

    logit_grad = gate_pull(gate_grad)[0].astype(BF16)
    router_grad = dot(normed_two_low, logit_grad, ((0,), (0,)))
    normed_two_grad = dot(any_route, back_grad) + mine(dot(logit_grad, w_router, ((1,), (1,))))
    gain_two_mine = mine(gain_moe)

    def rms_back(values, factor, gain, grad):
        projected_part = jnp.sum(grad * gain * values, axis=-1, keepdims=True)
        along = lax.psum(projected_part, "tensor")
        gain_grad = jnp.sum(grad * values * factor, axis=0)
        return factor * (grad * gain - values * (factor * factor * along / model_width)), gain_grad

    after_norm_grad, gain_moe_mine = rms_back(after_mine, scale_two, gain_two_mine, normed_two_grad)
    after_grad = out_grad + after_norm_grad
    branch_grad = gather_columns(after_grad.astype(BF16))
    out_proj_grad = dot(attended, branch_grad, ((0,), (0,)))
    attended_grad = dot(branch_grad, w_out, ((1,), (1,))).astype(BF16)

    projected_grad, diagonals = pl.pallas_call(
        functools.partial(attention_backward, heads_here, head_width),
        out_shape=(
            jax.ShapeDtypeStruct((3, tok_rows, width_here), BF16),
            jax.ShapeDtypeStruct((heads_here, SPAN), F32),
        ),
        in_specs=[VMEM, VMEM, VMEM],
        out_specs=(VMEM, VMEM),
        scratch_shapes=[
            pltpu.VMEM((TILE, SPAN), F32),
            pltpu.VMEM((SEQ_LEN, head_width), F32),
            pltpu.VMEM((SEQ_LEN, head_width), F32),
        ],
        compiler_params=pltpu.CompilerParams(vmem_limit_bytes=32 * 1024 * 1024),
        name="attention_backward",
    )(projected, probs, attended_grad)
    table_grad = jnp.dot(onehot_offsets.T, diagonals.T, precision=highest)

    qkv_grad = jnp.einsum("td,jte->jde", normed_low, projected_grad, preferred_element_type=F32)
    normed_one_part = jnp.einsum("jte,jde->td", projected_grad, w_qkv, preferred_element_type=F32)
    normed_one_grad = scatter_columns(normed_one_part.astype(BF16))
    input_norm_grad, gain_attn_mine = rms_back(
        mine(residual), scale_one, mine(gain_attn), normed_one_grad
    )
    input_grad = after_grad + input_norm_grad

    def place(part):
        whole = jnp.zeros((model_width,), F32)
        return lax.dynamic_update_slice_in_dim(whole, part, column_start, 0)

    gains = lax.psum(jnp.stack([place(gain_attn_mine), place(gain_moe_mine)]), ("dp", "tensor"))
    router_sum = lax.psum(router_grad.astype(BF16), "dp").astype(F32)
    qkv_sum = lax.psum(qkv_grad.astype(BF16), "dp").astype(F32)
    out_proj_sum = lax.psum(out_proj_grad.astype(BF16), "dp").astype(F32)
    table_sum = lax.psum(table_grad, "dp")
    return (
        block_out,
        loss,
        input_grad,
        gains[0],
        qkv_sum,
        out_proj_sum,
        table_sum,
        gains[1],
        router_sum,
        gate_up_grad,
        down_grad,
    )


def solution(mesh):
    placed = (
        P("dp", None),
        P("dp", None),
        P("dp"),
        P("dp", None),
        P("dp", None),
        P(),
        P(None, None, "tensor"),
        P("tensor", None),
        P(None, "tensor"),
        P(),
        P(),
        P("dp", None, None, "tensor"),
        P("dp", "tensor", None),
    )
    return jax.shard_map(
        body,
        mesh=mesh,
        in_specs=placed,
        out_specs=(
            P("dp", "tensor"),
            P(),
            P("dp", "tensor"),
            P(),
            P(None, None, "tensor"),
            P("tensor", None),
            P(None, "tensor"),
            P(),
            P(),
            P("dp", None, None, "tensor"),
            P("dp", "tensor", None),
        ),
        check_vma=False,
    )
```

```python
import functools
import math

import jax
import jax.numpy as jnp
from jax import lax
from jax.experimental import pallas as pl
from jax.experimental.pallas import tpu as pltpu
from jax.sharding import PartitionSpec as P

BUCKETS = 32
SEQ_LEN = 512
TILE = 128
SPAN = 2 * SEQ_LEN

EPSILON = 1e-06
FAR_STEPS = (12, 16, 23, 32, 46, 64, 91)
MASKED = -1000000000.0
F32 = jnp.float32
BF16 = jnp.bfloat16


def offset_bucket(offset):
    direction = jnp.where(offset > 0, 16, 0).astype(jnp.int32)
    distance = jnp.abs(offset)
    farther = jnp.full(offset.shape, 8, jnp.int32)
    for threshold in FAR_STEPS:
        farther = farther + (distance >= threshold).astype(jnp.int32)
    return direction + jnp.where(distance < 8, distance, farther)


def bucket_onehot(offsets):
    bucket_range = jnp.arange(BUCKETS, dtype=jnp.int32)
    return (offset_bucket(offsets)[:, None] == bucket_range[None, :]).astype(F32)


def route_gates(logits, picks):
    expert_probs = jax.nn.softmax(logits, axis=-1)
    chosen = jnp.sum(expert_probs[:, None, :] * picks, axis=-1)
    return chosen / jnp.sum(chosen, axis=-1, keepdims=True)


def dot(a, b, dims=((1,), (0,))):
    return lax.dot_general(a, b, (dims, ((), ())), preferred_element_type=F32)


def attention_forward(heads, width, len_ref, bias_ref, proj_ref, attended_ref, probs_ref):
    length = len_ref[0]
    alive = lax.broadcasted_iota(jnp.int32, (TILE, SEQ_LEN), 1) < length
    for h in range(heads):
        cols = slice(h * width, (h + 1) * width)
        keys = proj_ref[1, :, cols]
        values = proj_ref[2, :, cols]
        skew = pltpu.roll(
            jnp.broadcast_to(bias_ref[h : h + 1, :], (TILE, SPAN)), 0, 1, stride=1, stride_axis=0
        )
        for j in range(SEQ_LEN // TILE):
            rows = slice(j * TILE, (j + 1) * TILE)
            start = SEQ_LEN - j * TILE
            scores = dot(proj_ref[0, rows, cols], keys, ((1,), (1,)))
            scores = jnp.where(alive, scores + skew[:, start : start + SEQ_LEN], MASKED)
            exponent = jnp.exp(scores - jnp.max(scores, axis=1, keepdims=True))
            probs = exponent * (1.0 / jnp.sum(exponent, axis=1, keepdims=True))
            probs_ref[h, rows, :] = probs
            attended_ref[rows, cols] = dot(probs.astype(BF16), values).astype(BF16)


VMEM = pl.BlockSpec(memory_space=pltpu.VMEM)
SMEM = pl.BlockSpec(memory_space=pltpu.SMEM)


MESH_ID = pl.DeviceIdType.MESH
ANY = pl.BlockSpec(memory_space=pl.ANY)


class Mover:
    def __init__(self, groups, shards, cap, chunk, source, rows, part, back, scratch):
        self.groups, self.lines, self.cap, self.chunk = groups, shards // 2, cap, chunk
        self.source, self.rows, self.part, self.back = source, rows, part, back
        (self.mate_in, self.line_out, self.line_in, self.back_out, self.dp_sems, self.row_sems, self.sum_sems) = scratch
        self.me, self.place = lax.axis_index("dp"), lax.axis_index("tensor")
        self.line, self.core = lax.div(self.place, 2), lax.rem(self.place, 2)
        self.steps = groups // chunk

    def group(self, offset):
        return lax.rem(self.me + offset, self.groups)

    def shard(self, offset, core):
        return lax.rem(self.line + offset, self.lines) * 2 + core

    def greet(self):
        barrier = pltpu.get_barrier_semaphore()
        for i in range(1, self.groups):
            pl.semaphore_signal(barrier, inc=1, device_id={"dp": self.group(i)}, device_id_type=MESH_ID)
        for d in range(1, self.lines):
            pl.semaphore_signal(barrier, inc=1, device_id={"tensor": self.shard(d, self.core)}, device_id_type=MESH_ID)
        pl.semaphore_signal(barrier, inc=1, device_id={"tensor": self.shard(0, 1 - self.core)}, device_id_type=MESH_ID)
        pl.semaphore_wait(barrier, self.groups - 1 + self.lines)

    def remote(self, src, dst, sems, index, device):
        return pltpu.make_async_remote_copy(
            src_ref=src, dst_ref=dst, send_sem=sems.at[(0, *index)], recv_sem=sems.at[(1, *index)],
            device_id=device, device_id_type=MESH_ID,
        )

    def here(self, shard, i):
        return self.rows.at[shard, :, pl.ds(i * self.cap, self.cap), :]

    def send_out(self):
        pltpu.make_async_copy(self.source.at[self.me], self.here(self.place, 0), self.dp_sems.at[0, 1, 0]).start()
        for i in range(1, self.groups):
            self.out_copy(i).start()

    def out_copy(self, i):
        to = self.group(i)
        return self.remote(self.source.at[to], self.here(self.place, i), self.dp_sems.at[0], (i,), {"dp": to})

    def line_copy(self, d, i):
        return self.remote(
            self.here(self.place, i), self.here(self.place, i), self.row_sems.at[0], (d, i),
            {"tensor": self.shard(d, self.core)},
        )

    def mate_copy(self, d, i):
        shard = self.shard(self.lines - d, self.core)
        return self.remote(
            self.here(shard, i), self.here(shard, i), self.row_sems.at[1], (d, i),
            {"tensor": self.shard(0, 1 - self.core)},
        )

    def landed(self, where, sems, index):
        self.remote(where, where, sems, index, {"tensor": self.shard(0, 1 - self.core)}).wait_recv()

    def places(self, k):
        return range(k * self.chunk, (k + 1) * self.chunk)

    def spread(self, k):
        for i in self.places(k):
            where = self.here(self.place, i)
            if i == 0:
                pltpu.make_async_copy(self.source.at[self.me], where, self.dp_sems.at[0, 1, 0]).wait()
            else:
                self.landed(where, self.dp_sems.at[0], (i,))
            for d in range(1, self.lines):
                self.line_copy(d, i).start()
            self.mate_copy(0, i).start()

    def relay(self, k):
        for i in self.places(k):
            for d in range(1, self.lines):
                shard = self.shard(self.lines - d, self.core)
                self.landed(self.here(shard, i), self.row_sems.at[0], (d, i))
                self.mate_copy(d, i).start()

    def collect(self, k):
        for i in self.places(k):
            for d in range(self.lines):
                shard = self.shard(self.lines - d, 1 - self.core)
                self.landed(self.here(shard, i), self.row_sems.at[1], (d, i))

    def span(self, k):
        return pl.ds(k * self.chunk * self.cap, self.chunk * self.cap)

    def pair_copy(self, d, k):
        shard = self.shard(d, 1 - self.core)
        return self.remote(
            self.part.at[shard, :, self.span(k), :], self.mate_in.at[d, :, self.span(k), :], self.sum_sems.at[0], (d, k),
            {"tensor": self.shard(0, 1 - self.core)},
        )

    def sum_copy(self, d, k):
        return self.remote(
            self.line_out.at[d, :, self.span(k), :], self.line_in.at[d, :, self.span(k), :], self.sum_sems.at[1], (d, k),
            {"tensor": self.shard(d, self.core)},
        )

    def back_copy(self, i):
        return self.remote(
            self.back_out.at[:, pl.ds(i * self.cap, self.cap), :], self.back.at[self.me], self.dp_sems.at[1], (i,),
            {"dp": self.group(self.groups - i)},
        )

    def pair(self, k):
        for d in range(self.lines):
            self.pair_copy(d, k).start()

    def pair_sum(self, d, k):
        shard = self.shard(d, self.core)
        return self.part[shard, :, self.span(k), :].astype(F32) + self.mate_in[d, :, self.span(k), :].astype(F32)

    def along(self, k):
        for d in range(self.lines):
            self.landed(self.mate_in.at[d, :, self.span(k), :], self.sum_sems.at[0], (d, k))
        for d in range(1, self.lines):
            self.line_out[d, :, self.span(k), :] = self.pair_sum(d, k).astype(BF16)
            self.sum_copy(d, k).start()

    def give(self, k):
        total = self.pair_sum(0, k)
        for d in range(1, self.lines):
            self.landed(self.line_in.at[d, :, self.span(k), :], self.sum_sems.at[1], (d, k))
            total = total + self.line_in[d, :, self.span(k), :].astype(F32)
        self.back_out[:, self.span(k), :] = total.astype(BF16)
        for i in self.places(k):
            if i == 0:
                self.own_back().start()
            else:
                self.back_copy(i).start()

    def own_back(self):
        return pltpu.make_async_copy(
            self.back_out.at[:, pl.ds(0, self.cap), :], self.back.at[self.me], self.dp_sems.at[1, 1, 0]
        )

    def run(self, compute):
        self.send_out()
        for step in range(self.steps + 4):
            for lag, work in enumerate((self.spread, self.relay, compute, self.along, self.give)):
                k = step - lag
                if 0 <= k < self.steps:
                    if lag == 2:
                        self.collect(k)
                    work(k)
                    if lag == 2:
                        self.pair(k)

    def finish(self):
        self.own_back().wait()
        for i in range(1, self.groups):
            where = self.back.at[self.group(i)]
            self.landed(where, self.dp_sems.at[1], (i,))
            self.out_copy(i).wait_send()
            self.back_copy(i).wait_send()
        for i in range(self.groups):
            for d in range(self.lines):
                if d:
                    self.line_copy(d, i).wait_send()
                self.mate_copy(d, i).wait_send()
        for k in range(self.steps):
            for d in range(self.lines):
                if d:
                    self.sum_copy(d, k).wait_send()
                self.pair_copy(d, k).wait_send()


def mover_scratch(groups, shards, local, cap, share, chunk):
    lines, slots, steps = shards // 2, groups * cap, groups // chunk
    return [
        pltpu.VMEM((lines, local, slots, share), BF16),
        pltpu.VMEM((lines, local, slots, share), BF16),
        pltpu.VMEM((lines, local, slots, share), BF16),
        pltpu.VMEM((local, slots, share), BF16),
        pltpu.SemaphoreType.DMA((2, 2, groups)),
        pltpu.SemaphoreType.DMA((2, 2, lines, groups)),
        pltpu.SemaphoreType.DMA((2, 2, lines, steps)),
    ]


ROOT = math.sqrt(2.0 / math.pi)


def gelu_parts(v):
    inner = jnp.tanh(ROOT * (v + 0.044715 * (v * v * v)))
    half = 0.5 * (1.0 + inner)
    slope = half + 0.5 * v * (1.0 - inner * inner) * (ROOT * (1.0 + 3.0 * 0.044715 * v * v))
    return v * half, slope


def expert_forward(
    groups, shards, local, cap, chunk,
    source, gate_up_hbm, down_hbm, count,
    back, rows_hbm, pre_hbm, hidden_hbm, total,
    rows, part, gate_up, down, pre, hidden, load_sems, save_sems, counts, count_sems, *scratch,
):
    mover = Mover(groups, shards, cap, chunk, source, rows, part, back, scratch)
    share = rows.shape[-1]
    loads = [pltpu.make_async_copy(gate_up_hbm, gate_up, load_sems.at[0]), pltpu.make_async_copy(down_hbm, down, load_sems.at[1])]
    for load in loads:
        load.start()

    def saves(k):
        span = mover.span(k)
        return [
            pltpu.make_async_copy(rows.at[:, :, span, :], rows_hbm.at[:, :, span, :], save_sems.at[0, k]),
            pltpu.make_async_copy(pre.at[:, :, span, :], pre_hbm.at[:, :, span, :], save_sems.at[1, k]),
            pltpu.make_async_copy(hidden.at[:, span, :], hidden_hbm.at[:, span, :], save_sems.at[2, k]),
        ]

    def compute(k):
        span = mover.span(k)
        if k == 0:
            for load in loads:
                load.wait()
        for e in range(local):
            lhs = jnp.concatenate([rows[s, e, span, :] for s in range(shards)], axis=1)
            gate = dot(lhs, gate_up[e, 0], ((1,), (1,)))
            up = dot(lhs, gate_up[e, 1], ((1,), (1,)))
            pre[0, e, span, :] = gate
            pre[1, e, span, :] = up
            low = (gelu_parts(gate)[0] * up).astype(BF16)
            hidden[e, span, :] = low
            result = dot(low, down[e]).astype(BF16)
            for s in range(shards):
                part[s, e, span, :] = result[:, s * share : (s + 1) * share]
        for save in saves(k):
            save.start()

    def count_copy(i):
        return mover.remote(count, counts.at[i], count_sems, (i,), {"dp": mover.group(i)})

    mover.greet()
    for i in range(1, groups):
        count_copy(i).start()
    mover.run(compute)
    tally = count[...]
    for i in range(1, groups):
        count_copy(i).wait()
        tally = tally + counts[i]
    total[...] = tally
    mover.finish()
    for k in range(mover.steps):
        for save in saves(k):
            save.wait()


def expert_backward(
    groups, shards, local, cap, chunk,
    source, gate_up_hbm, down_hbm, pre_hbm,
    back, rows_hbm, side_hbm,
    rows, part, gate_up, down, pre, side, load_sems, save_sems, *scratch,
):
    mover = Mover(groups, shards, cap, chunk, source, rows, part, back, scratch)
    share = rows.shape[-1]
    loads = [
        pltpu.make_async_copy(gate_up_hbm, gate_up, load_sems.at[0]),
        pltpu.make_async_copy(down_hbm, down, load_sems.at[1]),
        pltpu.make_async_copy(pre_hbm, pre, load_sems.at[2]),
    ]
    for load in loads:
        load.start()

    def saves(k):
        span = mover.span(k)
        return [
            pltpu.make_async_copy(rows.at[:, :, span, :], rows_hbm.at[:, :, span, :], save_sems.at[0, k]),
            pltpu.make_async_copy(side.at[:, :, span, :], side_hbm.at[:, :, span, :], save_sems.at[1, k]),
        ]

    def compute(k):
        span = mover.span(k)
        if k == 0:
            for load in loads:
                load.wait()
        for e in range(local):
            lhs = jnp.concatenate([rows[s, e, span, :] for s in range(shards)], axis=1)
            hidden_grad = dot(lhs, down[e], ((1,), (1,)))
            activated, slope = gelu_parts(pre[0, e, span, :])
            gate_side = (hidden_grad * pre[1, e, span, :] * slope).astype(BF16)
            up_side = (hidden_grad * activated).astype(BF16)
            side[0, e, span, :] = gate_side
            side[1, e, span, :] = up_side
            result = dot(gate_side, gate_up[e, 0]) + dot(up_side, gate_up[e, 1])
            result = result.astype(BF16)
            for s in range(shards):
                part[s, e, span, :] = result[:, s * share : (s + 1) * share]
        for save in saves(k):
            save.start()

    mover.greet()
    mover.run(compute)
    mover.finish()
    for k in range(mover.steps):
        for save in saves(k):
            save.wait()


def weight_grads(shards, rows, grads, side, hidden, gate_up_out, down_out):
    step = pl.program_id(1)
    share = rows.shape[-1]

    @pl.when(step < 2)
    def _():
        for s in range(shards):
            gate_up_out[:, s * share : (s + 1) * share] = dot(side[...], rows[s], ((0,), (0,)))

    @pl.when(step == 2)
    def _():
        for s in range(shards):
            down_out[:, s * share : (s + 1) * share] = dot(hidden[...], grads[s], ((0,), (0,)))


def to_row(column):
    rows = column.shape[0]
    return jnp.transpose(jnp.broadcast_to(column, (rows, 128)))[:8]


def to_column(row):
    return jnp.transpose(jnp.broadcast_to(row[:1], (128, row.shape[1])))[:, :1]


def dense_backward(
    groups, shards, heads, width, experts,
    norm_grad, after, out_grad, residual, scales, gains, extras_in, onehot,
    attended_hbm, w_out_hbm, proj_hbm, probs_hbm, normed_hbm, w_qkv_hbm,
    dense_out, input_grad, extras_out,
    attended, w_out, proj, probs, normed, w_qkv, load_sems,
    dots, dot_sems, branch, branch_sems, grad_here, diag, key_acc, value_acc, proj_grad,
    part, mate_in, line_out, line_in, part_sems,
    dense, result, y_in, y_sum, z_in, dense_sems, z_sems, save_sems,
    extras, extras_in_dp, extras_sems, extras_ring_sems,
):
    model = normed.shape[1]
    share = branch.shape[-1]
    tokens = branch.shape[1]
    here = heads * width
    lines = shards // 2
    y_size = 1 << ((groups.bit_length() - 1) // 2)
    z_size = groups // y_size
    pieces = dense.shape[0]
    me, place = lax.axis_index("dp"), lax.axis_index("tensor")
    line, core = lax.div(place, 2), lax.rem(place, 2)
    z, y = lax.div(me, y_size), lax.rem(me, y_size)
    mate = {"tensor": line * 2 + 1 - core}
    inverse = 1.0 / model

    def group(i):
        return lax.rem(me + i, groups)

    def shard(d, c):
        return lax.rem(line + d, lines) * 2 + c

    def near(i):
        return lax.rem(place + i, shards)

    def remote(src, dst, sems, index, device):
        return pltpu.make_async_remote_copy(
            src_ref=src, dst_ref=dst, send_sem=sems.at[(0, *index)], recv_sem=sems.at[(1, *index)],
            device_id=device, device_id_type=MESH_ID,
        )

    def landed(where, sems, index):
        remote(where, where, sems, index, mate).wait_recv()

    loads = [
        pltpu.make_async_copy(src, dst, load_sems.at[n])
        for n, (src, dst) in enumerate(
            (
                (w_out_hbm, w_out), (attended_hbm, attended), (proj_hbm, proj), (probs_hbm, probs),
                (w_qkv_hbm, w_qkv), (normed_hbm, normed),
            )
        )
    ]
    for load in loads:
        load.start()

    barrier = pltpu.get_barrier_semaphore()
    for i in range(1, groups):
        pl.semaphore_signal(barrier, inc=1, device_id={"dp": group(i)}, device_id_type=MESH_ID)
    for i in range(1, shards):
        pl.semaphore_signal(barrier, inc=1, device_id={"tensor": near(i)}, device_id_type=MESH_ID)
    pl.semaphore_wait(barrier, groups + shards - 2)

    def dot_copy(n, i):
        return remote(dots.at[n, 0], dots.at[n, i], dot_sems, (n, i), {"tensor": near(i)})

    def dot_send(n, column):
        dots[n, 0] = to_row(column)
        for i in range(1, shards):
            dot_copy(n, i).start()

    def dot_sum(n):
        total = dots[n, 0]
        for i in range(1, shards):
            dot_copy(n, i).wait()
            total = total + dots[n, i]
        return to_column(total)

    scale_two = scales[:, 1:2]
    weighted = norm_grad[...] * gains[1:2, :]
    dot_send(0, jnp.sum(weighted * after[...], axis=1, keepdims=True))
    extras[0] = extras_in[...]
    extras[0, experts + 1 : experts + 2, :] = jnp.sum(norm_grad[...] * after[...] * scale_two, axis=0, keepdims=True)
    along = dot_sum(0)
    after_grad = out_grad[...] + scale_two * (weighted - after[...] * (scale_two * scale_two * along * inverse))
    grad_here[...] = after_grad
    branch[place] = after_grad.astype(BF16)

    blocks = tokens // TILE

    def row_block(j):
        return pl.ds(j * TILE, TILE)

    def branch_line(d, j):
        where = branch.at[place, row_block(j), :]
        return remote(where, where, branch_sems.at[0], (d, j), {"tensor": shard(d, core)})

    def branch_mate(d, j):
        where = branch.at[shard(lines - d, core), row_block(j), :]
        return remote(where, where, branch_sems.at[1], (d, j), mate)

    for j in range(blocks):
        for d in range(1, lines):
            branch_line(d, j).start()
        branch_mate(0, j).start()
    for j in range(blocks):
        for d in range(1, lines):
            landed(branch.at[shard(lines - d, core), row_block(j), :], branch_sems.at[0], (d, j))
            branch_mate(d, j).start()
    for j in range(blocks):
        for d in range(lines):
            landed(branch.at[shard(lines - d, 1 - core), row_block(j), :], branch_sems.at[1], (d, j))
    loads[0].wait()
    loads[1].wait()

    y_rows, z_rows = model // y_size, model // groups

    def y_copy(p, a):
        to = lax.rem(y + a, y_size)
        return remote(
            dense.at[p, pl.ds(to * y_rows, y_rows), :], y_in.at[p, a], dense_sems.at[0], (p, a), {"dp": z * y_size + to}
        )

    def z_copy(p, b):
        to = lax.rem(z + b, z_size)
        return remote(
            y_sum.at[p, pl.ds(to * z_rows, z_rows), :], z_in.at[p, b], z_sems.at[0], (p, b), {"dp": to * y_size + y}
        )

    def z_spread(p, b):
        to = lax.rem(z + b, z_size)
        where = result.at[p, pl.ds(y * y_rows + z * z_rows, z_rows), :]
        return remote(where, where, z_sems.at[1], (p, b), {"dp": to * y_size + y})

    def y_spread(p, a):
        to = lax.rem(y + a, y_size)
        where = result.at[p, pl.ds(y * y_rows, y_rows), :]
        return remote(where, where, dense_sems.at[1], (p, a), {"dp": z * y_size + to})

    def reduce_start(p):
        for a in range(1, y_size):
            y_copy(p, a).start()

    def reduce_y(p):
        total = dense[p, pl.ds(y * y_rows, y_rows), :].astype(F32)
        for a in range(1, y_size):
            landed(y_in.at[p, a], dense_sems.at[0], (p, a))
            total = total + y_in[p, a].astype(F32)
        y_sum[p] = total.astype(BF16)
        for b in range(1, z_size):
            z_copy(p, b).start()

    def reduce_z(p):
        total = y_sum[p, pl.ds(z * z_rows, z_rows), :].astype(F32)
        for a in range(1, y_size):
            y_copy(p, a).wait_send()
        for b in range(1, z_size):
            landed(z_in.at[p, b], z_sems.at[0], (p, b))
            total = total + z_in[p, b].astype(F32)
        result[p, pl.ds(y * y_rows + z * z_rows, z_rows), :] = total.astype(BF16)
        for b in range(1, z_size):
            z_spread(p, b).start()

    def spread_z(p):
        for b in range(1, z_size):
            origin = lax.rem(z + z_size - b, z_size)
            landed(result.at[p, pl.ds(y * y_rows + origin * z_rows, z_rows), :], z_sems.at[1], (p, b))
        for a in range(1, y_size):
            y_spread(p, a).start()

    def save(p):
        return pltpu.make_async_copy(result.at[p], dense_out.at[p], save_sems.at[p])

    def spread_y(p):
        for a in range(1, y_size):
            origin = lax.rem(y + y_size - a, y_size)
            landed(result.at[p, pl.ds(origin * y_rows, y_rows), :], dense_sems.at[1], (p, a))
        save(p).start()

    for s in range(shards):
        dense[0, s * here : (s + 1) * here, :] = dot(
            attended[...], branch[s], ((0,), (0,))
        ).astype(BF16)
    reduce_start(0)

    loads[2].wait()
    loads[3].wait()
    diag[...] = jnp.zeros_like(diag)
    for j in range(blocks):
        rows = slice(j * TILE, (j + 1) * TILE)
        start = SEQ_LEN - j * TILE
        wide = jnp.concatenate([branch[s, rows, :] for s in range(shards)], axis=1)
        grads = dot(wide, w_out[...], ((1,), (1,))).astype(BF16)
        for h in range(heads):
            cols = slice(h * width, (h + 1) * width)
            p = probs[h, rows, :]
            grad = grads[:, cols]
            prob_grad = dot(grad, proj[2, :, cols], ((1,), (1,)))
            score_grad = p * (prob_grad - jnp.sum(p * prob_grad, axis=1, keepdims=True))
            diag[h, :, start : start + SEQ_LEN] += score_grad
            low = score_grad.astype(BF16)
            proj_grad[0, rows, cols] = dot(low, proj[1, :, cols]).astype(BF16)
            key_part = dot(low, proj[0, rows, cols], ((0,), (0,)))
            value_part = dot(p.astype(BF16), grad, ((0,), (0,)))
            if j == 0:
                key_acc[:, cols] = key_part
                value_acc[:, cols] = value_part
            else:
                key_acc[:, cols] += key_part
                value_acc[:, cols] += value_part
        if j == 1:
            reduce_y(0)
    proj_grad[1] = key_acc[...].astype(BF16)
    proj_grad[2] = value_acc[...].astype(BF16)
    reduce_z(0)

    loads[4].wait()
    loads[5].wait()
    for p in range(1, pieces):
        dense[p] = dot(normed[...], proj_grad[p - 1], ((0,), (0,))).astype(BF16)
        reduce_start(p)
    half = tokens // 2

    def part_rows(k):
        return pl.ds(k * half, half)

    def pair_copy(d, k):
        return remote(
            part.at[shard(d, 1 - core), part_rows(k), :], mate_in.at[d, part_rows(k), :], part_sems.at[0], (d, k), mate
        )

    def line_copy(d, k):
        return remote(
            line_out.at[d, part_rows(k), :], line_in.at[d, part_rows(k), :], part_sems.at[1], (d, k),
            {"tensor": shard(d, core)},
        )

    for k in range(2):
        rows = slice(k * half, (k + 1) * half)
        total = dot(proj_grad[0, rows, :], w_qkv[0], ((1,), (1,)))
        for n in range(1, 3):
            total = total + dot(proj_grad[n, rows, :], w_qkv[n], ((1,), (1,)))
        low = total.astype(BF16)
        for s in range(shards):
            part[s, rows, :] = low[:, s * share : (s + 1) * share]
        for d in range(lines):
            pair_copy(d, k).start()
    spread_z(0)

    def pair_sum(d, rows):
        return part[shard(d, core), rows, :].astype(F32) + mate_in[d, rows, :].astype(F32)

    for k in range(2):
        rows = part_rows(k)
        for d in range(lines):
            landed(mate_in.at[d, rows, :], part_sems.at[0], (d, k))
        for d in range(1, lines):
            line_out[d, rows, :] = pair_sum(d, rows).astype(BF16)
            line_copy(d, k).start()
    for h in range(heads):
        total = diag[h]
        size = TILE // 2
        while size >= 1:
            total = total[:size] + pltpu.roll(total[size : 2 * size], SPAN - size, 1)
            size //= 2
        row = jnp.broadcast_to(total, (8, SPAN))
        high = row.astype(BF16)
        middle = (row - high.astype(F32)).astype(BF16)
        low = (row - high.astype(F32) - middle.astype(F32)).astype(BF16)
        table = dot(high, onehot[...]) + dot(middle, onehot[...]) + dot(low, onehot[...])
        extras[0, experts + 4 + h : experts + 5 + h, : onehot.shape[1]] = table[:1]
    for p in range(1, pieces):
        reduce_y(p)

    total = pair_sum(0, pl.ds(0, tokens))
    for k in range(2):
        for d in range(1, lines):
            landed(line_in.at[d, part_rows(k), :], part_sems.at[1], (d, k))
    for d in range(1, lines):
        total = total + line_in[d].astype(F32)
    scale_one = scales[:, 0:1]
    values = residual[...].astype(F32)
    weighted = total * gains[0:1, :]
    dot_send(1, jnp.sum(weighted * values, axis=1, keepdims=True))
    extras[0, experts : experts + 1, :] = jnp.sum(total * values * scale_one, axis=0, keepdims=True)

    def extras_copy(i):
        return remote(extras.at[0], extras_in_dp.at[i], extras_sems, (i,), {"dp": group(i)})

    for i in range(1, groups):
        extras_copy(i).start()
    for p in range(1, pieces):
        reduce_z(p)
    along = dot_sum(1)
    input_grad[...] = grad_here[...] + scale_one * (weighted - values * (scale_one * scale_one * along * inverse))

    summed = extras[0]
    for i in range(1, groups):
        extras_copy(i).wait()
        summed = summed + extras_in_dp[i]
    extras_out[place] = summed

    def ring_copy(i):
        return remote(extras_out.at[place], extras_out.at[place], extras_ring_sems, (i,), {"tensor": near(i)})

    for i in range(1, shards):
        ring_copy(i).start()
    for p in range(1, pieces):
        spread_z(p)
    for p in range(pieces):
        spread_y(p)
    for i in range(1, shards):
        landed(extras_out.at[near(shards - i)], extras_ring_sems, (i,))
        ring_copy(i).wait_send()
    for j in range(blocks):
        for d in range(lines):
            if d:
                branch_line(d, j).wait_send()
            branch_mate(d, j).wait_send()
    for k in range(2):
        for d in range(lines):
            if d:
                line_copy(d, k).wait_send()
            pair_copy(d, k).wait_send()
    for p in range(pieces):
        for b in range(1, z_size):
            z_copy(p, b).wait_send()
            z_spread(p, b).wait_send()
        for a in range(1, y_size):
            y_spread(p, a).wait_send()
        save(p).wait()


def rms_scale(values):
    return lax.rsqrt(jnp.mean(values * values, axis=-1, keepdims=True) + EPSILON)


def body(
    inputs,
    teacher,
    lengths,
    expert_ids,
    route_slots,
    gain_attn,
    w_qkv,
    w_out,
    rel_table,
    gain_moe,
    w_router,
    w_gate_up,
    w_down,
):
    highest = lax.Precision.HIGHEST
    tok_rows, model_width = inputs.shape
    groups = lax.axis_size("dp")
    shards = lax.axis_size("tensor")
    experts = w_router.shape[1]
    local_experts = w_gate_up.shape[0]
    capacity = 10 * tok_rows // (4 * experts)
    padded_cap = (capacity + 15) // 16 * 16
    slot_count = experts * padded_cap
    heads_here = rel_table.shape[1]
    width_here = w_qkv.shape[2]
    head_width = width_here // heads_here
    share = model_width // shards
    column_start = lax.axis_index("tensor") * share

    def mine(values):
        return lax.dynamic_slice_in_dim(values, column_start, share, values.ndim - 1)

    def gather_columns(values):
        return lax.all_gather(values, "tensor", axis=values.ndim - 1, tiled=True)

    offsets = jnp.arange(SPAN, dtype=jnp.int32) - SEQ_LEN
    onehot_offsets = bucket_onehot(offsets)
    offset_bias = jnp.dot(onehot_offsets, rel_table, precision=highest).T

    residual = inputs.astype(F32)
    scale_one = rms_scale(residual)
    normed_low = (residual * scale_one * gain_attn).astype(BF16)
    projected = jnp.einsum("td,jde->jte", normed_low, w_qkv, preferred_element_type=F32).astype(BF16)

    attended, probs = pl.pallas_call(
        functools.partial(attention_forward, heads_here, head_width),
        out_shape=(
            jax.ShapeDtypeStruct((tok_rows, width_here), BF16),
            jax.ShapeDtypeStruct((heads_here, SEQ_LEN, SEQ_LEN), F32),
        ),
        in_specs=[SMEM, VMEM, VMEM],
        out_specs=(VMEM, VMEM),
        compiler_params=pltpu.CompilerParams(vmem_limit_bytes=32 * 1024 * 1024),
        name="attention_forward",
    )(lengths, offset_bias, projected)

    w_out_full = lax.all_gather(w_out, "tensor", axis=0, tiled=True)
    attended_full = gather_columns(attended)
    after_attn = residual + jnp.dot(attended_full, w_out_full, preferred_element_type=F32)
    scale_two = rms_scale(after_attn)
    normed_two_low = (after_attn * scale_two * gain_moe).astype(BF16)
    logits = jnp.dot(normed_two_low, w_router, preferred_element_type=F32)
    expert_range = jnp.arange(experts, dtype=jnp.int32)
    picks = (expert_ids[:, :, None] == expert_range[None, None, :]).astype(F32)
    gates, gate_pull = jax.vjp(lambda values: route_gates(values, picks), logits)
    kept_route = route_slots < capacity
    target = jnp.where(kept_route, expert_ids * padded_cap + route_slots, -1)
    slot_range = jnp.arange(slot_count, dtype=jnp.int32)
    route_of = (target[:, :, None] == slot_range[None, None, :]).astype(BF16)
    first_route, second_route = route_of[:, 0], route_of[:, 1]
    any_route = first_route + second_route

    after_mine = mine(after_attn)
    teacher_mine = mine(teacher).astype(F32)
    normed_mine = mine(normed_two_low)
    dispatched = dot(any_route, normed_mine, ((0,), (0,))).astype(BF16)
    gate_up_t = jnp.swapaxes(w_gate_up, 2, 3)
    chunk = max(groups // 4, 1)
    slots = groups * padded_cap
    block_shape = (groups, local_experts, padded_cap, share)
    rows_type = jax.ShapeDtypeStruct((shards, local_experts, slots, share), BF16)
    back_type = jax.ShapeDtypeStruct(block_shape, BF16)
    ff_here = w_down.shape[1]
    sizes = (groups, shards, local_experts, padded_cap)
    rows_scratch = [
        pltpu.VMEM((shards, local_experts, slots, share), BF16),
        pltpu.VMEM((shards, local_experts, slots, share), BF16),
        pltpu.VMEM(gate_up_t.shape, BF16),
        pltpu.VMEM(w_down.shape, BF16),
        pltpu.VMEM((2, local_experts, slots, ff_here), F32),
    ]
    returned, expert_rows, pre_acts, hidden_low, count_total = pl.pallas_call(
        functools.partial(expert_forward, *sizes, chunk),
        out_shape=(
            back_type,
            rows_type,
            jax.ShapeDtypeStruct((2, local_experts, slots, ff_here), F32),
            jax.ShapeDtypeStruct((local_experts, slots, ff_here), BF16),
            jax.ShapeDtypeStruct((8, 128), jnp.int32),
        ),
        in_specs=[ANY] * 3 + [VMEM],
        out_specs=(ANY,) * 4 + (VMEM,),
        scratch_shapes=rows_scratch
        + [
            pltpu.VMEM((local_experts, slots, ff_here), BF16),
            pltpu.SemaphoreType.DMA((2,)),
            pltpu.SemaphoreType.DMA((3, groups // chunk)),
            pltpu.VMEM((groups, 8, 128), jnp.int32),
            pltpu.SemaphoreType.DMA((2, groups)),
        ]
        + mover_scratch(*sizes, share, chunk),
        compiler_params=pltpu.CompilerParams(
            vmem_limit_bytes=50 * 1024 * 1024, collective_id=1, has_side_effects=True
        ),
        name="expert_forward",
    )(dispatched.reshape(block_shape), gate_up_t, w_down, jnp.broadcast_to(lengths, (8, 128)))
    returned = returned.reshape(slot_count, share)
    routed_first = dot(first_route, returned)
    routed_second = dot(second_route, returned)

    row_alive = (jnp.arange(tok_rows, dtype=jnp.int32) < lengths[0]).astype(F32)[:, None]
    valid_total = count_total[0, 0].astype(F32)
    scale = groups * tok_rows / valid_total
    block_out = after_mine + gates[:, 0, None] * routed_first + gates[:, 1, None] * routed_second
    deviation = (block_out - teacher_mine) * row_alive
    out_grad = deviation * scale
    slot_grad = (
        dot(first_route, (gates[:, 0, None] * out_grad).astype(BF16), ((0,), (0,)))
        + dot(second_route, (gates[:, 1, None] * out_grad).astype(BF16), ((0,), (0,)))
    ).astype(BF16)
    gate_grad_part = jnp.stack(
        [jnp.sum(routed_first * out_grad, axis=-1), jnp.sum(routed_second * out_grad, axis=-1)],
        axis=1,
    )
    gate_grad = lax.psum(gate_grad_part, "tensor")
    back_grad, expert_grad, pre_grads = pl.pallas_call(
        functools.partial(expert_backward, *sizes, chunk),
        out_shape=(
            back_type,
            rows_type,
            jax.ShapeDtypeStruct((2, local_experts, slots, ff_here), BF16),
        ),
        in_specs=[ANY] * 4,
        out_specs=(ANY,) * 3,
        scratch_shapes=rows_scratch
        + [
            pltpu.VMEM((2, local_experts, slots, ff_here), BF16),
            pltpu.SemaphoreType.DMA((3,)),
            pltpu.SemaphoreType.DMA((2, groups // chunk)),
        ]
        + mover_scratch(*sizes, share, chunk),
        compiler_params=pltpu.CompilerParams(
            vmem_limit_bytes=50 * 1024 * 1024, collective_id=2, has_side_effects=True
        ),
        name="expert_backward",
    )(slot_grad.reshape(block_shape), gate_up_t, w_down, pre_acts)
    back_grad = back_grad.reshape(slot_count, share)
    gate_up_grad, down_grad = pl.pallas_call(
        functools.partial(weight_grads, shards),
        grid=(local_experts, 3),
        out_shape=(
            jax.ShapeDtypeStruct(gate_up_t.shape, F32),
            jax.ShapeDtypeStruct(w_down.shape, F32),
        ),
        in_specs=[
            pl.BlockSpec((shards, None, slots, share), lambda e, j: (0, e, 0, 0)),
            pl.BlockSpec((shards, None, slots, share), lambda e, j: (0, e, 0, 0)),
            pl.BlockSpec((None, None, slots, ff_here), lambda e, j: (jnp.minimum(j, 1), e, 0, 0)),
            pl.BlockSpec((None, slots, ff_here), lambda e, j: (e, 0, 0)),
        ],
        out_specs=(
            pl.BlockSpec((None, None, ff_here, model_width), lambda e, j: (e, jnp.minimum(j, 1), 0, 0)),
            pl.BlockSpec((None, ff_here, model_width), lambda e, j: (e, 0, 0)),
        ),
        compiler_params=pltpu.CompilerParams(vmem_limit_bytes=48 * 1024 * 1024),
        name="weight_grads",
    )(expert_rows, expert_grad, pre_grads, hidden_low)
    gate_up_grad = jnp.swapaxes(gate_up_grad, 2, 3)

    logit_grad = gate_pull(gate_grad)[0].astype(BF16)
    router_mine = dot(logit_grad, normed_mine, ((0,), (0,)))
    normed_two_grad = dot(any_route, back_grad) + mine(dot(logit_grad, w_router, ((1,), (1,))))
    squared = jnp.sum(deviation * deviation)
    extra_rows = experts + 8
    extras = jnp.concatenate(
        [router_mine, jnp.zeros((2, share), F32), jnp.broadcast_to(squared, (1, share)), jnp.zeros((5, share), F32)]
    )
    y_size = 1 << ((groups.bit_length() - 1) // 2)
    z_size = groups // y_size
    lines = shards // 2
    blocks = tok_rows // TILE
    pieces = 1 + 3
    dense, input_grad, extras = pl.pallas_call(
        functools.partial(dense_backward, groups, shards, heads_here, head_width, experts),
        out_shape=(
            jax.ShapeDtypeStruct((pieces, model_width, width_here), BF16),
            jax.ShapeDtypeStruct((tok_rows, share), F32),
            jax.ShapeDtypeStruct((shards, extra_rows, share), F32),
        ),
        in_specs=[VMEM] * 8 + [ANY] * 6,
        out_specs=(ANY, VMEM, VMEM),
        scratch_shapes=[
            pltpu.VMEM(attended.shape, BF16),
            pltpu.VMEM(w_out.shape, BF16),
            pltpu.VMEM(projected.shape, BF16),
            pltpu.VMEM(probs.shape, F32),
            pltpu.VMEM(normed_low.shape, BF16),
            pltpu.VMEM(w_qkv.shape, BF16),
            pltpu.SemaphoreType.DMA((6,)),
            pltpu.VMEM((2, shards, 8, tok_rows), F32),
            pltpu.SemaphoreType.DMA((2, 2, shards)),
            pltpu.VMEM((shards, tok_rows, share), BF16),
            pltpu.SemaphoreType.DMA((2, 2, lines, blocks)),
            pltpu.VMEM((tok_rows, share), F32),
            pltpu.VMEM((heads_here, TILE, SPAN), F32),
            pltpu.VMEM((SEQ_LEN, width_here), F32),
            pltpu.VMEM((SEQ_LEN, width_here), F32),
            pltpu.VMEM((3, tok_rows, width_here), BF16),
            pltpu.VMEM((shards, tok_rows, share), BF16),
            pltpu.VMEM((lines, tok_rows, share), BF16),
            pltpu.VMEM((lines, tok_rows, share), BF16),
            pltpu.VMEM((lines, tok_rows, share), BF16),
            pltpu.SemaphoreType.DMA((2, 2, lines, 2)),
            pltpu.VMEM((pieces, model_width, width_here), BF16),
            pltpu.VMEM((pieces, model_width, width_here), BF16),
            pltpu.VMEM((pieces, y_size, model_width // y_size, width_here), BF16),
            pltpu.VMEM((pieces, model_width // y_size, width_here), BF16),
            pltpu.VMEM((pieces, z_size, model_width // groups, width_here), BF16),
            pltpu.SemaphoreType.DMA((2, 2, pieces, y_size)),
            pltpu.SemaphoreType.DMA((2, 2, pieces, z_size)),
            pltpu.SemaphoreType.DMA((pieces,)),
            pltpu.VMEM((1, extra_rows, share), F32),
            pltpu.VMEM((groups, extra_rows, share), F32),
            pltpu.SemaphoreType.DMA((2, groups)),
            pltpu.SemaphoreType.DMA((2, shards)),
        ],
        compiler_params=pltpu.CompilerParams(
            vmem_limit_bytes=50 * 1024 * 1024, collective_id=3, has_side_effects=True
        ),
        name="dense_backward",
    )(
        normed_two_grad,
        after_mine,
        out_grad,
        mine(inputs),
        jnp.concatenate([scale_one, scale_two], axis=1),
        mine(jnp.stack([gain_attn, gain_moe])),
        extras,
        onehot_offsets.astype(BF16),
        attended,
        w_out,
        projected,
        probs,
        normed_low,
        w_qkv,
    )
    loss = jnp.sum(extras[:, experts + 2, 0]) / (2.0 * valid_total * model_width)
    whole = jnp.swapaxes(extras, 0, 1).reshape(extra_rows, model_width)
    table_rows = lax.dynamic_index_in_dim(extras, lax.axis_index("tensor"), 0, keepdims=False)
    table_sum = table_rows[experts + 4 : experts + 4 + heads_here, :BUCKETS].T
    out_proj_sum = jnp.swapaxes(dense[0].reshape(shards, width_here, width_here), 0, 1)
    return (
        block_out,
        loss,
        input_grad,
        whole[experts],
        dense[1:].astype(F32),
        out_proj_sum.reshape(width_here, model_width).astype(F32),
        table_sum,
        whole[experts + 1],
        whole[:experts].T,
        gate_up_grad,
        down_grad,
    )


def solution(mesh):
    placed = (
        P("dp", None),
        P("dp", None),
        P("dp"),
        P("dp", None),
        P("dp", None),
        P(),
        P(None, None, "tensor"),
        P("tensor", None),
        P(None, "tensor"),
        P(),
        P(),
        P("dp", None, None, "tensor"),
        P("dp", "tensor", None),
    )
    return jax.shard_map(
        body,
        mesh=mesh,
        in_specs=placed,
        out_specs=(
            P("dp", "tensor"),
            P(),
            P("dp", "tensor"),
            P(),
            P(None, None, "tensor"),
            P("tensor", None),
            P(None, "tensor"),
            P(),
            P(),
            P("dp", None, None, "tensor"),
            P("dp", "tensor", None),
        ),
        check_vma=False,
    )
```

```python
import functools
import math

import jax
import jax.numpy as jnp
from jax import lax
from jax.experimental import pallas as pl
from jax.experimental.pallas import tpu as pltpu
from jax.sharding import PartitionSpec as P

BUCKETS = 32
SEQ_LEN = 512
TILE = 128
SPAN = 2 * SEQ_LEN

EPSILON = 1e-06
FAR_STEPS = (12, 16, 23, 32, 46, 64, 91)
MASKED = -1000000000.0
F32 = jnp.float32
BF16 = jnp.bfloat16


def offset_bucket(offset):
    direction = jnp.where(offset > 0, 16, 0).astype(jnp.int32)
    distance = jnp.abs(offset)
    farther = jnp.full(offset.shape, 8, jnp.int32)
    for threshold in FAR_STEPS:
        farther = farther + (distance >= threshold).astype(jnp.int32)
    return direction + jnp.where(distance < 8, distance, farther)


def bucket_onehot(offsets):
    bucket_range = jnp.arange(BUCKETS, dtype=jnp.int32)
    return (offset_bucket(offsets)[:, None] == bucket_range[None, :]).astype(F32)


def dot(a, b, dims=((1,), (0,))):
    return lax.dot_general(a, b, (dims, ((), ())), preferred_element_type=F32)


VMEM = pl.BlockSpec(memory_space=pltpu.VMEM)
SMEM = pl.BlockSpec(memory_space=pltpu.SMEM)


MESH_ID = pl.DeviceIdType.MESH
ANY = pl.BlockSpec(memory_space=pl.ANY)


class Mover:
    def __init__(self, groups, shards, cap, chunk, source, rows, part, back, scratch):
        self.groups, self.lines, self.cap, self.chunk = groups, shards // 2, cap, chunk
        self.source, self.rows, self.part, self.back = source, rows, part, back
        (self.mate_in, self.line_out, self.line_in, self.back_out, self.dp_sems, self.row_sems, self.sum_sems) = scratch
        self.me, self.place = lax.axis_index("dp"), lax.axis_index("tensor")
        self.line, self.core = lax.div(self.place, 2), lax.rem(self.place, 2)
        self.steps = groups // chunk

    def group(self, offset):
        return lax.rem(self.me + offset, self.groups)

    def shard(self, offset, core):
        return lax.rem(self.line + offset, self.lines) * 2 + core

    def greet(self):
        barrier = pltpu.get_barrier_semaphore()
        for i in range(1, self.groups):
            pl.semaphore_signal(barrier, inc=1, device_id={"dp": self.group(i)}, device_id_type=MESH_ID)
        for d in range(1, self.lines):
            pl.semaphore_signal(barrier, inc=1, device_id={"tensor": self.shard(d, self.core)}, device_id_type=MESH_ID)
        pl.semaphore_signal(barrier, inc=1, device_id={"tensor": self.shard(0, 1 - self.core)}, device_id_type=MESH_ID)
        pl.semaphore_wait(barrier, self.groups - 1 + self.lines)

    def remote(self, src, dst, sems, index, device):
        return pltpu.make_async_remote_copy(
            src_ref=src, dst_ref=dst, send_sem=sems.at[(0, *index)], recv_sem=sems.at[(1, *index)],
            device_id=device, device_id_type=MESH_ID,
        )

    def here(self, shard, i):
        return self.rows.at[shard, :, pl.ds(i * self.cap, self.cap), :]

    def send_out(self):
        pltpu.make_async_copy(self.source.at[self.me], self.here(self.place, 0), self.dp_sems.at[0, 1, 0]).start()
        for i in range(1, self.groups):
            self.out_copy(i).start()

    def out_copy(self, i):
        to = self.group(i)
        return self.remote(self.source.at[to], self.here(self.place, i), self.dp_sems.at[0], (i,), {"dp": to})

    def line_copy(self, d, i):
        return self.remote(
            self.here(self.place, i), self.here(self.place, i), self.row_sems.at[0], (d, i),
            {"tensor": self.shard(d, self.core)},
        )

    def mate_copy(self, d, i):
        shard = self.shard(self.lines - d, self.core)
        return self.remote(
            self.here(shard, i), self.here(shard, i), self.row_sems.at[1], (d, i),
            {"tensor": self.shard(0, 1 - self.core)},
        )

    def landed(self, where, sems, index):
        self.remote(where, where, sems, index, {"tensor": self.shard(0, 1 - self.core)}).wait_recv()

    def places(self, k):
        return range(k * self.chunk, (k + 1) * self.chunk)

    def spread(self, k):
        for i in self.places(k):
            where = self.here(self.place, i)
            if i == 0:
                pltpu.make_async_copy(self.source.at[self.me], where, self.dp_sems.at[0, 1, 0]).wait()
            else:
                self.landed(where, self.dp_sems.at[0], (i,))
            for d in range(1, self.lines):
                self.line_copy(d, i).start()
            self.mate_copy(0, i).start()

    def relay(self, k):
        for i in self.places(k):
            for d in range(1, self.lines):
                shard = self.shard(self.lines - d, self.core)
                self.landed(self.here(shard, i), self.row_sems.at[0], (d, i))
                self.mate_copy(d, i).start()

    def collect(self, k):
        for i in self.places(k):
            for d in range(self.lines):
                shard = self.shard(self.lines - d, 1 - self.core)
                self.landed(self.here(shard, i), self.row_sems.at[1], (d, i))

    def span(self, k):
        return pl.ds(k * self.chunk * self.cap, self.chunk * self.cap)

    def pair_copy(self, d, k):
        shard = self.shard(d, 1 - self.core)
        return self.remote(
            self.part.at[shard, :, self.span(k), :], self.mate_in.at[d, :, self.span(k), :], self.sum_sems.at[0], (d, k),
            {"tensor": self.shard(0, 1 - self.core)},
        )

    def sum_copy(self, d, k):
        return self.remote(
            self.line_out.at[d, :, self.span(k), :], self.line_in.at[d, :, self.span(k), :], self.sum_sems.at[1], (d, k),
            {"tensor": self.shard(d, self.core)},
        )

    def back_copy(self, i):
        return self.remote(
            self.back_out.at[:, pl.ds(i * self.cap, self.cap), :], self.back.at[self.me], self.dp_sems.at[1], (i,),
            {"dp": self.group(self.groups - i)},
        )

    def pair(self, k):
        for d in range(self.lines):
            self.pair_copy(d, k).start()

    def pair_sum(self, d, k):
        shard = self.shard(d, self.core)
        return self.part[shard, :, self.span(k), :].astype(F32) + self.mate_in[d, :, self.span(k), :].astype(F32)

    def along(self, k):
        for d in range(self.lines):
            self.landed(self.mate_in.at[d, :, self.span(k), :], self.sum_sems.at[0], (d, k))
        for d in range(1, self.lines):
            self.line_out[d, :, self.span(k), :] = self.pair_sum(d, k).astype(BF16)
            self.sum_copy(d, k).start()

    def give(self, k):
        total = self.pair_sum(0, k)
        for d in range(1, self.lines):
            self.landed(self.line_in.at[d, :, self.span(k), :], self.sum_sems.at[1], (d, k))
            total = total + self.line_in[d, :, self.span(k), :].astype(F32)
        self.back_out[:, self.span(k), :] = total.astype(BF16)
        for i in self.places(k):
            if i == 0:
                self.own_back().start()
            else:
                self.back_copy(i).start()

    def own_back(self):
        return pltpu.make_async_copy(
            self.back_out.at[:, pl.ds(0, self.cap), :], self.back.at[self.me], self.dp_sems.at[1, 1, 0]
        )

    def run(self, compute):
        self.send_out()
        for step in range(self.steps + 4):
            for lag, work in enumerate((self.spread, self.relay, compute, self.along, self.give)):
                k = step - lag
                if 0 <= k < self.steps:
                    if lag == 2:
                        self.collect(k)
                    work(k)
                    if lag == 2:
                        self.pair(k)

    def finish(self):
        self.own_back().wait()
        for i in range(1, self.groups):
            where = self.back.at[self.group(i)]
            self.landed(where, self.dp_sems.at[1], (i,))
            self.out_copy(i).wait_send()
            self.back_copy(i).wait_send()
        for i in range(self.groups):
            for d in range(self.lines):
                if d:
                    self.line_copy(d, i).wait_send()
                self.mate_copy(d, i).wait_send()
        for k in range(self.steps):
            for d in range(self.lines):
                if d:
                    self.sum_copy(d, k).wait_send()
                self.pair_copy(d, k).wait_send()


def mover_scratch(groups, shards, local, cap, share, chunk):
    lines, slots, steps = shards // 2, groups * cap, groups // chunk
    return [
        pltpu.VMEM((lines, local, slots, share), BF16),
        pltpu.VMEM((lines, local, slots, share), BF16),
        pltpu.VMEM((lines, local, slots, share), BF16),
        pltpu.VMEM((local, slots, share), BF16),
        pltpu.SemaphoreType.DMA((2, 2, groups)),
        pltpu.SemaphoreType.DMA((2, 2, lines, groups)),
        pltpu.SemaphoreType.DMA((2, 2, lines, steps)),
    ]


ROOT = math.sqrt(2.0 / math.pi)


def gelu_parts(v):
    inner = jnp.tanh(ROOT * (v + 0.044715 * (v * v * v)))
    half = 0.5 * (1.0 + inner)
    slope = half + 0.5 * v * (1.0 - inner * inner) * (ROOT * (1.0 + 3.0 * 0.044715 * v * v))
    return v * half, slope


def expert_forward(
    groups, shards, local, cap, chunk,
    source, gate_up_hbm, down_hbm, count,
    back, rows_hbm, pre_hbm, hidden_hbm, total,
    rows, part, gate_up, down, pre, hidden, load_sems, save_sems, counts, count_sems, *scratch,
):
    mover = Mover(groups, shards, cap, chunk, source, rows, part, back, scratch)
    share = rows.shape[-1]
    loads = [pltpu.make_async_copy(gate_up_hbm, gate_up, load_sems.at[0]), pltpu.make_async_copy(down_hbm, down, load_sems.at[1])]
    for load in loads:
        load.start()

    def saves(k):
        span = mover.span(k)
        return [
            pltpu.make_async_copy(rows.at[:, :, span, :], rows_hbm.at[:, :, span, :], save_sems.at[0, k]),
            pltpu.make_async_copy(pre.at[:, :, span, :], pre_hbm.at[:, :, span, :], save_sems.at[1, k]),
            pltpu.make_async_copy(hidden.at[:, span, :], hidden_hbm.at[:, span, :], save_sems.at[2, k]),
        ]

    def compute(k):
        span = mover.span(k)
        if k == 0:
            for load in loads:
                load.wait()
        for e in range(local):
            lhs = jnp.concatenate([rows[s, e, span, :] for s in range(shards)], axis=1)
            gate = dot(lhs, gate_up[e, 0], ((1,), (1,)))
            up = dot(lhs, gate_up[e, 1], ((1,), (1,)))
            pre[0, e, span, :] = gate
            pre[1, e, span, :] = up
            low = (gelu_parts(gate)[0] * up).astype(BF16)
            hidden[e, span, :] = low
            result = dot(low, down[e]).astype(BF16)
            for s in range(shards):
                part[s, e, span, :] = result[:, s * share : (s + 1) * share]
        for save in saves(k):
            save.start()

    def count_copy(i):
        return mover.remote(count, counts.at[i], count_sems, (i,), {"dp": mover.group(i)})

    mover.greet()
    for i in range(1, groups):
        count_copy(i).start()
    mover.run(compute)
    tally = count[...]
    for i in range(1, groups):
        count_copy(i).wait()
        tally = tally + counts[i]
    total[...] = tally
    mover.finish()
    for k in range(mover.steps):
        for save in saves(k):
            save.wait()


def expert_backward(
    groups, shards, local, cap, chunk,
    source, gate_up_hbm, down_hbm, pre_hbm,
    back, rows_hbm, side_hbm,
    rows, part, gate_up, down, pre, side, load_sems, save_sems, *scratch,
):
    mover = Mover(groups, shards, cap, chunk, source, rows, part, back, scratch)
    share = rows.shape[-1]
    loads = [
        pltpu.make_async_copy(gate_up_hbm, gate_up, load_sems.at[0]),
        pltpu.make_async_copy(down_hbm, down, load_sems.at[1]),
        pltpu.make_async_copy(pre_hbm, pre, load_sems.at[2]),
    ]
    for load in loads:
        load.start()

    def saves(k):
        span = mover.span(k)
        return [
            pltpu.make_async_copy(rows.at[:, :, span, :], rows_hbm.at[:, :, span, :], save_sems.at[0, k]),
            pltpu.make_async_copy(side.at[:, :, span, :], side_hbm.at[:, :, span, :], save_sems.at[1, k]),
        ]

    def compute(k):
        span = mover.span(k)
        if k == 0:
            for load in loads:
                load.wait()
        for e in range(local):
            lhs = jnp.concatenate([rows[s, e, span, :] for s in range(shards)], axis=1)
            hidden_grad = dot(lhs, down[e], ((1,), (1,)))
            activated, slope = gelu_parts(pre[0, e, span, :])
            gate_side = (hidden_grad * pre[1, e, span, :] * slope).astype(BF16)
            up_side = (hidden_grad * activated).astype(BF16)
            side[0, e, span, :] = gate_side
            side[1, e, span, :] = up_side
            result = dot(gate_side, gate_up[e, 0]) + dot(up_side, gate_up[e, 1])
            result = result.astype(BF16)
            for s in range(shards):
                part[s, e, span, :] = result[:, s * share : (s + 1) * share]
        for save in saves(k):
            save.start()

    mover.greet()
    mover.run(compute)
    mover.finish()
    for k in range(mover.steps):
        for save in saves(k):
            save.wait()


def weight_grads(shards, rows, grads, side, hidden, gate_up_out, down_out):
    step = pl.program_id(1)
    share = rows.shape[-1]

    @pl.when(step < 2)
    def _():
        for s in range(shards):
            gate_up_out[:, s * share : (s + 1) * share] = dot(side[...], rows[s], ((0,), (0,)))

    @pl.when(step == 2)
    def _():
        for s in range(shards):
            down_out[:, s * share : (s + 1) * share] = dot(hidden[...], grads[s], ((0,), (0,)))


def to_row(column):
    rows = column.shape[0]
    return jnp.transpose(jnp.broadcast_to(column, (rows, 128)))[:8]


def to_column(row):
    return jnp.transpose(jnp.broadcast_to(row[:1], (128, row.shape[1])))[:, :1]


def gate_columns(logits, first, second):
    lanes = lax.broadcasted_iota(jnp.int32, logits.shape, 1)
    exponent = jnp.exp(logits - jnp.max(logits, axis=1, keepdims=True))
    expert_probs = exponent / jnp.sum(exponent, axis=1, keepdims=True)
    chosen = [jnp.sum(jnp.where(lanes == pick, expert_probs, 0.0), axis=1, keepdims=True) for pick in (first, second)]
    total = chosen[0] + chosen[1]
    return expert_probs, chosen[0] / total, chosen[1] / total


def dense_forward(
    groups, shards, heads, width, experts,
    len_ref, bias_ref, ids_ref, gains, router_ref,
    inputs_hbm, w_qkv_hbm, w_out_hbm,
    normed_out, proj_out, probs_out, attended_out, after_out, normed_two_out, columns_out,
    inputs, w_qkv, load_sems, w_out, w_sems, attended, attended_sems, skew, normed, proj, probs, after, normed_two, save_sems,
):
    tokens, model = inputs.shape
    here = heads * width
    share = model // shards
    lines = shards // 2
    blocks = tokens // TILE
    place = lax.axis_index("tensor")
    line, core = lax.div(place, 2), lax.rem(place, 2)
    mate = {"tensor": line * 2 + 1 - core}

    def shard(d, c):
        return lax.rem(line + d, lines) * 2 + c

    def remote(src, dst, sems, index, device):
        return pltpu.make_async_remote_copy(
            src_ref=src, dst_ref=dst, send_sem=sems.at[(0, *index)], recv_sem=sems.at[(1, *index)],
            device_id=device, device_id_type=MESH_ID,
        )

    def landed(where, sems, index):
        remote(where, where, sems, index, mate).wait_recv()

    loads = [
        pltpu.make_async_copy(inputs_hbm, inputs, load_sems.at[0]),
        pltpu.make_async_copy(w_qkv_hbm, w_qkv, load_sems.at[1]),
        pltpu.make_async_copy(w_out_hbm, w_out.at[place], load_sems.at[2]),
    ]
    for load in loads:
        load.start()
    barrier = pltpu.get_barrier_semaphore()
    for d in range(1, lines):
        pl.semaphore_signal(barrier, inc=1, device_id={"tensor": shard(d, core)}, device_id_type=MESH_ID)
    pl.semaphore_signal(barrier, inc=1, device_id=mate, device_id_type=MESH_ID)
    pl.semaphore_wait(barrier, lines)

    def w_line(d):
        return remote(w_out.at[place], w_out.at[place], w_sems.at[0], (d,), {"tensor": shard(d, core)})

    def w_mate(d):
        where = w_out.at[shard(lines - d, core)]
        return remote(where, where, w_sems.at[1], (d,), mate)

    def row_block(j):
        return pl.ds(j * TILE, TILE)

    def rows_line(d, j):
        where = attended.at[place, row_block(j), :]
        return remote(where, where, attended_sems.at[0], (d, j), {"tensor": shard(d, core)})

    def rows_mate(d, j):
        where = attended.at[shard(lines - d, core), row_block(j), :]
        return remote(where, where, attended_sems.at[1], (d, j), mate)

    loads[2].wait()
    for d in range(1, lines):
        w_line(d).start()
    w_mate(0).start()

    loads[0].wait()
    for j in range(blocks):
        rows = slice(j * TILE, (j + 1) * TILE)
        values = inputs[rows, :].astype(F32)
        scale = lax.rsqrt(jnp.mean(values * values, axis=1, keepdims=True) + EPSILON)
        columns_out[rows, 0:1] = scale
        normed[rows, :] = (values * scale * gains[0:1, :]).astype(BF16)
    loads[1].wait()
    for n in range(3):
        proj[n] = dot(normed[...], w_qkv[n]).astype(BF16)
    saves = [
        pltpu.make_async_copy(normed, normed_out, save_sems.at[0]),
        pltpu.make_async_copy(proj, proj_out, save_sems.at[1]),
    ]
    for h in range(heads):
        skew[h] = pltpu.roll(
            jnp.broadcast_to(bias_ref[h : h + 1, :], (TILE, SPAN)), 0, 1, stride=1, stride_axis=0
        )
    for item in saves:
        item.start()

    alive = lax.broadcasted_iota(jnp.int32, (TILE, SEQ_LEN), 1) < len_ref[0]
    for j in range(blocks):
        rows = slice(j * TILE, (j + 1) * TILE)
        start = SEQ_LEN - j * TILE
        for h in range(heads):
            cols = slice(h * width, (h + 1) * width)
            scores = dot(proj[0, rows, cols], proj[1, :, cols], ((1,), (1,)))
            scores = jnp.where(alive, scores + skew[h, :, start : start + SEQ_LEN], MASKED)
            exponent = jnp.exp(scores - jnp.max(scores, axis=1, keepdims=True))
            weights = exponent * (1.0 / jnp.sum(exponent, axis=1, keepdims=True))
            probs[h, rows, :] = weights
            attended[place, rows, cols] = dot(weights.astype(BF16), proj[2, :, cols]).astype(BF16)
        for d in range(1, lines):
            rows_line(d, j).start()
        rows_mate(0, j).start()
        if j == blocks - 2:
            for d in range(1, lines):
                landed(w_out.at[shard(lines - d, core)], w_sems.at[0], (d,))
                w_mate(d).start()
    saves += [
        pltpu.make_async_copy(probs, probs_out, save_sems.at[2]),
        pltpu.make_async_copy(attended.at[place], attended_out, save_sems.at[3]),
    ]
    for item in saves[2:]:
        item.start()

    ids = ids_ref[...].astype(F32)
    picks = [to_column(ids[n : n + 1]).astype(jnp.int32) for n in range(2)]

    def relay(j):
        for d in range(1, lines):
            landed(attended.at[shard(lines - d, core), row_block(j), :], attended_sems.at[0], (d, j))
            rows_mate(d, j).start()

    relay(0)
    for d in range(lines):
        landed(w_out.at[shard(lines - d, 1 - core)], w_sems.at[1], (d,))
    for j in range(blocks):
        rows = slice(j * TILE, (j + 1) * TILE)
        if j + 1 < blocks:
            relay(j + 1)
        for d in range(lines):
            landed(attended.at[shard(lines - d, 1 - core), row_block(j), :], attended_sems.at[1], (d, j))
        total = inputs[rows, :].astype(F32)
        for s in range(shards):
            total = total + dot(attended[s, rows, :], w_out[s])
        scale = lax.rsqrt(jnp.mean(total * total, axis=1, keepdims=True) + EPSILON)
        low = (total * scale * gains[1:2, :]).astype(BF16)
        after[...] = total
        normed_two[...] = low
        mine = pl.ds(pl.multiple_of(place * share, 128), share)
        after_out[rows, :] = after[:, mine]
        normed_two_out[rows, :] = normed_two[:, mine]
        expert_probs, first, second = gate_columns(
            dot(low, router_ref[...], ((1,), (1,))), picks[0][rows], picks[1][rows]
        )
        columns_out[rows, 1:2] = scale
        columns_out[rows, 2:3] = first
        columns_out[rows, 3:4] = second
        columns_out[rows, 16 : 16 + experts] = expert_probs
    for d in range(lines):
        if d:
            w_line(d).wait_send()
        w_mate(d).wait_send()
        for j in range(blocks):
            if d:
                rows_line(d, j).wait_send()
            rows_mate(d, j).wait_send()
    for item in saves:
        item.wait()


def dense_backward(
    groups, shards, heads, width, experts,
    norm_grad, after, out_grad, residual, scales, gains, extras_in, onehot,
    attended_hbm, w_out_hbm, proj_hbm, probs_hbm, normed_hbm, w_qkv_hbm,
    dense_out, input_grad, extras_out,
    attended, w_out, proj, probs, normed, w_qkv, load_sems,
    dots, dot_sems, branch, branch_sems, grad_here, diag, key_acc, value_acc, proj_grad,
    part, mate_in, line_out, line_in, part_sems,
    dense, result, y_in, y_sum, z_in, dense_sems, z_sems, save_sems,
    extras, extras_in_dp, extras_sems, extras_ring_sems,
):
    model = normed.shape[1]
    share = branch.shape[-1]
    tokens = branch.shape[1]
    here = heads * width
    lines = shards // 2
    y_size = 1 << ((groups.bit_length() - 1) // 2)
    z_size = groups // y_size
    pieces = dense.shape[0]
    me, place = lax.axis_index("dp"), lax.axis_index("tensor")
    line, core = lax.div(place, 2), lax.rem(place, 2)
    z, y = lax.div(me, y_size), lax.rem(me, y_size)
    mate = {"tensor": line * 2 + 1 - core}
    inverse = 1.0 / model

    def group(i):
        return lax.rem(me + i, groups)

    def shard(d, c):
        return lax.rem(line + d, lines) * 2 + c

    def near(i):
        return lax.rem(place + i, shards)

    def remote(src, dst, sems, index, device):
        return pltpu.make_async_remote_copy(
            src_ref=src, dst_ref=dst, send_sem=sems.at[(0, *index)], recv_sem=sems.at[(1, *index)],
            device_id=device, device_id_type=MESH_ID,
        )

    def landed(where, sems, index):
        remote(where, where, sems, index, mate).wait_recv()

    loads = [
        pltpu.make_async_copy(src, dst, load_sems.at[n])
        for n, (src, dst) in enumerate(
            (
                (w_out_hbm, w_out), (attended_hbm, attended), (proj_hbm, proj), (probs_hbm, probs),
                (w_qkv_hbm, w_qkv), (normed_hbm, normed),
            )
        )
    ]
    for load in loads:
        load.start()

    barrier = pltpu.get_barrier_semaphore()
    for i in range(1, groups):
        pl.semaphore_signal(barrier, inc=1, device_id={"dp": group(i)}, device_id_type=MESH_ID)
    for i in range(1, shards):
        pl.semaphore_signal(barrier, inc=1, device_id={"tensor": near(i)}, device_id_type=MESH_ID)
    pl.semaphore_wait(barrier, groups + shards - 2)

    def dot_copy(n, i):
        return remote(dots.at[n, 0], dots.at[n, i], dot_sems, (n, i), {"tensor": near(i)})

    def dot_send(n, column):
        dots[n, 0] = to_row(column)
        for i in range(1, shards):
            dot_copy(n, i).start()

    def dot_sum(n):
        total = dots[n, 0]
        for i in range(1, shards):
            dot_copy(n, i).wait()
            total = total + dots[n, i]
        return to_column(total)

    scale_two = scales[:, 1:2]
    weighted = norm_grad[...] * gains[1:2, :]
    dot_send(0, jnp.sum(weighted * after[...], axis=1, keepdims=True))
    extras[0] = extras_in[...]
    extras[0, experts + 1 : experts + 2, :] = jnp.sum(norm_grad[...] * after[...] * scale_two, axis=0, keepdims=True)
    along = dot_sum(0)
    after_grad = out_grad[...] + scale_two * (weighted - after[...] * (scale_two * scale_two * along * inverse))
    grad_here[...] = after_grad
    branch[place] = after_grad.astype(BF16)

    blocks = tokens // TILE

    def row_block(j):
        return pl.ds(j * TILE, TILE)

    def branch_line(d, j):
        where = branch.at[place, row_block(j), :]
        return remote(where, where, branch_sems.at[0], (d, j), {"tensor": shard(d, core)})

    def branch_mate(d, j):
        where = branch.at[shard(lines - d, core), row_block(j), :]
        return remote(where, where, branch_sems.at[1], (d, j), mate)

    for j in range(blocks):
        for d in range(1, lines):
            branch_line(d, j).start()
        branch_mate(0, j).start()
    for j in range(blocks):
        for d in range(1, lines):
            landed(branch.at[shard(lines - d, core), row_block(j), :], branch_sems.at[0], (d, j))
            branch_mate(d, j).start()
    for j in range(blocks):
        for d in range(lines):
            landed(branch.at[shard(lines - d, 1 - core), row_block(j), :], branch_sems.at[1], (d, j))
    loads[0].wait()
    loads[1].wait()

    y_rows, z_rows = model // y_size, model // groups

    def y_copy(p, a):
        to = lax.rem(y + a, y_size)
        return remote(
            dense.at[p, pl.ds(to * y_rows, y_rows), :], y_in.at[p, a], dense_sems.at[0], (p, a), {"dp": z * y_size + to}
        )

    def z_copy(p, b):
        to = lax.rem(z + b, z_size)
        return remote(
            y_sum.at[p, pl.ds(to * z_rows, z_rows), :], z_in.at[p, b], z_sems.at[0], (p, b), {"dp": to * y_size + y}
        )

    def z_spread(p, b):
        to = lax.rem(z + b, z_size)
        where = result.at[p, pl.ds(y * y_rows + z * z_rows, z_rows), :]
        return remote(where, where, z_sems.at[1], (p, b), {"dp": to * y_size + y})

    def y_spread(p, a):
        to = lax.rem(y + a, y_size)
        where = result.at[p, pl.ds(y * y_rows, y_rows), :]
        return remote(where, where, dense_sems.at[1], (p, a), {"dp": z * y_size + to})

    def reduce_start(p):
        for a in range(1, y_size):
            y_copy(p, a).start()

    def reduce_y(p):
        total = dense[p, pl.ds(y * y_rows, y_rows), :].astype(F32)
        for a in range(1, y_size):
            landed(y_in.at[p, a], dense_sems.at[0], (p, a))
            total = total + y_in[p, a].astype(F32)
        y_sum[p] = total.astype(BF16)
        for b in range(1, z_size):
            z_copy(p, b).start()

    def reduce_z(p):
        total = y_sum[p, pl.ds(z * z_rows, z_rows), :].astype(F32)
        for a in range(1, y_size):
            y_copy(p, a).wait_send()
        for b in range(1, z_size):
            landed(z_in.at[p, b], z_sems.at[0], (p, b))
            total = total + z_in[p, b].astype(F32)
        result[p, pl.ds(y * y_rows + z * z_rows, z_rows), :] = total.astype(BF16)
        for b in range(1, z_size):
            z_spread(p, b).start()

    def spread_z(p):
        for b in range(1, z_size):
            origin = lax.rem(z + z_size - b, z_size)
            landed(result.at[p, pl.ds(y * y_rows + origin * z_rows, z_rows), :], z_sems.at[1], (p, b))
        for a in range(1, y_size):
            y_spread(p, a).start()

    def save(p):
        return pltpu.make_async_copy(result.at[p], dense_out.at[p], save_sems.at[p])

    def spread_y(p):
        for a in range(1, y_size):
            origin = lax.rem(y + y_size - a, y_size)
            landed(result.at[p, pl.ds(origin * y_rows, y_rows), :], dense_sems.at[1], (p, a))
        save(p).start()

    for s in range(shards):
        dense[0, s * here : (s + 1) * here, :] = dot(
            attended[...], branch[s], ((0,), (0,))
        ).astype(BF16)
    reduce_start(0)

    loads[2].wait()
    loads[3].wait()
    diag[...] = jnp.zeros_like(diag)
    for j in range(blocks):
        rows = slice(j * TILE, (j + 1) * TILE)
        start = SEQ_LEN - j * TILE
        wide = jnp.concatenate([branch[s, rows, :] for s in range(shards)], axis=1)
        grads = dot(wide, w_out[...], ((1,), (1,))).astype(BF16)
        for h in range(heads):
            cols = slice(h * width, (h + 1) * width)
            p = probs[h, rows, :]
            grad = grads[:, cols]
            prob_grad = dot(grad, proj[2, :, cols], ((1,), (1,)))
            score_grad = p * (prob_grad - jnp.sum(p * prob_grad, axis=1, keepdims=True))
            diag[h, :, start : start + SEQ_LEN] += score_grad
            low = score_grad.astype(BF16)
            proj_grad[0, rows, cols] = dot(low, proj[1, :, cols]).astype(BF16)
            key_part = dot(low, proj[0, rows, cols], ((0,), (0,)))
            value_part = dot(p.astype(BF16), grad, ((0,), (0,)))
            if j == 0:
                key_acc[:, cols] = key_part
                value_acc[:, cols] = value_part
            else:
                key_acc[:, cols] += key_part
                value_acc[:, cols] += value_part
        if j == 1:
            reduce_y(0)
    proj_grad[1] = key_acc[...].astype(BF16)
    proj_grad[2] = value_acc[...].astype(BF16)
    reduce_z(0)

    loads[4].wait()
    loads[5].wait()
    for p in range(1, pieces):
        dense[p] = dot(normed[...], proj_grad[p - 1], ((0,), (0,))).astype(BF16)
        reduce_start(p)
    half = tokens // 2

    def part_rows(k):
        return pl.ds(k * half, half)

    def pair_copy(d, k):
        return remote(
            part.at[shard(d, 1 - core), part_rows(k), :], mate_in.at[d, part_rows(k), :], part_sems.at[0], (d, k), mate
        )

    def line_copy(d, k):
        return remote(
            line_out.at[d, part_rows(k), :], line_in.at[d, part_rows(k), :], part_sems.at[1], (d, k),
            {"tensor": shard(d, core)},
        )

    for k in range(2):
        rows = slice(k * half, (k + 1) * half)
        total = dot(proj_grad[0, rows, :], w_qkv[0], ((1,), (1,)))
        for n in range(1, 3):
            total = total + dot(proj_grad[n, rows, :], w_qkv[n], ((1,), (1,)))
        low = total.astype(BF16)
        for s in range(shards):
            part[s, rows, :] = low[:, s * share : (s + 1) * share]
        for d in range(lines):
            pair_copy(d, k).start()
    spread_z(0)

    def pair_sum(d, rows):
        return part[shard(d, core), rows, :].astype(F32) + mate_in[d, rows, :].astype(F32)

    for k in range(2):
        rows = part_rows(k)
        for d in range(lines):
            landed(mate_in.at[d, rows, :], part_sems.at[0], (d, k))
        for d in range(1, lines):
            line_out[d, rows, :] = pair_sum(d, rows).astype(BF16)
            line_copy(d, k).start()
    for h in range(heads):
        total = diag[h]
        size = TILE // 2
        while size >= 1:
            total = total[:size] + pltpu.roll(total[size : 2 * size], SPAN - size, 1)
            size //= 2
        row = jnp.broadcast_to(total, (8, SPAN))
        high = row.astype(BF16)
        middle = (row - high.astype(F32)).astype(BF16)
        low = (row - high.astype(F32) - middle.astype(F32)).astype(BF16)
        table = dot(high, onehot[...]) + dot(middle, onehot[...]) + dot(low, onehot[...])
        extras[0, experts + 4 + h : experts + 5 + h, : onehot.shape[1]] = table[:1]
    for p in range(1, pieces):
        reduce_y(p)

    total = pair_sum(0, pl.ds(0, tokens))
    for k in range(2):
        for d in range(1, lines):
            landed(line_in.at[d, part_rows(k), :], part_sems.at[1], (d, k))
    for d in range(1, lines):
        total = total + line_in[d].astype(F32)
    scale_one = scales[:, 0:1]
    values = residual[...].astype(F32)
    weighted = total * gains[0:1, :]
    dot_send(1, jnp.sum(weighted * values, axis=1, keepdims=True))
    extras[0, experts : experts + 1, :] = jnp.sum(total * values * scale_one, axis=0, keepdims=True)

    def extras_copy(i):
        return remote(extras.at[0], extras_in_dp.at[i], extras_sems, (i,), {"dp": group(i)})

    for i in range(1, groups):
        extras_copy(i).start()
    for p in range(1, pieces):
        reduce_z(p)
    along = dot_sum(1)
    input_grad[...] = grad_here[...] + scale_one * (weighted - values * (scale_one * scale_one * along * inverse))

    summed = extras[0]
    for i in range(1, groups):
        extras_copy(i).wait()
        summed = summed + extras_in_dp[i]
    extras_out[place] = summed

    def ring_copy(i):
        return remote(extras_out.at[place], extras_out.at[place], extras_ring_sems, (i,), {"tensor": near(i)})

    for i in range(1, shards):
        ring_copy(i).start()
    for p in range(1, pieces):
        spread_z(p)
    for p in range(pieces):
        spread_y(p)
    for i in range(1, shards):
        landed(extras_out.at[near(shards - i)], extras_ring_sems, (i,))
        ring_copy(i).wait_send()
    for j in range(blocks):
        for d in range(lines):
            if d:
                branch_line(d, j).wait_send()
            branch_mate(d, j).wait_send()
    for k in range(2):
        for d in range(lines):
            if d:
                line_copy(d, k).wait_send()
            pair_copy(d, k).wait_send()
    for p in range(pieces):
        for b in range(1, z_size):
            z_copy(p, b).wait_send()
            z_spread(p, b).wait_send()
        for a in range(1, y_size):
            y_spread(p, a).wait_send()
        save(p).wait()


def body(
    inputs,
    teacher,
    lengths,
    expert_ids,
    route_slots,
    gain_attn,
    w_qkv,
    w_out,
    rel_table,
    gain_moe,
    w_router,
    w_gate_up,
    w_down,
):
    highest = lax.Precision.HIGHEST
    tok_rows, model_width = inputs.shape
    groups = lax.axis_size("dp")
    shards = lax.axis_size("tensor")
    experts = w_router.shape[1]
    local_experts = w_gate_up.shape[0]
    capacity = 10 * tok_rows // (4 * experts)
    padded_cap = (capacity + 15) // 16 * 16
    slot_count = experts * padded_cap
    heads_here = rel_table.shape[1]
    width_here = w_qkv.shape[2]
    head_width = width_here // heads_here
    share = model_width // shards
    column_start = lax.axis_index("tensor") * share

    def mine(values):
        return lax.dynamic_slice_in_dim(values, column_start, share, values.ndim - 1)

    offsets = jnp.arange(SPAN, dtype=jnp.int32) - SEQ_LEN
    onehot_offsets = bucket_onehot(offsets)
    offset_bias = jnp.dot(onehot_offsets, rel_table, precision=highest).T
    lines = shards // 2
    blocks = tok_rows // TILE
    ids = expert_ids.T
    normed_low, projected, probs, attended, after_mine, normed_mine, columns = pl.pallas_call(
        functools.partial(dense_forward, groups, shards, heads_here, head_width, experts),
        out_shape=(
            jax.ShapeDtypeStruct((tok_rows, model_width), BF16),
            jax.ShapeDtypeStruct((3, tok_rows, width_here), BF16),
            jax.ShapeDtypeStruct((heads_here, SEQ_LEN, SEQ_LEN), F32),
            jax.ShapeDtypeStruct((tok_rows, width_here), BF16),
            jax.ShapeDtypeStruct((tok_rows, share), F32),
            jax.ShapeDtypeStruct((tok_rows, share), BF16),
            jax.ShapeDtypeStruct((tok_rows, 128), F32),
        ),
        in_specs=[SMEM] + [VMEM] * 4 + [ANY] * 3,
        out_specs=(ANY,) * 4 + (VMEM,) * 3,
        scratch_shapes=[
            pltpu.VMEM((tok_rows, model_width), BF16),
            pltpu.VMEM(w_qkv.shape, BF16),
            pltpu.SemaphoreType.DMA((3,)),
            pltpu.VMEM((shards, width_here, model_width), BF16),
            pltpu.SemaphoreType.DMA((2, 2, lines)),
            pltpu.VMEM((shards, tok_rows, width_here), BF16),
            pltpu.SemaphoreType.DMA((2, 2, lines, blocks)),
            pltpu.VMEM((heads_here, TILE, SPAN), F32),
            pltpu.VMEM((tok_rows, model_width), BF16),
            pltpu.VMEM((3, tok_rows, width_here), BF16),
            pltpu.VMEM((heads_here, SEQ_LEN, SEQ_LEN), F32),
            pltpu.VMEM((TILE, model_width), F32),
            pltpu.VMEM((TILE, model_width), BF16),
            pltpu.SemaphoreType.DMA((4,)),
        ],
        compiler_params=pltpu.CompilerParams(
            vmem_limit_bytes=40 * 1024 * 1024, collective_id=4, has_side_effects=True
        ),
        name="dense_forward",
    )(lengths, offset_bias, ids, jnp.stack([gain_attn, gain_moe]), w_router.T, inputs, w_qkv, w_out)
    scale_one, scale_two = columns[:, 0:1], columns[:, 1:2]
    gates = columns[:, 2:4]
    expert_probs = columns[:, 16 : 16 + experts]
    expert_range = jnp.arange(experts, dtype=jnp.int32)
    picks = (expert_ids[:, :, None] == expert_range[None, None, :]).astype(F32)

    def gate_pull(grad):
        chosen_total = jnp.sum(expert_probs[:, None, :] * picks, axis=(1, 2))[:, None]
        chosen_grad = (grad - jnp.sum(grad * gates, axis=1, keepdims=True)) / chosen_total
        probs_grad = jnp.sum(chosen_grad[:, :, None] * picks, axis=1)
        return expert_probs * (probs_grad - jnp.sum(probs_grad * expert_probs, axis=1, keepdims=True))

    kept_route = route_slots < capacity
    target = jnp.where(kept_route, expert_ids * padded_cap + route_slots, -1)
    slot_range = jnp.arange(slot_count, dtype=jnp.int32)
    route_of = (target[:, :, None] == slot_range[None, None, :]).astype(BF16)
    first_route, second_route = route_of[:, 0], route_of[:, 1]
    any_route = first_route + second_route

    teacher_mine = mine(teacher).astype(F32)
    dispatched = dot(any_route, normed_mine, ((0,), (0,))).astype(BF16)
    gate_up_t = jnp.swapaxes(w_gate_up, 2, 3)
    chunk = max(groups // 4, 1)
    slots = groups * padded_cap
    block_shape = (groups, local_experts, padded_cap, share)
    rows_type = jax.ShapeDtypeStruct((shards, local_experts, slots, share), BF16)
    back_type = jax.ShapeDtypeStruct(block_shape, BF16)
    ff_here = w_down.shape[1]
    sizes = (groups, shards, local_experts, padded_cap)
    rows_scratch = [
        pltpu.VMEM((shards, local_experts, slots, share), BF16),
        pltpu.VMEM((shards, local_experts, slots, share), BF16),
        pltpu.VMEM(gate_up_t.shape, BF16),
        pltpu.VMEM(w_down.shape, BF16),
        pltpu.VMEM((2, local_experts, slots, ff_here), F32),
    ]
    returned, expert_rows, pre_acts, hidden_low, count_total = pl.pallas_call(
        functools.partial(expert_forward, *sizes, chunk),
        out_shape=(
            back_type,
            rows_type,
            jax.ShapeDtypeStruct((2, local_experts, slots, ff_here), F32),
            jax.ShapeDtypeStruct((local_experts, slots, ff_here), BF16),
            jax.ShapeDtypeStruct((8, 128), jnp.int32),
        ),
        in_specs=[ANY] * 3 + [VMEM],
        out_specs=(ANY,) * 4 + (VMEM,),
        scratch_shapes=rows_scratch
        + [
            pltpu.VMEM((local_experts, slots, ff_here), BF16),
            pltpu.SemaphoreType.DMA((2,)),
            pltpu.SemaphoreType.DMA((3, groups // chunk)),
            pltpu.VMEM((groups, 8, 128), jnp.int32),
            pltpu.SemaphoreType.DMA((2, groups)),
        ]
        + mover_scratch(*sizes, share, chunk),
        compiler_params=pltpu.CompilerParams(
            vmem_limit_bytes=50 * 1024 * 1024, collective_id=1, has_side_effects=True
        ),
        name="expert_forward",
    )(dispatched.reshape(block_shape), gate_up_t, w_down, jnp.broadcast_to(lengths, (8, 128)))
    returned = returned.reshape(slot_count, share)
    routed_first = dot(first_route, returned)
    routed_second = dot(second_route, returned)

    row_alive = (jnp.arange(tok_rows, dtype=jnp.int32) < lengths[0]).astype(F32)[:, None]
    valid_total = count_total[0, 0].astype(F32)
    scale = groups * tok_rows / valid_total
    block_out = after_mine + gates[:, 0, None] * routed_first + gates[:, 1, None] * routed_second
    deviation = (block_out - teacher_mine) * row_alive
    out_grad = deviation * scale
    slot_grad = (
        dot(first_route, (gates[:, 0, None] * out_grad).astype(BF16), ((0,), (0,)))
        + dot(second_route, (gates[:, 1, None] * out_grad).astype(BF16), ((0,), (0,)))
    ).astype(BF16)
    gate_grad_part = jnp.stack(
        [jnp.sum(routed_first * out_grad, axis=-1), jnp.sum(routed_second * out_grad, axis=-1)],
        axis=1,
    )
    gate_grad = lax.psum(gate_grad_part, "tensor")
    back_grad, expert_grad, pre_grads = pl.pallas_call(
        functools.partial(expert_backward, *sizes, chunk),
        out_shape=(
            back_type,
            rows_type,
            jax.ShapeDtypeStruct((2, local_experts, slots, ff_here), BF16),
        ),
        in_specs=[ANY] * 4,
        out_specs=(ANY,) * 3,
        scratch_shapes=rows_scratch
        + [
            pltpu.VMEM((2, local_experts, slots, ff_here), BF16),
            pltpu.SemaphoreType.DMA((3,)),
            pltpu.SemaphoreType.DMA((2, groups // chunk)),
        ]
        + mover_scratch(*sizes, share, chunk),
        compiler_params=pltpu.CompilerParams(
            vmem_limit_bytes=50 * 1024 * 1024, collective_id=2, has_side_effects=True
        ),
        name="expert_backward",
    )(slot_grad.reshape(block_shape), gate_up_t, w_down, pre_acts)
    back_grad = back_grad.reshape(slot_count, share)
    gate_up_grad, down_grad = pl.pallas_call(
        functools.partial(weight_grads, shards),
        grid=(local_experts, 3),
        out_shape=(
            jax.ShapeDtypeStruct(gate_up_t.shape, F32),
            jax.ShapeDtypeStruct(w_down.shape, F32),
        ),
        in_specs=[
            pl.BlockSpec((shards, None, slots, share), lambda e, j: (0, e, 0, 0)),
            pl.BlockSpec((shards, None, slots, share), lambda e, j: (0, e, 0, 0)),
            pl.BlockSpec((None, None, slots, ff_here), lambda e, j: (jnp.minimum(j, 1), e, 0, 0)),
            pl.BlockSpec((None, slots, ff_here), lambda e, j: (e, 0, 0)),
        ],
        out_specs=(
            pl.BlockSpec((None, None, ff_here, model_width), lambda e, j: (e, jnp.minimum(j, 1), 0, 0)),
            pl.BlockSpec((None, ff_here, model_width), lambda e, j: (e, 0, 0)),
        ),
        compiler_params=pltpu.CompilerParams(vmem_limit_bytes=48 * 1024 * 1024),
        name="weight_grads",
    )(expert_rows, expert_grad, pre_grads, hidden_low)
    gate_up_grad = jnp.swapaxes(gate_up_grad, 2, 3)

    logit_grad = gate_pull(gate_grad).astype(BF16)
    router_mine = dot(logit_grad, normed_mine, ((0,), (0,)))
    normed_two_grad = dot(any_route, back_grad) + mine(dot(logit_grad, w_router, ((1,), (1,))))
    squared = jnp.sum(deviation * deviation)
    extra_rows = experts + 8
    extras = jnp.concatenate(
        [router_mine, jnp.zeros((2, share), F32), jnp.broadcast_to(squared, (1, share)), jnp.zeros((5, share), F32)]
    )
    y_size = 1 << ((groups.bit_length() - 1) // 2)
    z_size = groups // y_size
    pieces = 1 + 3
    dense, input_grad, extras = pl.pallas_call(
        functools.partial(dense_backward, groups, shards, heads_here, head_width, experts),
        out_shape=(
            jax.ShapeDtypeStruct((pieces, model_width, width_here), BF16),
            jax.ShapeDtypeStruct((tok_rows, share), F32),
            jax.ShapeDtypeStruct((shards, extra_rows, share), F32),
        ),
        in_specs=[VMEM] * 8 + [ANY] * 6,
        out_specs=(ANY, VMEM, VMEM),
        scratch_shapes=[
            pltpu.VMEM(attended.shape, BF16),
            pltpu.VMEM(w_out.shape, BF16),
            pltpu.VMEM(projected.shape, BF16),
            pltpu.VMEM(probs.shape, F32),
            pltpu.VMEM(normed_low.shape, BF16),
            pltpu.VMEM(w_qkv.shape, BF16),
            pltpu.SemaphoreType.DMA((6,)),
            pltpu.VMEM((2, shards, 8, tok_rows), F32),
            pltpu.SemaphoreType.DMA((2, 2, shards)),
            pltpu.VMEM((shards, tok_rows, share), BF16),
            pltpu.SemaphoreType.DMA((2, 2, lines, blocks)),
            pltpu.VMEM((tok_rows, share), F32),
            pltpu.VMEM((heads_here, TILE, SPAN), F32),
            pltpu.VMEM((SEQ_LEN, width_here), F32),
            pltpu.VMEM((SEQ_LEN, width_here), F32),
            pltpu.VMEM((3, tok_rows, width_here), BF16),
            pltpu.VMEM((shards, tok_rows, share), BF16),
            pltpu.VMEM((lines, tok_rows, share), BF16),
            pltpu.VMEM((lines, tok_rows, share), BF16),
            pltpu.VMEM((lines, tok_rows, share), BF16),
            pltpu.SemaphoreType.DMA((2, 2, lines, 2)),
            pltpu.VMEM((pieces, model_width, width_here), BF16),
            pltpu.VMEM((pieces, model_width, width_here), BF16),
            pltpu.VMEM((pieces, y_size, model_width // y_size, width_here), BF16),
            pltpu.VMEM((pieces, model_width // y_size, width_here), BF16),
            pltpu.VMEM((pieces, z_size, model_width // groups, width_here), BF16),
            pltpu.SemaphoreType.DMA((2, 2, pieces, y_size)),
            pltpu.SemaphoreType.DMA((2, 2, pieces, z_size)),
            pltpu.SemaphoreType.DMA((pieces,)),
            pltpu.VMEM((1, extra_rows, share), F32),
            pltpu.VMEM((groups, extra_rows, share), F32),
            pltpu.SemaphoreType.DMA((2, groups)),
            pltpu.SemaphoreType.DMA((2, shards)),
        ],
        compiler_params=pltpu.CompilerParams(
            vmem_limit_bytes=50 * 1024 * 1024, collective_id=3, has_side_effects=True
        ),
        name="dense_backward",
    )(
        normed_two_grad,
        after_mine,
        out_grad,
        mine(inputs),
        jnp.concatenate([scale_one, scale_two], axis=1),
        mine(jnp.stack([gain_attn, gain_moe])),
        extras,
        onehot_offsets.astype(BF16),
        attended,
        w_out,
        projected,
        probs,
        normed_low,
        w_qkv,
    )
    loss = jnp.sum(extras[:, experts + 2, 0]) / (2.0 * valid_total * model_width)
    whole = jnp.swapaxes(extras, 0, 1).reshape(extra_rows, model_width)
    table_rows = lax.dynamic_index_in_dim(extras, lax.axis_index("tensor"), 0, keepdims=False)
    table_sum = table_rows[experts + 4 : experts + 4 + heads_here, :BUCKETS].T
    out_proj_sum = jnp.swapaxes(dense[0].reshape(shards, width_here, width_here), 0, 1)
    return (
        block_out,
        loss,
        input_grad,
        whole[experts],
        dense[1:].astype(F32),
        out_proj_sum.reshape(width_here, model_width).astype(F32),
        table_sum,
        whole[experts + 1],
        whole[:experts].T,
        gate_up_grad,
        down_grad,
    )


def solution(mesh):
    placed = (
        P("dp", None),
        P("dp", None),
        P("dp"),
        P("dp", None),
        P("dp", None),
        P(),
        P(None, None, "tensor"),
        P("tensor", None),
        P(None, "tensor"),
        P(),
        P(),
        P("dp", None, None, "tensor"),
        P("dp", "tensor", None),
    )
    return jax.shard_map(
        body,
        mesh=mesh,
        in_specs=placed,
        out_specs=(
            P("dp", "tensor"),
            P(),
            P("dp", "tensor"),
            P(),
            P(None, None, "tensor"),
            P("tensor", None),
            P(None, "tensor"),
            P(),
            P(),
            P("dp", None, None, "tensor"),
            P("dp", "tensor", None),
        ),
        check_vma=False,
    )
```

```python
import functools
import math

import jax
import jax.numpy as jnp
from jax import lax
from jax.experimental import pallas as pl
from jax.experimental.pallas import tpu as pltpu
from jax.sharding import PartitionSpec as P

BUCKETS = 32
SEQ_LEN = 512
TILE = 128
SPAN = 2 * SEQ_LEN

EPSILON = 1e-06
FAR_STEPS = (12, 16, 23, 32, 46, 64, 91)
MASKED = -1000000000.0
F32 = jnp.float32
BF16 = jnp.bfloat16


def offset_bucket(offset):
    direction = jnp.where(offset > 0, 16, 0).astype(jnp.int32)
    distance = jnp.abs(offset)
    farther = jnp.full(offset.shape, 8, jnp.int32)
    for threshold in FAR_STEPS:
        farther = farther + (distance >= threshold).astype(jnp.int32)
    return direction + jnp.where(distance < 8, distance, farther)


def bucket_onehot(offsets):
    bucket_range = jnp.arange(BUCKETS, dtype=jnp.int32)
    return (offset_bucket(offsets)[:, None] == bucket_range[None, :]).astype(F32)


def dot(a, b, dims=((1,), (0,))):
    return lax.dot_general(a, b, (dims, ((), ())), preferred_element_type=F32)


VMEM = pl.BlockSpec(memory_space=pltpu.VMEM)
SMEM = pl.BlockSpec(memory_space=pltpu.SMEM)


MESH_ID = pl.DeviceIdType.MESH
ANY = pl.BlockSpec(memory_space=pl.ANY)


def weight_grads(shards, rows, grads, side, hidden, gate_up_out, down_out):
    step = pl.program_id(1)
    share = rows.shape[-1]

    @pl.when(step < 2)
    def _():
        for s in range(shards):
            gate_up_out[:, s * share : (s + 1) * share] = dot(side[...], rows[s], ((0,), (0,)))

    @pl.when(step == 2)
    def _():
        for s in range(shards):
            down_out[:, s * share : (s + 1) * share] = dot(hidden[...], grads[s], ((0,), (0,)))


def to_row(column):
    rows = column.shape[0]
    return jnp.transpose(jnp.broadcast_to(column, (rows, 128)))[:8]


def to_column(row):
    return jnp.transpose(jnp.broadcast_to(row[:1], (128, row.shape[1])))[:, :1]


def flip(value, mask, size):
    total, unit = 0, 1
    while unit < size:
        bit = lax.rem(lax.div(value, unit), 2)
        total = total + unit * ((1 - bit) if mask & unit else bit)
        unit *= 2
    return total


def plan(groups, chunk):
    kinds = ("spread", "relay", "products", "along", "give", "taken")
    steps = []
    for step in range(groups // chunk + len(kinds) - 1):
        for lag, kind in enumerate(kinds):
            k = step - lag
            if 0 <= k < groups // chunk:
                steps += [(kind, k)] if kind == "products" else [(kind, k * chunk + n) for n in range(chunk)]
    return steps


class Mover:
    def __init__(self, groups, shards, cap, chunk, rows, part, scratch):
        self.groups, self.lines, self.cap, self.chunk = groups, shards // 2, cap, chunk
        self.rows, self.part = rows, part
        (
            self.source, self.mate_in, self.line_out, self.line_in, self.back_out, self.back,
            self.dp_sems, self.row_sems, self.sum_sems,
        ) = scratch
        self.me, self.place = lax.axis_index("dp"), lax.axis_index("tensor")
        self.line, self.core = lax.div(self.place, 2), lax.rem(self.place, 2)
        self.steps = groups // chunk

    def peer(self, i):
        return flip(self.me, i, self.groups)

    def shard(self, offset, core):
        return lax.rem(self.line + offset, self.lines) * 2 + core

    def near(self, i):
        return lax.rem(self.place + i, 2 * self.lines)

    def remote(self, src, dst, sems, index, device):
        return pltpu.make_async_remote_copy(
            src_ref=src, dst_ref=dst, send_sem=sems.at[(0, *index)], recv_sem=sems.at[(1, *index)],
            device_id=device, device_id_type=MESH_ID,
        )

    def mate(self):
        return {"tensor": self.shard(0, 1 - self.core)}

    def landed(self, where, sems, index):
        self.remote(where, where, sems, index, self.mate()).wait_recv()

    def here(self, shard, i):
        return self.rows.at[shard, :, pl.ds(i * self.cap, self.cap), :]

    def send(self, i, block):
        block = block.reshape(-1, self.cap, block.shape[-1])
        if i == 0:
            self.rows[self.place, :, : self.cap, :] = block
        else:
            self.source[i] = block
            self.out_copy(i).start()

    def out_copy(self, i):
        return self.remote(
            self.source.at[i], self.here(self.place, i), self.dp_sems.at[0], (i,), {"dp": self.peer(i)}
        )

    def line_copy(self, d, i):
        return self.remote(
            self.here(self.place, i), self.here(self.place, i), self.row_sems.at[0], (d, i),
            {"tensor": self.shard(d, self.core)},
        )

    def mate_copy(self, d, i):
        shard = self.shard(self.lines - d, self.core)
        return self.remote(self.here(shard, i), self.here(shard, i), self.row_sems.at[1], (d, i), self.mate())

    def places(self, k):
        return range(k * self.chunk, (k + 1) * self.chunk)

    def spread(self, i):
        if i:
            self.landed(self.here(self.place, i), self.dp_sems.at[0], (i,))
        for d in range(1, self.lines):
            self.line_copy(d, i).start()
        self.mate_copy(0, i).start()

    def relay(self, i):
        for d in range(1, self.lines):
            shard = self.shard(self.lines - d, self.core)
            self.landed(self.here(shard, i), self.row_sems.at[0], (d, i))
            self.mate_copy(d, i).start()

    def collect(self, i):
        for d in range(self.lines):
            shard = self.shard(self.lines - d, 1 - self.core)
            self.landed(self.here(shard, i), self.row_sems.at[1], (d, i))

    def span(self, k):
        return pl.ds(k * self.chunk * self.cap, self.chunk * self.cap)

    def block(self, i):
        return pl.ds(i * self.cap, self.cap)

    def pair_copy(self, d, i):
        shard = self.shard(d, 1 - self.core)
        return self.remote(
            self.part.at[shard, :, self.block(i), :], self.mate_in.at[d, :, self.block(i), :], self.sum_sems.at[0], (d, i),
            self.mate(),
        )

    def sum_copy(self, d, i):
        return self.remote(
            self.line_out.at[d - 1, :, self.block(i), :], self.line_in.at[d - 1, :, self.block(i), :],
            self.sum_sems.at[1], (d, i), {"tensor": self.shard(d, self.core)},
        )

    def back_copy(self, i):
        return self.remote(
            self.back_out.at[:, self.block(i), :], self.back.at[i], self.dp_sems.at[1], (i,), {"dp": self.peer(i)}
        )

    def pair(self, k):
        for i in self.places(k):
            for d in range(self.lines):
                self.pair_copy(d, i).start()

    def pair_sum(self, d, i):
        shard = self.shard(d, self.core)
        return self.part[shard, :, self.block(i), :].astype(F32) + self.mate_in[d, :, self.block(i), :].astype(F32)

    def along(self, i):
        for d in range(self.lines):
            self.landed(self.mate_in.at[d, :, self.block(i), :], self.sum_sems.at[0], (d, i))
        for d in range(1, self.lines):
            self.line_out[d - 1, :, self.block(i), :] = self.pair_sum(d, i).astype(BF16)
            self.sum_copy(d, i).start()

    def give(self, i):
        total = self.pair_sum(0, i)
        for d in range(1, self.lines):
            self.landed(self.line_in.at[d - 1, :, self.block(i), :], self.sum_sems.at[1], (d, i))
            total = total + self.line_in[d - 1, :, self.block(i), :].astype(F32)
        total = total.astype(BF16)
        if i == 0:
            self.back[0] = total
        else:
            self.back_out[:, self.block(i), :] = total
            self.back_copy(i).start()

    def arrived(self, i):
        if i:
            self.landed(self.back.at[i], self.dp_sems.at[1], (i,))
        return self.back[i].reshape(-1, self.back.shape[-1])

    def run(self, compute, take):
        def products(k):
            for i in self.places(k):
                self.collect(i)
            compute(k)
            self.pair(k)

        def taken(i):
            take(i, self.arrived(i))

        works = dict(
            spread=self.spread, relay=self.relay, products=products, along=self.along, give=self.give, taken=taken
        )
        for work, index in plan(self.groups, self.chunk):
            works[work](index)

    def finish(self):
        for i in range(1, self.groups):
            self.out_copy(i).wait_send()
            self.back_copy(i).wait_send()
        for i in range(self.groups):
            for d in range(self.lines):
                if d:
                    self.line_copy(d, i).wait_send()
                    self.sum_copy(d, i).wait_send()
                self.mate_copy(d, i).wait_send()
                self.pair_copy(d, i).wait_send()


def mover_scratch(groups, shards, local, cap, share):
    lines, slots = shards // 2, groups * cap
    return [
        pltpu.VMEM((groups, local, cap, share), BF16),
        pltpu.VMEM((lines, local, slots, share), BF16),
        pltpu.VMEM((lines - 1, local, slots, share), BF16),
        pltpu.VMEM((lines - 1, local, slots, share), BF16),
        pltpu.VMEM((local, slots, share), BF16),
        pltpu.VMEM((groups, local, cap, share), BF16),
        pltpu.SemaphoreType.DMA((2, 2, groups)),
        pltpu.SemaphoreType.DMA((2, 2, lines, groups)),
        pltpu.SemaphoreType.DMA((2, 2, lines, groups)),
    ]


MOVER_REFS = 9
ROOT = math.sqrt(2.0 / math.pi)


def gelu_parts(v):
    inner = jnp.tanh(ROOT * (v + 0.044715 * (v * v * v)))
    half = 0.5 * (1.0 + inner)
    slope = half + 0.5 * v * (1.0 - inner * inner) * (ROOT * (1.0 + 3.0 * 0.044715 * v * v))
    return v * half, slope


def experts_both(
    groups, shards, local, cap, chunk, experts,
    len_ref, normed, after, columns, target_ref, ids_ref, router,
    teacher_hbm, gate_up_hbm, down_hbm,
    block_out, out_grad, norm_grad, extras, info,
    rows_hbm, grads_hbm, side_hbm, hidden_hbm,
    teacher, gate_up, down, rows, grads, part, pre, hidden, side, routed, gated, load_sems, save_sems,
    counts, count_sems, dots, dot_sems, *scratch,
):
    ahead = Mover(groups, shards, cap, chunk, rows, part, scratch[:MOVER_REFS])
    behind = Mover(groups, shards, cap, chunk, grads, part, scratch[MOVER_REFS:])
    tokens, share = normed.shape
    width = local * cap
    place = ahead.place
    mine = pl.ds(pl.multiple_of(place * share, 128), share)
    loads = [
        pltpu.make_async_copy(gate_up_hbm, gate_up, load_sems.at[0]),
        pltpu.make_async_copy(down_hbm, down, load_sems.at[1]),
        pltpu.make_async_copy(teacher_hbm.at[:, mine], teacher, load_sems.at[2]),
    ]
    for load in loads:
        load.start()

    barrier = pltpu.get_barrier_semaphore()
    for i in range(1, groups):
        pl.semaphore_signal(barrier, inc=1, device_id={"dp": ahead.peer(i)}, device_id_type=MESH_ID)
    for i in range(1, shards):
        pl.semaphore_signal(barrier, inc=1, device_id={"tensor": ahead.near(i)}, device_id_type=MESH_ID)
    counts[0] = jnp.full((8, 128), len_ref[0], jnp.int32)
    slot_lines = lax.broadcasted_iota(jnp.int32, (width, tokens), 0)
    slot_lanes = lax.broadcasted_iota(jnp.int32, (tokens, width), 1)
    row_targets = [target_ref[n : n + 1, :] for n in range(2)]
    column_targets = [to_column(target_ref[n : n + 1, :].astype(F32)).astype(jnp.int32) for n in range(2)]

    def by_slot(i, n):
        return slot_lines + ahead.peer(i) * width == row_targets[n]

    def by_token(i, n):
        return slot_lanes + ahead.peer(i) * width == column_targets[n]

    def ones(mask):
        return jnp.where(mask, 1.0, 0.0).astype(BF16)

    pl.semaphore_wait(barrier, groups + shards - 2)

    def count_copy(i):
        return ahead.remote(counts.at[0], counts.at[i], count_sems, (i,), {"dp": ahead.peer(i)})

    order = [*range(1, groups), 0]
    for i in order:
        ahead.send(i, dot(ones(by_slot(i, 0) | by_slot(i, 1)), normed[...]).astype(BF16))
    for i in range(1, groups):
        count_copy(i).start()

    def forward_saves(k):
        span = ahead.span(k)
        return [
            pltpu.make_async_copy(rows.at[:, :, span, :], rows_hbm.at[:, :, span, :], save_sems.at[0, k]),
            pltpu.make_async_copy(hidden.at[:, span, :], hidden_hbm.at[:, span, :], save_sems.at[1, k]),
        ]

    def backward_saves(k):
        span = ahead.span(k)
        return [
            pltpu.make_async_copy(grads.at[:, :, span, :], grads_hbm.at[:, :, span, :], save_sems.at[2, k]),
            pltpu.make_async_copy(side.at[:, :, span, :], side_hbm.at[:, :, span, :], save_sems.at[3, k]),
        ]

    def put(e, span, result):
        result = result.astype(BF16)
        for s in range(shards):
            part[s, e, span, :] = result[:, s * share : (s + 1) * share]

    def forward(k):
        span = ahead.span(k)
        if k == 0:
            loads[0].wait()
            loads[1].wait()
        for e in range(local):
            lhs = jnp.concatenate([rows[s, e, span, :] for s in range(shards)], axis=1)
            gate = dot(lhs, gate_up[e, 0], ((1,), (1,)))
            up = dot(lhs, gate_up[e, 1], ((1,), (1,)))
            pre[0, e, span, :] = gate
            pre[1, e, span, :] = up
            low = (gelu_parts(gate)[0] * up).astype(BF16)
            hidden[e, span, :] = low
            put(e, span, dot(low, down[e]))
        for save in forward_saves(k):
            save.start()

    def take(i, block):
        for n in range(2):
            value = dot(ones(by_token(i, n)), block)
            if i == 0:
                routed[n] = value
            else:
                routed[n] += value

    ahead.run(forward, take)

    tally = counts[0]
    for i in range(1, groups):
        count_copy(i).wait()
        tally = tally + counts[i]
    valid = tally.astype(F32)
    loads[2].wait()
    gates = [columns[:, 2:3], columns[:, 3:4]]
    output = after[...] + gates[0] * routed[0] + gates[1] * routed[1]
    block_out[...] = output
    alive = lax.broadcasted_iota(jnp.int32, (tokens, share), 0) < len_ref[0]
    deviation = jnp.where(alive, output - teacher[...].astype(F32), 0.0)
    scaled = deviation * (groups * tokens / valid[0:1, 0:1])
    out_grad[...] = scaled
    for n in range(2):
        gated[n * tokens : (n + 1) * tokens, :] = (gates[n] * scaled).astype(BF16)
    for i in order:
        both = jnp.concatenate([ones(by_slot(i, 0)), ones(by_slot(i, 1))], axis=1)
        behind.send(i, dot(both, gated[...]).astype(BF16))
    for n in range(2):
        dots[n, 0] = to_row(jnp.sum(routed[n] * scaled, axis=1, keepdims=True))

    def dot_copy(n, i):
        return ahead.remote(dots.at[n, 0], dots.at[n, i], dot_sems, (n, i), {"tensor": ahead.near(i)})

    for n in range(2):
        for i in range(1, shards):
            dot_copy(n, i).start()
    info[...] = valid
    extras[...] = jnp.zeros_like(extras)
    extras[experts + 2 : experts + 3, :] = jnp.sum(deviation * deviation, axis=0, keepdims=True)
    ahead.finish()

    def route_grads():
        parts = []
        for n in range(2):
            total = dots[n, 0]
            for i in range(1, shards):
                dot_copy(n, i).wait()
                total = total + dots[n, i]
            parts.append(to_column(total))
        expert_probs = columns[:, 16 : 16 + experts]
        lanes = lax.broadcasted_iota(jnp.int32, (tokens, experts), 1)
        picks = [
            jnp.where(lanes == to_column(ids_ref[n : n + 1, :].astype(F32)).astype(jnp.int32), 1.0, 0.0)
            for n in range(2)
        ]
        chosen_total = jnp.sum(expert_probs * (picks[0] + picks[1]), axis=1, keepdims=True)
        along = parts[0] * gates[0] + parts[1] * gates[1]
        probs_grad = sum(picks[n] * ((parts[n] - along) / chosen_total) for n in range(2))
        logit_grad = expert_probs * (probs_grad - jnp.sum(probs_grad * expert_probs, axis=1, keepdims=True))
        logit_grad = logit_grad.astype(BF16)
        extras[0:experts, :] = dot(logit_grad, normed[...], ((0,), (0,)))
        norm_grad[...] = dot(logit_grad, router[:, mine])

    def backward(k):
        span = ahead.span(k)
        for e in range(local):
            lhs = jnp.concatenate([grads[s, e, span, :] for s in range(shards)], axis=1)
            hidden_grad = dot(lhs, down[e], ((1,), (1,)))
            activated, slope = gelu_parts(pre[0, e, span, :])
            gate_side = (hidden_grad * pre[1, e, span, :] * slope).astype(BF16)
            up_side = (hidden_grad * activated).astype(BF16)
            side[0, e, span, :] = gate_side
            side[1, e, span, :] = up_side
            put(e, span, dot(gate_side, gate_up[e, 0]) + dot(up_side, gate_up[e, 1]))
        for save in backward_saves(k):
            save.start()
        if k == 0:
            route_grads()

    def take_back(i, block):
        norm_grad[...] += dot(ones(by_token(i, 0) | by_token(i, 1)), block)

    behind.run(backward, take_back)
    behind.finish()
    for k in range(ahead.steps):
        for save in forward_saves(k) + backward_saves(k):
            save.wait()


def gate_columns(logits, first, second):
    lanes = lax.broadcasted_iota(jnp.int32, logits.shape, 1)
    exponent = jnp.exp(logits - jnp.max(logits, axis=1, keepdims=True))
    expert_probs = exponent / jnp.sum(exponent, axis=1, keepdims=True)
    chosen = [jnp.sum(jnp.where(lanes == pick, expert_probs, 0.0), axis=1, keepdims=True) for pick in (first, second)]
    total = chosen[0] + chosen[1]
    return expert_probs, chosen[0] / total, chosen[1] / total


def dense_forward(
    groups, shards, heads, width, experts,
    len_ref, bias_ref, ids_ref, gains, router_ref,
    inputs_hbm, w_qkv_hbm, w_out_hbm,
    normed_out, proj_out, probs_out, attended_out, after_out, normed_two_out, columns_out,
    inputs, w_qkv, load_sems, w_out, w_sems, attended, attended_sems, skew, normed, proj, probs, after, normed_two, save_sems,
):
    tokens, model = inputs.shape
    here = heads * width
    share = model // shards
    lines = shards // 2
    blocks = tokens // TILE
    place = lax.axis_index("tensor")
    line, core = lax.div(place, 2), lax.rem(place, 2)
    mate = {"tensor": line * 2 + 1 - core}

    def shard(d, c):
        return lax.rem(line + d, lines) * 2 + c

    def remote(src, dst, sems, index, device):
        return pltpu.make_async_remote_copy(
            src_ref=src, dst_ref=dst, send_sem=sems.at[(0, *index)], recv_sem=sems.at[(1, *index)],
            device_id=device, device_id_type=MESH_ID,
        )

    def landed(where, sems, index):
        remote(where, where, sems, index, mate).wait_recv()

    loads = [
        pltpu.make_async_copy(inputs_hbm, inputs, load_sems.at[0]),
        pltpu.make_async_copy(w_qkv_hbm, w_qkv, load_sems.at[1]),
        pltpu.make_async_copy(w_out_hbm, w_out.at[place], load_sems.at[2]),
    ]
    for load in loads:
        load.start()
    barrier = pltpu.get_barrier_semaphore()
    for d in range(1, lines):
        pl.semaphore_signal(barrier, inc=1, device_id={"tensor": shard(d, core)}, device_id_type=MESH_ID)
    pl.semaphore_signal(barrier, inc=1, device_id=mate, device_id_type=MESH_ID)
    pl.semaphore_wait(barrier, lines)

    def w_line(d):
        return remote(w_out.at[place], w_out.at[place], w_sems.at[0], (d,), {"tensor": shard(d, core)})

    def w_mate(d):
        where = w_out.at[shard(lines - d, core)]
        return remote(where, where, w_sems.at[1], (d,), mate)

    def row_block(j):
        return pl.ds(j * TILE, TILE)

    def rows_line(d, j):
        where = attended.at[place, row_block(j), :]
        return remote(where, where, attended_sems.at[0], (d, j), {"tensor": shard(d, core)})

    def rows_mate(d, j):
        where = attended.at[shard(lines - d, core), row_block(j), :]
        return remote(where, where, attended_sems.at[1], (d, j), mate)

    loads[2].wait()
    for d in range(1, lines):
        w_line(d).start()
    w_mate(0).start()

    loads[0].wait()
    for j in range(blocks):
        rows = slice(j * TILE, (j + 1) * TILE)
        values = inputs[rows, :].astype(F32)
        scale = lax.rsqrt(jnp.mean(values * values, axis=1, keepdims=True) + EPSILON)
        columns_out[rows, 0:1] = scale
        normed[rows, :] = (values * scale * gains[0:1, :]).astype(BF16)
    loads[1].wait()
    for n in range(3):
        proj[n] = dot(normed[...], w_qkv[n]).astype(BF16)
    saves = [
        pltpu.make_async_copy(normed, normed_out, save_sems.at[0]),
        pltpu.make_async_copy(proj, proj_out, save_sems.at[1]),
    ]
    for h in range(heads):
        skew[h] = pltpu.roll(
            jnp.broadcast_to(bias_ref[h : h + 1, :], (TILE, SPAN)), 0, 1, stride=1, stride_axis=0
        )
    for item in saves:
        item.start()

    alive = lax.broadcasted_iota(jnp.int32, (TILE, SEQ_LEN), 1) < len_ref[0]
    for j in range(blocks):
        rows = slice(j * TILE, (j + 1) * TILE)
        start = SEQ_LEN - j * TILE
        for h in range(heads):
            cols = slice(h * width, (h + 1) * width)
            scores = dot(proj[0, rows, cols], proj[1, :, cols], ((1,), (1,)))
            scores = jnp.where(alive, scores + skew[h, :, start : start + SEQ_LEN], MASKED)
            exponent = jnp.exp(scores - jnp.max(scores, axis=1, keepdims=True))
            weights = exponent * (1.0 / jnp.sum(exponent, axis=1, keepdims=True))
            probs[h, rows, :] = weights
            attended[place, rows, cols] = dot(weights.astype(BF16), proj[2, :, cols]).astype(BF16)
        for d in range(1, lines):
            rows_line(d, j).start()
        rows_mate(0, j).start()
        if j == blocks - 2:
            for d in range(1, lines):
                landed(w_out.at[shard(lines - d, core)], w_sems.at[0], (d,))
                w_mate(d).start()
    saves += [
        pltpu.make_async_copy(probs, probs_out, save_sems.at[2]),
        pltpu.make_async_copy(attended.at[place], attended_out, save_sems.at[3]),
    ]
    for item in saves[2:]:
        item.start()

    ids = ids_ref[...].astype(F32)
    picks = [to_column(ids[n : n + 1]).astype(jnp.int32) for n in range(2)]

    def relay(j):
        for d in range(1, lines):
            landed(attended.at[shard(lines - d, core), row_block(j), :], attended_sems.at[0], (d, j))
            rows_mate(d, j).start()

    relay(0)
    for d in range(lines):
        landed(w_out.at[shard(lines - d, 1 - core)], w_sems.at[1], (d,))
    for j in range(blocks):
        rows = slice(j * TILE, (j + 1) * TILE)
        if j + 1 < blocks:
            relay(j + 1)
        for d in range(lines):
            landed(attended.at[shard(lines - d, 1 - core), row_block(j), :], attended_sems.at[1], (d, j))
        total = inputs[rows, :].astype(F32)
        for s in range(shards):
            total = total + dot(attended[s, rows, :], w_out[s])
        scale = lax.rsqrt(jnp.mean(total * total, axis=1, keepdims=True) + EPSILON)
        low = (total * scale * gains[1:2, :]).astype(BF16)
        after[...] = total
        normed_two[...] = low
        mine = pl.ds(pl.multiple_of(place * share, 128), share)
        after_out[rows, :] = after[:, mine]
        normed_two_out[rows, :] = normed_two[:, mine]
        expert_probs, first, second = gate_columns(
            dot(low, router_ref[...], ((1,), (1,))), picks[0][rows], picks[1][rows]
        )
        columns_out[rows, 1:2] = scale
        columns_out[rows, 2:3] = first
        columns_out[rows, 3:4] = second
        columns_out[rows, 16 : 16 + experts] = expert_probs
    for d in range(lines):
        if d:
            w_line(d).wait_send()
        w_mate(d).wait_send()
        for j in range(blocks):
            if d:
                rows_line(d, j).wait_send()
            rows_mate(d, j).wait_send()
    for item in saves:
        item.wait()


def dense_backward(
    groups, shards, heads, width, experts,
    norm_grad, after, out_grad, residual, scales, gains, extras_in, onehot,
    attended_hbm, w_out_hbm, proj_hbm, probs_hbm, normed_hbm, w_qkv_hbm,
    dense_out, input_grad, extras_out,
    attended, w_out, proj, probs, normed, w_qkv, load_sems,
    dots, dot_sems, branch, branch_sems, grad_here, diag, key_acc, value_acc, proj_grad,
    part, mate_in, line_out, line_in, part_sems,
    dense, result, y_in, y_sum, z_in, dense_sems, z_sems, save_sems,
    extras, extras_in_dp, extras_sems, extras_ring_sems,
):
    model = normed.shape[1]
    share = branch.shape[-1]
    tokens = branch.shape[1]
    here = heads * width
    lines = shards // 2
    y_size = 1 << ((groups.bit_length() - 1) // 2)
    z_size = groups // y_size
    pieces = dense.shape[0]
    me, place = lax.axis_index("dp"), lax.axis_index("tensor")
    line, core = lax.div(place, 2), lax.rem(place, 2)
    z, y = lax.div(me, y_size), lax.rem(me, y_size)
    mate = {"tensor": line * 2 + 1 - core}
    inverse = 1.0 / model

    def group(i):
        return lax.rem(me + i, groups)

    def shard(d, c):
        return lax.rem(line + d, lines) * 2 + c

    def near(i):
        return lax.rem(place + i, shards)

    def remote(src, dst, sems, index, device):
        return pltpu.make_async_remote_copy(
            src_ref=src, dst_ref=dst, send_sem=sems.at[(0, *index)], recv_sem=sems.at[(1, *index)],
            device_id=device, device_id_type=MESH_ID,
        )

    def landed(where, sems, index):
        remote(where, where, sems, index, mate).wait_recv()

    loads = [
        pltpu.make_async_copy(src, dst, load_sems.at[n])
        for n, (src, dst) in enumerate(
            (
                (w_out_hbm, w_out), (attended_hbm, attended), (proj_hbm, proj), (probs_hbm, probs),
                (w_qkv_hbm, w_qkv), (normed_hbm, normed),
            )
        )
    ]
    for load in loads:
        load.start()

    barrier = pltpu.get_barrier_semaphore()
    for i in range(1, groups):
        pl.semaphore_signal(barrier, inc=1, device_id={"dp": group(i)}, device_id_type=MESH_ID)
    for i in range(1, shards):
        pl.semaphore_signal(barrier, inc=1, device_id={"tensor": near(i)}, device_id_type=MESH_ID)
    pl.semaphore_wait(barrier, groups + shards - 2)

    def dot_copy(n, i):
        return remote(dots.at[n, 0], dots.at[n, i], dot_sems, (n, i), {"tensor": near(i)})

    def dot_send(n, column):
        dots[n, 0] = to_row(column)
        for i in range(1, shards):
            dot_copy(n, i).start()

    def dot_sum(n):
        total = dots[n, 0]
        for i in range(1, shards):
            dot_copy(n, i).wait()
            total = total + dots[n, i]
        return to_column(total)

    scale_two = scales[:, 1:2]
    weighted = norm_grad[...] * gains[1:2, :]
    dot_send(0, jnp.sum(weighted * after[...], axis=1, keepdims=True))
    extras[0] = extras_in[...]
    extras[0, experts + 1 : experts + 2, :] = jnp.sum(norm_grad[...] * after[...] * scale_two, axis=0, keepdims=True)
    along = dot_sum(0)
    after_grad = out_grad[...] + scale_two * (weighted - after[...] * (scale_two * scale_two * along * inverse))
    grad_here[...] = after_grad
    branch[place] = after_grad.astype(BF16)

    blocks = tokens // TILE

    def row_block(j):
        return pl.ds(j * TILE, TILE)

    def branch_line(d, j):
        where = branch.at[place, row_block(j), :]
        return remote(where, where, branch_sems.at[0], (d, j), {"tensor": shard(d, core)})

    def branch_mate(d, j):
        where = branch.at[shard(lines - d, core), row_block(j), :]
        return remote(where, where, branch_sems.at[1], (d, j), mate)

    for j in range(blocks):
        for d in range(1, lines):
            branch_line(d, j).start()
        branch_mate(0, j).start()
    for j in range(blocks):
        for d in range(1, lines):
            landed(branch.at[shard(lines - d, core), row_block(j), :], branch_sems.at[0], (d, j))
            branch_mate(d, j).start()
    for j in range(blocks):
        for d in range(lines):
            landed(branch.at[shard(lines - d, 1 - core), row_block(j), :], branch_sems.at[1], (d, j))
    loads[0].wait()
    loads[1].wait()

    y_rows, z_rows = model // y_size, model // groups

    def y_copy(p, a):
        to = lax.rem(y + a, y_size)
        return remote(
            dense.at[p, pl.ds(to * y_rows, y_rows), :], y_in.at[p, a], dense_sems.at[0], (p, a), {"dp": z * y_size + to}
        )

    def z_copy(p, b):
        to = lax.rem(z + b, z_size)
        return remote(
            y_sum.at[p, pl.ds(to * z_rows, z_rows), :], z_in.at[p, b], z_sems.at[0], (p, b), {"dp": to * y_size + y}
        )

    def z_spread(p, b):
        to = lax.rem(z + b, z_size)
        where = result.at[p, pl.ds(y * y_rows + z * z_rows, z_rows), :]
        return remote(where, where, z_sems.at[1], (p, b), {"dp": to * y_size + y})

    def y_spread(p, a):
        to = lax.rem(y + a, y_size)
        where = result.at[p, pl.ds(y * y_rows, y_rows), :]
        return remote(where, where, dense_sems.at[1], (p, a), {"dp": z * y_size + to})

    def reduce_start(p):
        for a in range(1, y_size):
            y_copy(p, a).start()

    def reduce_y(p):
        total = dense[p, pl.ds(y * y_rows, y_rows), :].astype(F32)
        for a in range(1, y_size):
            landed(y_in.at[p, a], dense_sems.at[0], (p, a))
            total = total + y_in[p, a].astype(F32)
        y_sum[p] = total.astype(BF16)
        for b in range(1, z_size):
            z_copy(p, b).start()

    def reduce_z(p):
        total = y_sum[p, pl.ds(z * z_rows, z_rows), :].astype(F32)
        for a in range(1, y_size):
            y_copy(p, a).wait_send()
        for b in range(1, z_size):
            landed(z_in.at[p, b], z_sems.at[0], (p, b))
            total = total + z_in[p, b].astype(F32)
        result[p, pl.ds(y * y_rows + z * z_rows, z_rows), :] = total.astype(BF16)
        for b in range(1, z_size):
            z_spread(p, b).start()

    def spread_z(p):
        for b in range(1, z_size):
            origin = lax.rem(z + z_size - b, z_size)
            landed(result.at[p, pl.ds(y * y_rows + origin * z_rows, z_rows), :], z_sems.at[1], (p, b))
        for a in range(1, y_size):
            y_spread(p, a).start()

    def save(p):
        return pltpu.make_async_copy(result.at[p], dense_out.at[p], save_sems.at[p])

    def spread_y(p):
        for a in range(1, y_size):
            origin = lax.rem(y + y_size - a, y_size)
            landed(result.at[p, pl.ds(origin * y_rows, y_rows), :], dense_sems.at[1], (p, a))
        save(p).start()

    for s in range(shards):
        dense[0, s * here : (s + 1) * here, :] = dot(
            attended[...], branch[s], ((0,), (0,))
        ).astype(BF16)
    reduce_start(0)

    loads[2].wait()
    loads[3].wait()
    diag[...] = jnp.zeros_like(diag)
    for j in range(blocks):
        rows = slice(j * TILE, (j + 1) * TILE)
        start = SEQ_LEN - j * TILE
        wide = jnp.concatenate([branch[s, rows, :] for s in range(shards)], axis=1)
        grads = dot(wide, w_out[...], ((1,), (1,))).astype(BF16)
        for h in range(heads):
            cols = slice(h * width, (h + 1) * width)
            p = probs[h, rows, :]
            grad = grads[:, cols]
            prob_grad = dot(grad, proj[2, :, cols], ((1,), (1,)))
            score_grad = p * (prob_grad - jnp.sum(p * prob_grad, axis=1, keepdims=True))
            diag[h, :, start : start + SEQ_LEN] += score_grad
            low = score_grad.astype(BF16)
            proj_grad[0, rows, cols] = dot(low, proj[1, :, cols]).astype(BF16)
            key_part = dot(low, proj[0, rows, cols], ((0,), (0,)))
            value_part = dot(p.astype(BF16), grad, ((0,), (0,)))
            if j == 0:
                key_acc[:, cols] = key_part
                value_acc[:, cols] = value_part
            else:
                key_acc[:, cols] += key_part
                value_acc[:, cols] += value_part
        if j == 1:
            reduce_y(0)
    proj_grad[1] = key_acc[...].astype(BF16)
    proj_grad[2] = value_acc[...].astype(BF16)
    reduce_z(0)

    loads[4].wait()
    loads[5].wait()
    for p in range(1, pieces):
        dense[p] = dot(normed[...], proj_grad[p - 1], ((0,), (0,))).astype(BF16)
        reduce_start(p)
    half = tokens // 2

    def part_rows(k):
        return pl.ds(k * half, half)

    def pair_copy(d, k):
        return remote(
            part.at[shard(d, 1 - core), part_rows(k), :], mate_in.at[d, part_rows(k), :], part_sems.at[0], (d, k), mate
        )

    def line_copy(d, k):
        return remote(
            line_out.at[d, part_rows(k), :], line_in.at[d, part_rows(k), :], part_sems.at[1], (d, k),
            {"tensor": shard(d, core)},
        )

    for k in range(2):
        rows = slice(k * half, (k + 1) * half)
        total = dot(proj_grad[0, rows, :], w_qkv[0], ((1,), (1,)))
        for n in range(1, 3):
            total = total + dot(proj_grad[n, rows, :], w_qkv[n], ((1,), (1,)))
        low = total.astype(BF16)
        for s in range(shards):
            part[s, rows, :] = low[:, s * share : (s + 1) * share]
        for d in range(lines):
            pair_copy(d, k).start()
    spread_z(0)

    def pair_sum(d, rows):
        return part[shard(d, core), rows, :].astype(F32) + mate_in[d, rows, :].astype(F32)

    for k in range(2):
        rows = part_rows(k)
        for d in range(lines):
            landed(mate_in.at[d, rows, :], part_sems.at[0], (d, k))
        for d in range(1, lines):
            line_out[d, rows, :] = pair_sum(d, rows).astype(BF16)
            line_copy(d, k).start()
    for h in range(heads):
        total = diag[h]
        size = TILE // 2
        while size >= 1:
            total = total[:size] + pltpu.roll(total[size : 2 * size], SPAN - size, 1)
            size //= 2
        row = jnp.broadcast_to(total, (8, SPAN))
        high = row.astype(BF16)
        middle = (row - high.astype(F32)).astype(BF16)
        low = (row - high.astype(F32) - middle.astype(F32)).astype(BF16)
        table = dot(high, onehot[...]) + dot(middle, onehot[...]) + dot(low, onehot[...])
        extras[0, experts + 4 + h : experts + 5 + h, : onehot.shape[1]] = table[:1]
    for p in range(1, pieces):
        reduce_y(p)

    total = pair_sum(0, pl.ds(0, tokens))
    for k in range(2):
        for d in range(1, lines):
            landed(line_in.at[d, part_rows(k), :], part_sems.at[1], (d, k))
    for d in range(1, lines):
        total = total + line_in[d].astype(F32)
    scale_one = scales[:, 0:1]
    values = residual[...].astype(F32)
    weighted = total * gains[0:1, :]
    dot_send(1, jnp.sum(weighted * values, axis=1, keepdims=True))
    extras[0, experts : experts + 1, :] = jnp.sum(total * values * scale_one, axis=0, keepdims=True)

    def extras_copy(i):
        return remote(extras.at[0], extras_in_dp.at[i], extras_sems, (i,), {"dp": group(i)})

    for i in range(1, groups):
        extras_copy(i).start()
    for p in range(1, pieces):
        reduce_z(p)
    along = dot_sum(1)
    input_grad[...] = grad_here[...] + scale_one * (weighted - values * (scale_one * scale_one * along * inverse))

    summed = extras[0]
    for i in range(1, groups):
        extras_copy(i).wait()
        summed = summed + extras_in_dp[i]
    extras_out[place] = summed

    def ring_copy(i):
        return remote(extras_out.at[place], extras_out.at[place], extras_ring_sems, (i,), {"tensor": near(i)})

    for i in range(1, shards):
        ring_copy(i).start()
    for p in range(1, pieces):
        spread_z(p)
    for p in range(pieces):
        spread_y(p)
    for i in range(1, shards):
        landed(extras_out.at[near(shards - i)], extras_ring_sems, (i,))
        ring_copy(i).wait_send()
    for j in range(blocks):
        for d in range(lines):
            if d:
                branch_line(d, j).wait_send()
            branch_mate(d, j).wait_send()
    for k in range(2):
        for d in range(lines):
            if d:
                line_copy(d, k).wait_send()
            pair_copy(d, k).wait_send()
    for p in range(pieces):
        for b in range(1, z_size):
            z_copy(p, b).wait_send()
            z_spread(p, b).wait_send()
        for a in range(1, y_size):
            y_spread(p, a).wait_send()
        save(p).wait()


def body(
    inputs,
    teacher,
    lengths,
    expert_ids,
    route_slots,
    gain_attn,
    w_qkv,
    w_out,
    rel_table,
    gain_moe,
    w_router,
    w_gate_up,
    w_down,
):
    highest = lax.Precision.HIGHEST
    tok_rows, model_width = inputs.shape
    groups = lax.axis_size("dp")
    shards = lax.axis_size("tensor")
    experts = w_router.shape[1]
    local_experts = w_gate_up.shape[0]
    capacity = 10 * tok_rows // (4 * experts)
    padded_cap = (capacity + 15) // 16 * 16
    slot_count = experts * padded_cap
    heads_here = rel_table.shape[1]
    width_here = w_qkv.shape[2]
    head_width = width_here // heads_here
    share = model_width // shards
    column_start = lax.axis_index("tensor") * share

    def mine(values):
        return lax.dynamic_slice_in_dim(values, column_start, share, values.ndim - 1)

    offsets = jnp.arange(SPAN, dtype=jnp.int32) - SEQ_LEN
    onehot_offsets = bucket_onehot(offsets)
    offset_bias = jnp.dot(onehot_offsets, rel_table, precision=highest).T
    lines = shards // 2
    blocks = tok_rows // TILE
    ids = expert_ids.T
    normed_low, projected, probs, attended, after_mine, normed_mine, columns = pl.pallas_call(
        functools.partial(dense_forward, groups, shards, heads_here, head_width, experts),
        out_shape=(
            jax.ShapeDtypeStruct((tok_rows, model_width), BF16),
            jax.ShapeDtypeStruct((3, tok_rows, width_here), BF16),
            jax.ShapeDtypeStruct((heads_here, SEQ_LEN, SEQ_LEN), F32),
            jax.ShapeDtypeStruct((tok_rows, width_here), BF16),
            jax.ShapeDtypeStruct((tok_rows, share), F32),
            jax.ShapeDtypeStruct((tok_rows, share), BF16),
            jax.ShapeDtypeStruct((tok_rows, 128), F32),
        ),
        in_specs=[SMEM] + [VMEM] * 4 + [ANY] * 3,
        out_specs=(ANY,) * 4 + (VMEM,) * 3,
        scratch_shapes=[
            pltpu.VMEM((tok_rows, model_width), BF16),
            pltpu.VMEM(w_qkv.shape, BF16),
            pltpu.SemaphoreType.DMA((3,)),
            pltpu.VMEM((shards, width_here, model_width), BF16),
            pltpu.SemaphoreType.DMA((2, 2, lines)),
            pltpu.VMEM((shards, tok_rows, width_here), BF16),
            pltpu.SemaphoreType.DMA((2, 2, lines, blocks)),
            pltpu.VMEM((heads_here, TILE, SPAN), F32),
            pltpu.VMEM((tok_rows, model_width), BF16),
            pltpu.VMEM((3, tok_rows, width_here), BF16),
            pltpu.VMEM((heads_here, SEQ_LEN, SEQ_LEN), F32),
            pltpu.VMEM((TILE, model_width), F32),
            pltpu.VMEM((TILE, model_width), BF16),
            pltpu.SemaphoreType.DMA((4,)),
        ],
        compiler_params=pltpu.CompilerParams(
            vmem_limit_bytes=40 * 1024 * 1024, collective_id=4, has_side_effects=True
        ),
        name="dense_forward",
    )(lengths, offset_bias, ids, jnp.stack([gain_attn, gain_moe]), w_router.T, inputs, w_qkv, w_out)
    scale_one, scale_two = columns[:, 0:1], columns[:, 1:2]
    kept_route = route_slots < capacity
    target = jnp.where(kept_route, expert_ids * padded_cap + route_slots, -1).T
    gate_up_t = jnp.swapaxes(w_gate_up, 2, 3)
    chunk = max(groups // 4, 1)
    steps = groups // chunk
    slots = groups * padded_cap
    ff_here = w_down.shape[1]
    sizes = (groups, shards, local_experts, padded_cap)
    rows_shape = (shards, local_experts, slots, share)
    extra_rows = experts + 8
    token_type = jax.ShapeDtypeStruct((tok_rows, share), F32)
    block_out, out_grad, normed_two_grad, extras, info, expert_rows, expert_grad, pre_grads, hidden_low = pl.pallas_call(
        functools.partial(experts_both, *sizes, chunk, experts),
        out_shape=(
            token_type,
            token_type,
            token_type,
            jax.ShapeDtypeStruct((extra_rows, share), F32),
            jax.ShapeDtypeStruct((8, 128), F32),
            jax.ShapeDtypeStruct(rows_shape, BF16),
            jax.ShapeDtypeStruct(rows_shape, BF16),
            jax.ShapeDtypeStruct((2, local_experts, slots, ff_here), BF16),
            jax.ShapeDtypeStruct((local_experts, slots, ff_here), BF16),
        ),
        in_specs=[SMEM] + [VMEM] * 6 + [ANY] * 3,
        out_specs=(VMEM,) * 5 + (ANY,) * 4,
        scratch_shapes=[
            pltpu.VMEM((tok_rows, share), BF16),
            pltpu.VMEM(gate_up_t.shape, BF16),
            pltpu.VMEM(w_down.shape, BF16),
            pltpu.VMEM(rows_shape, BF16),
            pltpu.VMEM(rows_shape, BF16),
            pltpu.VMEM(rows_shape, BF16),
            pltpu.VMEM((2, local_experts, slots, ff_here), F32),
            pltpu.VMEM((local_experts, slots, ff_here), BF16),
            pltpu.VMEM((2, local_experts, slots, ff_here), BF16),
            pltpu.VMEM((2, tok_rows, share), F32),
            pltpu.VMEM((2 * tok_rows, share), BF16),
            pltpu.SemaphoreType.DMA((3,)),
            pltpu.SemaphoreType.DMA((4, steps)),
            pltpu.VMEM((groups, 8, 128), jnp.int32),
            pltpu.SemaphoreType.DMA((2, groups)),
            pltpu.VMEM((2, shards, 8, tok_rows), F32),
            pltpu.SemaphoreType.DMA((2, 2, shards)),
        ]
        + mover_scratch(*sizes, share) * 2,
        compiler_params=pltpu.CompilerParams(
            vmem_limit_bytes=58 * 1024 * 1024, collective_id=1, has_side_effects=True
        ),
        name="experts_both",
    )(lengths, normed_mine, after_mine, columns, target, ids, w_router.T, teacher, gate_up_t, w_down)
    valid_total = info[0, 0]

    gate_up_grad, down_grad = pl.pallas_call(
        functools.partial(weight_grads, shards),
        grid=(local_experts, 3),
        out_shape=(
            jax.ShapeDtypeStruct(gate_up_t.shape, F32),
            jax.ShapeDtypeStruct(w_down.shape, F32),
        ),
        in_specs=[
            pl.BlockSpec((shards, None, slots, share), lambda e, j: (0, e, 0, 0)),
            pl.BlockSpec((shards, None, slots, share), lambda e, j: (0, e, 0, 0)),
            pl.BlockSpec((None, None, slots, ff_here), lambda e, j: (jnp.minimum(j, 1), e, 0, 0)),
            pl.BlockSpec((None, slots, ff_here), lambda e, j: (e, 0, 0)),
        ],
        out_specs=(
            pl.BlockSpec((None, None, ff_here, model_width), lambda e, j: (e, jnp.minimum(j, 1), 0, 0)),
            pl.BlockSpec((None, ff_here, model_width), lambda e, j: (e, 0, 0)),
        ),
        compiler_params=pltpu.CompilerParams(vmem_limit_bytes=48 * 1024 * 1024),
        name="weight_grads",
    )(expert_rows, expert_grad, pre_grads, hidden_low)
    gate_up_grad = jnp.swapaxes(gate_up_grad, 2, 3)

    y_size = 1 << ((groups.bit_length() - 1) // 2)
    z_size = groups // y_size
    pieces = 1 + 3
    dense, input_grad, extras = pl.pallas_call(
        functools.partial(dense_backward, groups, shards, heads_here, head_width, experts),
        out_shape=(
            jax.ShapeDtypeStruct((pieces, model_width, width_here), BF16),
            jax.ShapeDtypeStruct((tok_rows, share), F32),
            jax.ShapeDtypeStruct((shards, extra_rows, share), F32),
        ),
        in_specs=[VMEM] * 8 + [ANY] * 6,
        out_specs=(ANY, VMEM, VMEM),
        scratch_shapes=[
            pltpu.VMEM(attended.shape, BF16),
            pltpu.VMEM(w_out.shape, BF16),
            pltpu.VMEM(projected.shape, BF16),
            pltpu.VMEM(probs.shape, F32),
            pltpu.VMEM(normed_low.shape, BF16),
            pltpu.VMEM(w_qkv.shape, BF16),
            pltpu.SemaphoreType.DMA((6,)),
            pltpu.VMEM((2, shards, 8, tok_rows), F32),
            pltpu.SemaphoreType.DMA((2, 2, shards)),
            pltpu.VMEM((shards, tok_rows, share), BF16),
            pltpu.SemaphoreType.DMA((2, 2, lines, blocks)),
            pltpu.VMEM((tok_rows, share), F32),
            pltpu.VMEM((heads_here, TILE, SPAN), F32),
            pltpu.VMEM((SEQ_LEN, width_here), F32),
            pltpu.VMEM((SEQ_LEN, width_here), F32),
            pltpu.VMEM((3, tok_rows, width_here), BF16),
            pltpu.VMEM((shards, tok_rows, share), BF16),
            pltpu.VMEM((lines, tok_rows, share), BF16),
            pltpu.VMEM((lines, tok_rows, share), BF16),
            pltpu.VMEM((lines, tok_rows, share), BF16),
            pltpu.SemaphoreType.DMA((2, 2, lines, 2)),
            pltpu.VMEM((pieces, model_width, width_here), BF16),
            pltpu.VMEM((pieces, model_width, width_here), BF16),
            pltpu.VMEM((pieces, y_size, model_width // y_size, width_here), BF16),
            pltpu.VMEM((pieces, model_width // y_size, width_here), BF16),
            pltpu.VMEM((pieces, z_size, model_width // groups, width_here), BF16),
            pltpu.SemaphoreType.DMA((2, 2, pieces, y_size)),
            pltpu.SemaphoreType.DMA((2, 2, pieces, z_size)),
            pltpu.SemaphoreType.DMA((pieces,)),
            pltpu.VMEM((1, extra_rows, share), F32),
            pltpu.VMEM((groups, extra_rows, share), F32),
            pltpu.SemaphoreType.DMA((2, groups)),
            pltpu.SemaphoreType.DMA((2, shards)),
        ],
        compiler_params=pltpu.CompilerParams(
            vmem_limit_bytes=50 * 1024 * 1024, collective_id=3, has_side_effects=True
        ),
        name="dense_backward",
    )(
        normed_two_grad,
        after_mine,
        out_grad,
        mine(inputs),
        jnp.concatenate([scale_one, scale_two], axis=1),
        mine(jnp.stack([gain_attn, gain_moe])),
        extras,
        onehot_offsets.astype(BF16),
        attended,
        w_out,
        projected,
        probs,
        normed_low,
        w_qkv,
    )
    loss = jnp.sum(extras[:, experts + 2]) / (2.0 * valid_total * model_width)
    whole = jnp.swapaxes(extras, 0, 1).reshape(extra_rows, model_width)
    table_rows = lax.dynamic_index_in_dim(extras, lax.axis_index("tensor"), 0, keepdims=False)
    table_sum = table_rows[experts + 4 : experts + 4 + heads_here, :BUCKETS].T
    out_proj_sum = jnp.swapaxes(dense[0].reshape(shards, width_here, width_here), 0, 1)
    return (
        block_out,
        loss,
        input_grad,
        whole[experts],
        dense[1:].astype(F32),
        out_proj_sum.reshape(width_here, model_width).astype(F32),
        table_sum,
        whole[experts + 1],
        whole[:experts].T,
        gate_up_grad,
        down_grad,
    )


def solution(mesh):
    placed = (
        P("dp", None),
        P("dp", None),
        P("dp"),
        P("dp", None),
        P("dp", None),
        P(),
        P(None, None, "tensor"),
        P("tensor", None),
        P(None, "tensor"),
        P(),
        P(),
        P("dp", None, None, "tensor"),
        P("dp", "tensor", None),
    )
    return jax.shard_map(
        body,
        mesh=mesh,
        in_specs=placed,
        out_specs=(
            P("dp", "tensor"),
            P(),
            P("dp", "tensor"),
            P(),
            P(None, None, "tensor"),
            P("tensor", None),
            P(None, "tensor"),
            P(),
            P(),
            P("dp", None, None, "tensor"),
            P("dp", "tensor", None),
        ),
        check_vma=False,
    )
```

```python
import functools
import math

import jax
import jax.numpy as jnp
from jax import lax
from jax.experimental import pallas as pl
from jax.experimental.pallas import tpu as pltpu
from jax.sharding import PartitionSpec as P

BUCKETS = 32
SEQ_LEN = 512
TILE = 128
SPAN = 2 * SEQ_LEN

EPSILON = 1e-06
FAR_STEPS = (12, 16, 23, 32, 46, 64, 91)
MASKED = -1000000000.0
F32 = jnp.float32
BF16 = jnp.bfloat16


def offset_bucket(offset):
    direction = jnp.where(offset > 0, 16, 0).astype(jnp.int32)
    distance = jnp.abs(offset)
    farther = jnp.full(offset.shape, 8, jnp.int32)
    for threshold in FAR_STEPS:
        farther = farther + (distance >= threshold).astype(jnp.int32)
    return direction + jnp.where(distance < 8, distance, farther)


def bucket_onehot(offsets):
    bucket_range = jnp.arange(BUCKETS, dtype=jnp.int32)
    return (offset_bucket(offsets)[:, None] == bucket_range[None, :]).astype(F32)


def dot(a, b, dims=((1,), (0,))):
    return lax.dot_general(a, b, (dims, ((), ())), preferred_element_type=F32)


SMEM = pl.BlockSpec(memory_space=pltpu.SMEM)


def staged_call(body, kinds, arrays, out_types, out_kinds, scratch, limit, collective, name):
    staged_in = [n for n, kind in enumerate(kinds) if kind == "v"]
    staged_out = [n for n, kind in enumerate(out_kinds) if kind == "v"]

    def kernel(*refs):
        ins, outs = list(refs[: len(kinds)]), list(refs[len(kinds) : len(kinds) + len(out_kinds)])
        rest = list(refs[len(kinds) + len(out_kinds) :])
        in_sems, out_sems = rest[:2]
        in_bufs = rest[2 : 2 + len(staged_in)]
        out_bufs = rest[2 + len(staged_in) : 2 + len(staged_in) + len(staged_out)]
        rest = rest[2 + len(staged_in) + len(staged_out) :]
        loads = []
        for m, n in enumerate(staged_in):
            loads.append(pltpu.make_async_copy(ins[n], in_bufs[m], in_sems.at[m]))
            ins[n] = in_bufs[m]
        for load in loads:
            load.start()
        results = []
        for m, n in enumerate(staged_out):
            results.append((out_bufs[m], outs[n], out_sems.at[m]))
            outs[n] = out_bufs[m]

        def ready():
            for load in loads:
                load.wait()

        body(ready, *ins, *outs, *rest)
        copies = [pltpu.make_async_copy(*result) for result in results]
        for copy in copies:
            copy.start()
        for copy in copies:
            copy.wait()

    return pl.pallas_call(
        kernel,
        out_shape=tuple(out_types),
        in_specs=[SMEM if kind == "s" else ANY for kind in kinds],
        out_specs=tuple(ANY for _ in out_kinds),
        scratch_shapes=[
            pltpu.SemaphoreType.DMA((max(len(staged_in), 1),)),
            pltpu.SemaphoreType.DMA((max(len(staged_out), 1),)),
        ]
        + [pltpu.VMEM(arrays[n].shape, arrays[n].dtype) for n in staged_in]
        + [pltpu.VMEM(out_types[n].shape, out_types[n].dtype) for n in staged_out]
        + scratch,
        compiler_params=pltpu.CompilerParams(
            vmem_limit_bytes=limit * 1024 * 1024, collective_id=collective, has_side_effects=True
        ),
        name=name,
    )(*arrays)


MESH_ID = pl.DeviceIdType.MESH
ANY = pl.BlockSpec(memory_space=pltpu.HBM)


def weight_grads(shards, rows, grads, side, hidden, gate_up_out, down_out):
    step = pl.program_id(1)
    share = rows.shape[-1]

    @pl.when(step < 2)
    def _():
        for s in range(shards):
            gate_up_out[:, s * share : (s + 1) * share] = dot(side[...], rows[s], ((0,), (0,)))

    @pl.when(step == 2)
    def _():
        for s in range(shards):
            down_out[:, s * share : (s + 1) * share] = dot(hidden[...], grads[s], ((0,), (0,)))


def to_row(column):
    rows = column.shape[0]
    return jnp.transpose(jnp.broadcast_to(column, (rows, 128)))[:8]


def to_column(row):
    return jnp.transpose(jnp.broadcast_to(row[:1], (128, row.shape[1])))[:, :1]


def flip(value, mask, size):
    total, unit = 0, 1
    while unit < size:
        bit = lax.rem(lax.div(value, unit), 2)
        total = total + unit * ((1 - bit) if mask & unit else bit)
        unit *= 2
    return total


def plan(groups, chunk):
    kinds = ("spread", "relay", "products", "along", "give", "taken")
    steps = []
    for step in range(groups // chunk + len(kinds) - 1):
        for lag, kind in enumerate(kinds):
            k = step - lag
            if 0 <= k < groups // chunk:
                steps += [(kind, k)] if kind == "products" else [(kind, k * chunk + n) for n in range(chunk)]
    return steps


class Mover:
    def __init__(self, groups, shards, cap, chunk, rows, part, scratch):
        self.groups, self.lines, self.cap, self.chunk = groups, shards // 2, cap, chunk
        self.rows, self.part = rows, part
        (
            self.source, self.mate_in, self.line_out, self.line_in, self.back_out, self.back,
            self.dp_sems, self.row_sems, self.sum_sems,
        ) = scratch
        self.me, self.place = lax.axis_index("dp"), lax.axis_index("tensor")
        self.line, self.core = lax.div(self.place, 2), lax.rem(self.place, 2)
        self.steps = groups // chunk

    def peer(self, i):
        return flip(self.me, i, self.groups)

    def shard(self, offset, core):
        return lax.rem(self.line + offset, self.lines) * 2 + core

    def near(self, i):
        return lax.rem(self.place + i, 2 * self.lines)

    def remote(self, src, dst, sems, index, device):
        return pltpu.make_async_remote_copy(
            src_ref=src, dst_ref=dst, send_sem=sems.at[(0, *index)], recv_sem=sems.at[(1, *index)],
            device_id=device, device_id_type=MESH_ID,
        )

    def mate(self):
        return {"tensor": self.shard(0, 1 - self.core)}

    def landed(self, where, sems, index):
        self.remote(where, where, sems, index, self.mate()).wait_recv()

    def here(self, shard, i):
        return self.rows.at[shard, :, pl.ds(i * self.cap, self.cap), :]

    def send(self, i, block):
        block = block.reshape(-1, self.cap, block.shape[-1])
        if i == 0:
            self.rows[self.place, :, : self.cap, :] = block
        else:
            self.source[i] = block
            self.out_copy(i).start()

    def out_copy(self, i):
        return self.remote(
            self.source.at[i], self.here(self.place, i), self.dp_sems.at[0], (i,), {"dp": self.peer(i)}
        )

    def line_copy(self, d, i):
        return self.remote(
            self.here(self.place, i), self.here(self.place, i), self.row_sems.at[0], (d, i),
            {"tensor": self.shard(d, self.core)},
        )

    def mate_copy(self, d, i):
        shard = self.shard(self.lines - d, self.core)
        return self.remote(self.here(shard, i), self.here(shard, i), self.row_sems.at[1], (d, i), self.mate())

    def places(self, k):
        return range(k * self.chunk, (k + 1) * self.chunk)

    def spread(self, i):
        if i:
            self.landed(self.here(self.place, i), self.dp_sems.at[0], (i,))
        for d in range(1, self.lines):
            self.line_copy(d, i).start()
        self.mate_copy(0, i).start()

    def relay(self, i):
        for d in range(1, self.lines):
            shard = self.shard(self.lines - d, self.core)
            self.landed(self.here(shard, i), self.row_sems.at[0], (d, i))
            self.mate_copy(d, i).start()

    def collect(self, i):
        for d in range(self.lines):
            shard = self.shard(self.lines - d, 1 - self.core)
            self.landed(self.here(shard, i), self.row_sems.at[1], (d, i))

    def span(self, k):
        return pl.ds(k * self.chunk * self.cap, self.chunk * self.cap)

    def block(self, i):
        return pl.ds(i * self.cap, self.cap)

    def pair_copy(self, d, i):
        shard = self.shard(d, 1 - self.core)
        return self.remote(
            self.part.at[shard, :, self.block(i), :], self.mate_in.at[d, :, self.block(i), :], self.sum_sems.at[0], (d, i),
            self.mate(),
        )

    def sum_copy(self, d, i):
        return self.remote(
            self.line_out.at[d - 1, :, self.block(i), :], self.line_in.at[d - 1, :, self.block(i), :],
            self.sum_sems.at[1], (d, i), {"tensor": self.shard(d, self.core)},
        )

    def back_copy(self, i):
        return self.remote(
            self.back_out.at[:, self.block(i), :], self.back.at[i], self.dp_sems.at[1], (i,), {"dp": self.peer(i)}
        )

    def pair(self, k):
        for i in self.places(k):
            for d in range(self.lines):
                self.pair_copy(d, i).start()

    def pair_sum(self, d, i):
        shard = self.shard(d, self.core)
        return self.part[shard, :, self.block(i), :].astype(F32) + self.mate_in[d, :, self.block(i), :].astype(F32)

    def along(self, i):
        for d in range(self.lines):
            self.landed(self.mate_in.at[d, :, self.block(i), :], self.sum_sems.at[0], (d, i))
        for d in range(1, self.lines):
            self.line_out[d - 1, :, self.block(i), :] = self.pair_sum(d, i).astype(BF16)
            self.sum_copy(d, i).start()

    def give(self, i):
        total = self.pair_sum(0, i)
        for d in range(1, self.lines):
            self.landed(self.line_in.at[d - 1, :, self.block(i), :], self.sum_sems.at[1], (d, i))
            total = total + self.line_in[d - 1, :, self.block(i), :].astype(F32)
        total = total.astype(BF16)
        if i == 0:
            self.back[0] = total
        else:
            self.back_out[:, self.block(i), :] = total
            self.back_copy(i).start()

    def arrived(self, i):
        if i:
            self.landed(self.back.at[i], self.dp_sems.at[1], (i,))
        return self.back[i].reshape(-1, self.back.shape[-1])

    def run(self, compute, take):
        def products(k):
            for i in self.places(k):
                self.collect(i)
            compute(k)
            self.pair(k)

        def taken(i):
            take(i, self.arrived(i))

        works = dict(
            spread=self.spread, relay=self.relay, products=products, along=self.along, give=self.give, taken=taken
        )
        for work, index in plan(self.groups, self.chunk):
            works[work](index)

    def finish(self):
        for i in range(1, self.groups):
            self.out_copy(i).wait_send()
            self.back_copy(i).wait_send()
        for i in range(self.groups):
            for d in range(self.lines):
                if d:
                    self.line_copy(d, i).wait_send()
                    self.sum_copy(d, i).wait_send()
                self.mate_copy(d, i).wait_send()
                self.pair_copy(d, i).wait_send()


def mover_scratch(groups, shards, local, cap, share):
    lines, slots = shards // 2, groups * cap
    return [
        pltpu.VMEM((groups, local, cap, share), BF16),
        pltpu.VMEM((lines, local, slots, share), BF16),
        pltpu.VMEM((lines - 1, local, slots, share), BF16),
        pltpu.VMEM((lines - 1, local, slots, share), BF16),
        pltpu.VMEM((local, slots, share), BF16),
        pltpu.VMEM((groups, local, cap, share), BF16),
        pltpu.SemaphoreType.DMA((2, 2, groups)),
        pltpu.SemaphoreType.DMA((2, 2, lines, groups)),
        pltpu.SemaphoreType.DMA((2, 2, lines, groups)),
    ]


MOVER_REFS = 9
ROOT = math.sqrt(2.0 / math.pi)


def gelu_parts(v):
    inner = jnp.tanh(ROOT * (v + 0.044715 * (v * v * v)))
    half = 0.5 * (1.0 + inner)
    slope = half + 0.5 * v * (1.0 - inner * inner) * (ROOT * (1.0 + 3.0 * 0.044715 * v * v))
    return v * half, slope


def experts_both(
    groups, shards, local, cap, chunk, experts,
    ready, len_ref, normed, after, columns, target_ref, ids_ref, router,
    teacher_hbm, gate_up_hbm, down_hbm,
    block_out, out_grad, norm_grad, extras, info,
    rows_hbm, grads_hbm, side_hbm, hidden_hbm,
    teacher, gate_up, down, rows, grads, part, pre, hidden, side, routed, gated, load_sems, save_sems,
    counts, count_sems, dots, dot_sems, *scratch,
):
    ahead = Mover(groups, shards, cap, chunk, rows, part, scratch[:MOVER_REFS])
    behind = Mover(groups, shards, cap, chunk, grads, part, scratch[MOVER_REFS:])
    tokens, share = normed.shape
    width = local * cap
    place = ahead.place
    mine = pl.ds(pl.multiple_of(place * share, 128), share)
    loads = [
        pltpu.make_async_copy(gate_up_hbm, gate_up, load_sems.at[0]),
        pltpu.make_async_copy(down_hbm, down, load_sems.at[1]),
        pltpu.make_async_copy(teacher_hbm.at[:, mine], teacher, load_sems.at[2]),
    ]
    for load in loads:
        load.start()

    barrier = pltpu.get_barrier_semaphore()
    for i in range(1, groups):
        pl.semaphore_signal(barrier, inc=1, device_id={"dp": ahead.peer(i)}, device_id_type=MESH_ID)
    for i in range(1, shards):
        pl.semaphore_signal(barrier, inc=1, device_id={"tensor": ahead.near(i)}, device_id_type=MESH_ID)
    counts[0] = jnp.full((8, 128), len_ref[0], jnp.int32)
    slot_lines = lax.broadcasted_iota(jnp.int32, (width, tokens), 0)
    slot_lanes = lax.broadcasted_iota(jnp.int32, (tokens, width), 1)
    ready()
    row_targets = [target_ref[n : n + 1, :] for n in range(2)]
    column_targets = [to_column(target_ref[n : n + 1, :].astype(F32)).astype(jnp.int32) for n in range(2)]

    def by_slot(i, n):
        return slot_lines + ahead.peer(i) * width == row_targets[n]

    def by_token(i, n):
        return slot_lanes + ahead.peer(i) * width == column_targets[n]

    def ones(mask):
        return jnp.where(mask, 1.0, 0.0).astype(BF16)

    pl.semaphore_wait(barrier, groups + shards - 2)

    def count_copy(i):
        return ahead.remote(counts.at[0], counts.at[i], count_sems, (i,), {"dp": ahead.peer(i)})

    order = [*range(1, groups), 0]
    for i in order:
        ahead.send(i, dot(ones(by_slot(i, 0) | by_slot(i, 1)), normed[...]).astype(BF16))
    for i in range(1, groups):
        count_copy(i).start()

    def forward_saves(k):
        span = ahead.span(k)
        return [
            pltpu.make_async_copy(rows.at[:, :, span, :], rows_hbm.at[:, :, span, :], save_sems.at[0, k]),
            pltpu.make_async_copy(hidden.at[:, span, :], hidden_hbm.at[:, span, :], save_sems.at[1, k]),
        ]

    def backward_saves(k):
        span = ahead.span(k)
        return [
            pltpu.make_async_copy(grads.at[:, :, span, :], grads_hbm.at[:, :, span, :], save_sems.at[2, k]),
            pltpu.make_async_copy(side.at[:, :, span, :], side_hbm.at[:, :, span, :], save_sems.at[3, k]),
        ]

    def put(e, span, result):
        result = result.astype(BF16)
        for s in range(shards):
            part[s, e, span, :] = result[:, s * share : (s + 1) * share]

    def forward(k):
        span = ahead.span(k)
        if k == 0:
            loads[0].wait()
            loads[1].wait()
        for e in range(local):
            lhs = jnp.concatenate([rows[s, e, span, :] for s in range(shards)], axis=1)
            gate = dot(lhs, gate_up[e, 0], ((1,), (1,)))
            up = dot(lhs, gate_up[e, 1], ((1,), (1,)))
            pre[0, e, span, :] = gate
            pre[1, e, span, :] = up
            low = (gelu_parts(gate)[0] * up).astype(BF16)
            hidden[e, span, :] = low
            put(e, span, dot(low, down[e]))
        for save in forward_saves(k):
            save.start()

    def take(i, block):
        for n in range(2):
            value = dot(ones(by_token(i, n)), block)
            if i == 0:
                routed[n] = value
            else:
                routed[n] += value

    ahead.run(forward, take)

    tally = counts[0]
    for i in range(1, groups):
        count_copy(i).wait()
        tally = tally + counts[i]
    valid = tally.astype(F32)
    loads[2].wait()
    gates = [columns[:, 2:3], columns[:, 3:4]]
    output = after[...] + gates[0] * routed[0] + gates[1] * routed[1]
    block_out[...] = output
    alive = lax.broadcasted_iota(jnp.int32, (tokens, share), 0) < len_ref[0]
    deviation = jnp.where(alive, output - teacher[...].astype(F32), 0.0)
    scaled = deviation * (groups * tokens / valid[0:1, 0:1])
    out_grad[...] = scaled
    for n in range(2):
        gated[n * tokens : (n + 1) * tokens, :] = (gates[n] * scaled).astype(BF16)
    for i in order:
        both = jnp.concatenate([ones(by_slot(i, 0)), ones(by_slot(i, 1))], axis=1)
        behind.send(i, dot(both, gated[...]).astype(BF16))
    for n in range(2):
        dots[n, 0] = to_row(jnp.sum(routed[n] * scaled, axis=1, keepdims=True))

    def dot_copy(n, i):
        return ahead.remote(dots.at[n, 0], dots.at[n, i], dot_sems, (n, i), {"tensor": ahead.near(i)})

    for n in range(2):
        for i in range(1, shards):
            dot_copy(n, i).start()
    info[...] = valid
    extras[...] = jnp.zeros_like(extras)
    extras[experts + 2 : experts + 3, :] = jnp.sum(deviation * deviation, axis=0, keepdims=True)
    ahead.finish()

    def route_grads():
        parts = []
        for n in range(2):
            total = dots[n, 0]
            for i in range(1, shards):
                dot_copy(n, i).wait()
                total = total + dots[n, i]
            parts.append(to_column(total))
        expert_probs = columns[:, 16 : 16 + experts]
        lanes = lax.broadcasted_iota(jnp.int32, (tokens, experts), 1)
        picks = [
            jnp.where(lanes == to_column(ids_ref[n : n + 1, :].astype(F32)).astype(jnp.int32), 1.0, 0.0)
            for n in range(2)
        ]
        chosen_total = jnp.sum(expert_probs * (picks[0] + picks[1]), axis=1, keepdims=True)
        along = parts[0] * gates[0] + parts[1] * gates[1]
        probs_grad = sum(picks[n] * ((parts[n] - along) / chosen_total) for n in range(2))
        logit_grad = expert_probs * (probs_grad - jnp.sum(probs_grad * expert_probs, axis=1, keepdims=True))
        logit_grad = logit_grad.astype(BF16)
        extras[0:experts, :] = dot(logit_grad, normed[...], ((0,), (0,)))
        norm_grad[...] = dot(logit_grad, router[:, mine])

    def backward(k):
        span = ahead.span(k)
        for e in range(local):
            lhs = jnp.concatenate([grads[s, e, span, :] for s in range(shards)], axis=1)
            hidden_grad = dot(lhs, down[e], ((1,), (1,)))
            activated, slope = gelu_parts(pre[0, e, span, :])
            gate_side = (hidden_grad * pre[1, e, span, :] * slope).astype(BF16)
            up_side = (hidden_grad * activated).astype(BF16)
            side[0, e, span, :] = gate_side
            side[1, e, span, :] = up_side
            put(e, span, dot(gate_side, gate_up[e, 0]) + dot(up_side, gate_up[e, 1]))
        for save in backward_saves(k):
            save.start()
        if k == 0:
            route_grads()

    def take_back(i, block):
        norm_grad[...] += dot(ones(by_token(i, 0) | by_token(i, 1)), block)

    behind.run(backward, take_back)
    behind.finish()
    for k in range(ahead.steps):
        for save in forward_saves(k) + backward_saves(k):
            save.wait()


def gate_columns(logits, first, second):
    lanes = lax.broadcasted_iota(jnp.int32, logits.shape, 1)
    exponent = jnp.exp(logits - jnp.max(logits, axis=1, keepdims=True))
    expert_probs = exponent / jnp.sum(exponent, axis=1, keepdims=True)
    chosen = [jnp.sum(jnp.where(lanes == pick, expert_probs, 0.0), axis=1, keepdims=True) for pick in (first, second)]
    total = chosen[0] + chosen[1]
    return expert_probs, chosen[0] / total, chosen[1] / total


def dense_forward(
    groups, shards, heads, width, experts,
    ready, len_ref, bias_ref, ids_ref, gain_one, gain_two, router_ref,
    inputs_hbm, w_qkv_hbm, w_out_hbm,
    normed_out, proj_out, probs_out, attended_out, after_out, normed_two_out, columns_out,
    inputs, w_qkv, load_sems, w_out, w_sems, attended, attended_sems, skew, normed, proj, probs, after, normed_two, save_sems,
):
    tokens, model = inputs.shape
    here = heads * width
    share = model // shards
    lines = shards // 2
    blocks = tokens // TILE
    place = lax.axis_index("tensor")
    line, core = lax.div(place, 2), lax.rem(place, 2)
    mate = {"tensor": line * 2 + 1 - core}

    def shard(d, c):
        return lax.rem(line + d, lines) * 2 + c

    def remote(src, dst, sems, index, device):
        return pltpu.make_async_remote_copy(
            src_ref=src, dst_ref=dst, send_sem=sems.at[(0, *index)], recv_sem=sems.at[(1, *index)],
            device_id=device, device_id_type=MESH_ID,
        )

    def landed(where, sems, index):
        remote(where, where, sems, index, mate).wait_recv()

    loads = [
        pltpu.make_async_copy(inputs_hbm, inputs, load_sems.at[0]),
        pltpu.make_async_copy(w_qkv_hbm, w_qkv, load_sems.at[1]),
        pltpu.make_async_copy(w_out_hbm, w_out.at[place], load_sems.at[2]),
    ]
    for load in loads:
        load.start()
    barrier = pltpu.get_barrier_semaphore()
    for d in range(1, lines):
        pl.semaphore_signal(barrier, inc=1, device_id={"tensor": shard(d, core)}, device_id_type=MESH_ID)
    pl.semaphore_signal(barrier, inc=1, device_id=mate, device_id_type=MESH_ID)
    pl.semaphore_wait(barrier, lines)

    def w_line(d):
        return remote(w_out.at[place], w_out.at[place], w_sems.at[0], (d,), {"tensor": shard(d, core)})

    def w_mate(d):
        where = w_out.at[shard(lines - d, core)]
        return remote(where, where, w_sems.at[1], (d,), mate)

    def row_block(j):
        return pl.ds(j * TILE, TILE)

    def rows_line(d, j):
        where = attended.at[place, row_block(j), :]
        return remote(where, where, attended_sems.at[0], (d, j), {"tensor": shard(d, core)})

    def rows_mate(d, j):
        where = attended.at[shard(lines - d, core), row_block(j), :]
        return remote(where, where, attended_sems.at[1], (d, j), mate)

    ready()
    loads[2].wait()
    for d in range(1, lines):
        w_line(d).start()
    w_mate(0).start()

    loads[0].wait()
    for j in range(blocks):
        rows = slice(j * TILE, (j + 1) * TILE)
        values = inputs[rows, :].astype(F32)
        scale = lax.rsqrt(jnp.mean(values * values, axis=1, keepdims=True) + EPSILON)
        columns_out[rows, 0:1] = scale
        normed[rows, :] = (values * scale * gain_one[...]).astype(BF16)
    loads[1].wait()
    for n in range(3):
        proj[n] = dot(normed[...], w_qkv[n]).astype(BF16)
    saves = [
        pltpu.make_async_copy(normed, normed_out, save_sems.at[0]),
        pltpu.make_async_copy(proj, proj_out, save_sems.at[1]),
    ]
    for h in range(heads):
        skew[h] = pltpu.roll(
            jnp.broadcast_to(bias_ref[h : h + 1, :], (TILE, SPAN)), 0, 1, stride=1, stride_axis=0
        )
    for item in saves:
        item.start()

    alive = lax.broadcasted_iota(jnp.int32, (TILE, SEQ_LEN), 1) < len_ref[0]
    for j in range(blocks):
        rows = slice(j * TILE, (j + 1) * TILE)
        start = SEQ_LEN - j * TILE
        for h in range(heads):
            cols = slice(h * width, (h + 1) * width)
            scores = dot(proj[0, rows, cols], proj[1, :, cols], ((1,), (1,)))
            scores = jnp.where(alive, scores + skew[h, :, start : start + SEQ_LEN], MASKED)
            exponent = jnp.exp(scores - jnp.max(scores, axis=1, keepdims=True))
            weights = exponent * (1.0 / jnp.sum(exponent, axis=1, keepdims=True))
            probs[h, rows, :] = weights
            attended[place, rows, cols] = dot(weights.astype(BF16), proj[2, :, cols]).astype(BF16)
        for d in range(1, lines):
            rows_line(d, j).start()
        rows_mate(0, j).start()
        if j == blocks - 2:
            for d in range(1, lines):
                landed(w_out.at[shard(lines - d, core)], w_sems.at[0], (d,))
                w_mate(d).start()
    saves += [
        pltpu.make_async_copy(probs, probs_out, save_sems.at[2]),
        pltpu.make_async_copy(attended.at[place], attended_out, save_sems.at[3]),
    ]
    for item in saves[2:]:
        item.start()

    ids = ids_ref[...].astype(F32)
    picks = [to_column(ids[n : n + 1]).astype(jnp.int32) for n in range(2)]

    def relay(j):
        for d in range(1, lines):
            landed(attended.at[shard(lines - d, core), row_block(j), :], attended_sems.at[0], (d, j))
            rows_mate(d, j).start()

    relay(0)
    for d in range(lines):
        landed(w_out.at[shard(lines - d, 1 - core)], w_sems.at[1], (d,))
    for j in range(blocks):
        rows = slice(j * TILE, (j + 1) * TILE)
        if j + 1 < blocks:
            relay(j + 1)
        for d in range(lines):
            landed(attended.at[shard(lines - d, 1 - core), row_block(j), :], attended_sems.at[1], (d, j))
        total = inputs[rows, :].astype(F32)
        for s in range(shards):
            total = total + dot(attended[s, rows, :], w_out[s])
        scale = lax.rsqrt(jnp.mean(total * total, axis=1, keepdims=True) + EPSILON)
        low = (total * scale * gain_two[...]).astype(BF16)
        after[...] = total
        normed_two[...] = low
        mine = pl.ds(pl.multiple_of(place * share, 128), share)
        after_out[rows, :] = after[:, mine]
        normed_two_out[rows, :] = normed_two[:, mine]
        expert_probs, first, second = gate_columns(
            dot(low, router_ref[...], ((1,), (1,))), picks[0][rows], picks[1][rows]
        )
        columns_out[rows, 1:2] = scale
        columns_out[rows, 2:3] = first
        columns_out[rows, 3:4] = second
        columns_out[rows, 16 : 16 + experts] = expert_probs
    for d in range(lines):
        if d:
            w_line(d).wait_send()
        w_mate(d).wait_send()
        for j in range(blocks):
            if d:
                rows_line(d, j).wait_send()
            rows_mate(d, j).wait_send()
    for item in saves:
        item.wait()


def dense_backward(
    groups, shards, heads, width, experts,
    ready, norm_grad, after, out_grad, scales, gain_one, gain_two, extras_in, onehot,
    inputs_hbm, attended_hbm, w_out_hbm, proj_hbm, probs_hbm, normed_hbm, w_qkv_hbm,
    dense_out, out_proj_out, input_grad, extras_out,
    residual, attended, w_out, proj, probs, normed, w_qkv, load_sems,
    dots, dot_sems, branch, branch_sems, grad_here, diag, key_acc, value_acc, proj_grad,
    part, mate_in, line_out, line_in, part_sems,
    dense, result, y_in, y_sum, half_in, half_sum, block_in, dense_sems, z_sems, save_sems,
    extras, extras_in_dp, extras_sems, extras_ring_sems,
):
    model = normed.shape[1]
    share = branch.shape[-1]
    tokens = branch.shape[1]
    here = heads * width
    lines = shards // 2
    y_size = 1 << ((groups.bit_length() - 1) // 2)
    z_size = groups // y_size
    pieces = dense.shape[0]
    me, place = lax.axis_index("dp"), lax.axis_index("tensor")
    line, core = lax.div(place, 2), lax.rem(place, 2)
    z, y = lax.div(me, y_size), lax.rem(me, y_size)
    mate = {"tensor": line * 2 + 1 - core}
    inverse = 1.0 / model
    mine = pl.ds(pl.multiple_of(place * share, 128), share)

    def group(i):
        return lax.rem(me + i, groups)

    def shard(d, c):
        return lax.rem(line + d, lines) * 2 + c

    def near(i):
        return lax.rem(place + i, shards)

    def remote(src, dst, sems, index, device):
        return pltpu.make_async_remote_copy(
            src_ref=src, dst_ref=dst, send_sem=sems.at[(0, *index)], recv_sem=sems.at[(1, *index)],
            device_id=device, device_id_type=MESH_ID,
        )

    def landed(where, sems, index):
        remote(where, where, sems, index, mate).wait_recv()

    loads = [
        pltpu.make_async_copy(src, dst, load_sems.at[n])
        for n, (src, dst) in enumerate(
            (
                (w_out_hbm, w_out), (attended_hbm, attended), (proj_hbm, proj), (probs_hbm, probs),
                (w_qkv_hbm, w_qkv), (normed_hbm, normed), (inputs_hbm.at[:, mine], residual),
            )
        )
    ]
    for load in loads:
        load.start()

    barrier = pltpu.get_barrier_semaphore()
    for i in range(1, groups):
        pl.semaphore_signal(barrier, inc=1, device_id={"dp": group(i)}, device_id_type=MESH_ID)
    for i in range(1, shards):
        pl.semaphore_signal(barrier, inc=1, device_id={"tensor": near(i)}, device_id_type=MESH_ID)
    def dot_copy(n, i):
        return remote(dots.at[n, 0], dots.at[n, i], dot_sems, (n, i), {"tensor": near(i)})

    def dot_send(n, column):
        dots[n, 0] = to_row(column)
        if n == 0:
            pl.semaphore_wait(barrier, groups + shards - 2)
        for i in range(1, shards):
            dot_copy(n, i).start()

    def dot_sum(n):
        total = dots[n, 0]
        for i in range(1, shards):
            dot_copy(n, i).wait()
            total = total + dots[n, i]
        return to_column(total)

    ready()
    scale_two = scales[:, 1:2]
    weighted = norm_grad[...] * gain_two[:, mine]
    dot_send(0, jnp.sum(weighted * after[...], axis=1, keepdims=True))
    extras[0] = extras_in[...]
    extras[0, experts + 1 : experts + 2, :] = jnp.sum(norm_grad[...] * after[...] * scale_two, axis=0, keepdims=True)
    along = dot_sum(0)
    after_grad = out_grad[...] + scale_two * (weighted - after[...] * (scale_two * scale_two * along * inverse))
    grad_here[...] = after_grad
    branch[place] = after_grad.astype(BF16)

    blocks = tokens // TILE

    def row_block(j):
        return pl.ds(j * TILE, TILE)

    def branch_line(d, j):
        where = branch.at[place, row_block(j), :]
        return remote(where, where, branch_sems.at[0], (d, j), {"tensor": shard(d, core)})

    def branch_mate(d, j):
        where = branch.at[shard(lines - d, core), row_block(j), :]
        return remote(where, where, branch_sems.at[1], (d, j), mate)

    for j in range(blocks):
        for d in range(1, lines):
            branch_line(d, j).start()
        branch_mate(0, j).start()
    for j in range(blocks):
        for d in range(1, lines):
            landed(branch.at[shard(lines - d, core), row_block(j), :], branch_sems.at[0], (d, j))
            branch_mate(d, j).start()
    def branch_landed(j):
        for d in range(lines):
            landed(branch.at[shard(lines - d, 1 - core), row_block(j), :], branch_sems.at[1], (d, j))

    rows_here = dense.shape[1]
    y_rows, z_rows = rows_here // y_size, rows_here // groups

    def y_copy(p, a):
        to = lax.rem(y + a, y_size)
        return remote(
            dense.at[p, pl.ds(to * y_rows, y_rows), :], y_in.at[p, a], dense_sems.at[0], (p, a), {"dp": z * y_size + to}
        )

    z_low, z_high = lax.rem(z, 2), lax.div(z, 2)
    half_rows = y_rows // 2
    kept_half, kept_block = y * y_rows + z_low * half_rows, y * y_rows + z_low * half_rows + z_high * z_rows
    near_z = {"dp": (z_high * 2 + 1 - z_low) * y_size + y}
    far_z = {"dp": ((1 - z_high) * 2 + z_low) * y_size + y}

    def half_copy(p):
        return remote(
            y_sum.at[p, pl.ds((1 - z_low) * half_rows, half_rows), :], half_in.at[p], z_sems.at[0], (p, 0), near_z
        )

    def block_copy(p):
        return remote(
            half_sum.at[p, pl.ds((1 - z_high) * z_rows, z_rows), :], block_in.at[p], z_sems.at[0], (p, 1), far_z
        )

    def block_spread(p):
        where = result.at[p, pl.ds(kept_block, z_rows), :]
        return remote(where, where, z_sems.at[1], (p, 1), far_z)

    def half_spread(p):
        where = result.at[p, pl.ds(kept_half, half_rows), :]
        return remote(where, where, z_sems.at[1], (p, 0), near_z)

    def y_spread(p, a):
        to = lax.rem(y + a, y_size)
        where = result.at[p, pl.ds(y * y_rows, y_rows), :]
        return remote(where, where, dense_sems.at[1], (p, a), {"dp": z * y_size + to})

    def reduce_start(p):
        for a in range(1, y_size):
            y_copy(p, a).start()

    def reduce_y(p):
        total = dense[p, pl.ds(y * y_rows, y_rows), :].astype(F32)
        for a in range(1, y_size):
            landed(y_in.at[p, a], dense_sems.at[0], (p, a))
            total = total + y_in[p, a].astype(F32)
        y_sum[p] = total.astype(BF16)
        half_copy(p).start()

    def reduce_half(p):
        for a in range(1, y_size):
            y_copy(p, a).wait_send()
        landed(half_in.at[p], z_sems.at[0], (p, 0))
        mine_half = y_sum[p, pl.ds(z_low * half_rows, half_rows), :].astype(F32)
        half_sum[p] = (mine_half + half_in[p].astype(F32)).astype(BF16)
        block_copy(p).start()

    def reduce_block(p):
        landed(block_in.at[p], z_sems.at[0], (p, 1))
        mine_block = half_sum[p, pl.ds(z_high * z_rows, z_rows), :].astype(F32)
        result[p, pl.ds(kept_block, z_rows), :] = (mine_block + block_in[p].astype(F32)).astype(BF16)
        block_spread(p).start()

    def spread_block(p):
        landed(result.at[p, pl.ds(kept_half + (1 - z_high) * z_rows, z_rows), :], z_sems.at[1], (p, 1))
        half_spread(p).start()

    def spread_half(p):
        landed(result.at[p, pl.ds(y * y_rows + (1 - z_low) * half_rows, half_rows), :], z_sems.at[1], (p, 0))
        for a in range(1, y_size):
            y_spread(p, a).start()

    per_piece = shards // 2

    def save(p):
        if p >= 2:
            return [pltpu.make_async_copy(result.at[p], dense_out.at[p - 2], save_sems.at[p, 0])]
        return [
            pltpu.make_async_copy(
                result.at[p, pl.ds(n * here, here), :],
                out_proj_out.at[:, pl.ds((p * per_piece + n) * here, here)],
                save_sems.at[p, n],
            )
            for n in range(per_piece)
        ]

    def spread_y(p):
        for a in range(1, y_size):
            origin = lax.rem(y + y_size - a, y_size)
            landed(result.at[p, pl.ds(origin * y_rows, y_rows), :], dense_sems.at[1], (p, a))
        for copy in save(p):
            copy.start()

    def out_projection():
        loads[1].wait()
        for s in range(shards):
            n = s % per_piece
            dense[s // per_piece, n * here : (n + 1) * here, :] = dot(
                attended[...], branch[s], ((0,), (0,))
            ).astype(BF16)
        for p in range(2):
            reduce_start(p)

    loads[0].wait()
    loads[2].wait()
    loads[3].wait()
    diag[...] = jnp.zeros_like(diag)
    for j in range(blocks):
        rows = slice(j * TILE, (j + 1) * TILE)
        start = SEQ_LEN - j * TILE
        branch_landed(j)
        if j == blocks - 1:
            out_projection()
        wide = jnp.concatenate([branch[s, rows, :] for s in range(shards)], axis=1)
        grads = dot(wide, w_out[...], ((1,), (1,))).astype(BF16)
        for h in range(heads):
            cols = slice(h * width, (h + 1) * width)
            p = probs[h, rows, :]
            grad = grads[:, cols]
            prob_grad = dot(grad, proj[2, :, cols], ((1,), (1,)))
            score_grad = p * (prob_grad - jnp.sum(p * prob_grad, axis=1, keepdims=True))
            diag[h, :, start : start + SEQ_LEN] += score_grad
            low = score_grad.astype(BF16)
            proj_grad[0, rows, cols] = dot(low, proj[1, :, cols]).astype(BF16)
            key_part = dot(low, proj[0, rows, cols], ((0,), (0,)))
            value_part = dot(p.astype(BF16), grad, ((0,), (0,)))
            if j == 0:
                key_acc[:, cols] = key_part
                value_acc[:, cols] = value_part
            else:
                key_acc[:, cols] += key_part
                value_acc[:, cols] += value_part
    proj_grad[1] = key_acc[...].astype(BF16)
    proj_grad[2] = value_acc[...].astype(BF16)
    loads[4].wait()
    loads[5].wait()
    for p in range(2, pieces):
        half = slice((p % 2) * rows_here, (p % 2 + 1) * rows_here)
        dense[p] = dot(normed[:, half], proj_grad[p // 2 - 1], ((0,), (0,))).astype(BF16)
        reduce_start(p)
    half = tokens // 2

    def part_rows(k):
        return pl.ds(k * half, half)

    def pair_copy(d, k):
        return remote(
            part.at[shard(d, 1 - core), part_rows(k), :], mate_in.at[d, part_rows(k), :], part_sems.at[0], (d, k), mate
        )

    def line_copy(d, k):
        return remote(
            line_out.at[d, part_rows(k), :], line_in.at[d, part_rows(k), :], part_sems.at[1], (d, k),
            {"tensor": shard(d, core)},
        )

    for k in range(2):
        rows = slice(k * half, (k + 1) * half)
        total = dot(proj_grad[0, rows, :], w_qkv[0], ((1,), (1,)))
        for n in range(1, 3):
            total = total + dot(proj_grad[n, rows, :], w_qkv[n], ((1,), (1,)))
        low = total.astype(BF16)
        for s in range(shards):
            part[s, rows, :] = low[:, s * share : (s + 1) * share]
        for d in range(lines):
            pair_copy(d, k).start()
    def advance(step):
        for lag, work in enumerate((reduce_y, reduce_half, reduce_block, spread_block, spread_half)):
            if 0 <= step - lag < pieces:
                work(step - lag)

    advance(0)

    def pair_sum(d, rows):
        return part[shard(d, core), rows, :].astype(F32) + mate_in[d, rows, :].astype(F32)

    for k in range(2):
        rows = part_rows(k)
        for d in range(lines):
            landed(mate_in.at[d, rows, :], part_sems.at[0], (d, k))
        for d in range(1, lines):
            line_out[d, rows, :] = pair_sum(d, rows).astype(BF16)
            line_copy(d, k).start()
    for h in range(heads):
        total = diag[h]
        size = TILE // 2
        while size >= 1:
            total = total[:size] + pltpu.roll(total[size : 2 * size], SPAN - size, 1)
            size //= 2
        row = jnp.broadcast_to(total, (8, SPAN))
        high = row.astype(BF16)
        middle = (row - high.astype(F32)).astype(BF16)
        low = (row - high.astype(F32) - middle.astype(F32)).astype(BF16)
        table = dot(high, onehot[...]) + dot(middle, onehot[...]) + dot(low, onehot[...])
        extras[0, experts + 4 + h : experts + 5 + h, : onehot.shape[1]] = table[:1]
    for step in range(1, 4):
        advance(step)

    total = pair_sum(0, pl.ds(0, tokens))
    for k in range(2):
        for d in range(1, lines):
            landed(line_in.at[d, part_rows(k), :], part_sems.at[1], (d, k))
    for d in range(1, lines):
        total = total + line_in[d].astype(F32)
    scale_one = scales[:, 0:1]
    loads[6].wait()
    values = residual[...].astype(F32)
    weighted = total * gain_one[:, mine]
    dot_send(1, jnp.sum(weighted * values, axis=1, keepdims=True))
    extras[0, experts : experts + 1, :] = jnp.sum(total * values * scale_one, axis=0, keepdims=True)

    def extras_copy(i):
        return remote(extras.at[0], extras_in_dp.at[i], extras_sems, (i,), {"dp": group(i)})

    for i in range(1, groups):
        extras_copy(i).start()
    advance(4)
    along = dot_sum(1)
    input_grad[...] = grad_here[...] + scale_one * (weighted - values * (scale_one * scale_one * along * inverse))
    for step in range(5, pieces + 4):
        advance(step)

    summed = extras[0]
    for i in range(1, groups):
        extras_copy(i).wait()
        summed = summed + extras_in_dp[i]
    extras_out[place] = summed

    def ring_copy(i):
        return remote(extras_out.at[place], extras_out.at[place], extras_ring_sems, (i,), {"tensor": near(i)})

    for i in range(1, shards):
        ring_copy(i).start()
    for p in range(pieces):
        spread_y(p)
    for i in range(1, shards):
        landed(extras_out.at[near(shards - i)], extras_ring_sems, (i,))
        ring_copy(i).wait_send()
    for j in range(blocks):
        for d in range(lines):
            if d:
                branch_line(d, j).wait_send()
            branch_mate(d, j).wait_send()
    for k in range(2):
        for d in range(lines):
            if d:
                line_copy(d, k).wait_send()
            pair_copy(d, k).wait_send()
    for p in range(pieces):
        for copy in (half_copy(p), block_copy(p), block_spread(p), half_spread(p)):
            copy.wait_send()
        for a in range(1, y_size):
            y_spread(p, a).wait_send()
        for copy in save(p):
            copy.wait()


def body(
    inputs,
    teacher,
    lengths,
    expert_ids,
    route_slots,
    gain_attn,
    w_qkv,
    w_out,
    rel_table,
    gain_moe,
    w_router,
    w_gate_up,
    w_down,
):
    highest = lax.Precision.HIGHEST
    tok_rows, model_width = inputs.shape
    groups = lax.axis_size("dp")
    shards = lax.axis_size("tensor")
    experts = w_router.shape[1]
    local_experts = w_gate_up.shape[0]
    capacity = 10 * tok_rows // (4 * experts)
    padded_cap = (capacity + 15) // 16 * 16
    slot_count = experts * padded_cap
    heads_here = rel_table.shape[1]
    width_here = w_qkv.shape[2]
    head_width = width_here // heads_here
    share = model_width // shards

    offsets = jnp.arange(SPAN, dtype=jnp.int32) - SEQ_LEN
    onehot_offsets = bucket_onehot(offsets)
    offset_bias = jnp.dot(onehot_offsets, rel_table, precision=highest).T
    lines = shards // 2
    blocks = tok_rows // TILE
    ids = expert_ids.T
    gain_one, gain_two = gain_attn.reshape(1, model_width), gain_moe.reshape(1, model_width)
    router_t = w_router.T
    normed_low, projected, probs, attended, after_mine, normed_mine, columns = staged_call(
        functools.partial(dense_forward, groups, shards, heads_here, head_width, experts),
        "svvvvvaaa",
        (lengths, offset_bias, ids, gain_one, gain_two, router_t, inputs, w_qkv, w_out),
        (
            jax.ShapeDtypeStruct((tok_rows, model_width), BF16),
            jax.ShapeDtypeStruct((3, tok_rows, width_here), BF16),
            jax.ShapeDtypeStruct((heads_here, SEQ_LEN, SEQ_LEN), F32),
            jax.ShapeDtypeStruct((tok_rows, width_here), BF16),
            jax.ShapeDtypeStruct((tok_rows, share), F32),
            jax.ShapeDtypeStruct((tok_rows, share), BF16),
            jax.ShapeDtypeStruct((tok_rows, 128), F32),
        ),
        "aaaavvv",
        [
            pltpu.VMEM((tok_rows, model_width), BF16),
            pltpu.VMEM(w_qkv.shape, BF16),
            pltpu.SemaphoreType.DMA((3,)),
            pltpu.VMEM((shards, width_here, model_width), BF16),
            pltpu.SemaphoreType.DMA((2, 2, lines)),
            pltpu.VMEM((shards, tok_rows, width_here), BF16),
            pltpu.SemaphoreType.DMA((2, 2, lines, blocks)),
            pltpu.VMEM((heads_here, TILE, SPAN), F32),
            pltpu.VMEM((tok_rows, model_width), BF16),
            pltpu.VMEM((3, tok_rows, width_here), BF16),
            pltpu.VMEM((heads_here, SEQ_LEN, SEQ_LEN), F32),
            pltpu.VMEM((TILE, model_width), F32),
            pltpu.VMEM((TILE, model_width), BF16),
            pltpu.SemaphoreType.DMA((4,)),
        ],
        60,
        4,
        "dense_forward",
    )
    kept_route = route_slots < capacity
    target = jnp.where(kept_route, expert_ids * padded_cap + route_slots, -1).T
    gate_up_t = jnp.swapaxes(w_gate_up, 2, 3)
    chunk = max(groups // 4, 1)
    steps = groups // chunk
    slots = groups * padded_cap
    ff_here = w_down.shape[1]
    sizes = (groups, shards, local_experts, padded_cap)
    rows_shape = (shards, local_experts, slots, share)
    extra_rows = experts + 8
    token_type = jax.ShapeDtypeStruct((tok_rows, share), F32)
    block_out, out_grad, normed_two_grad, extras, info, expert_rows, expert_grad, pre_grads, hidden_low = staged_call(
        functools.partial(experts_both, *sizes, chunk, experts),
        "svvvvvvaaa",
        (lengths, normed_mine, after_mine, columns, target, ids, router_t, teacher, gate_up_t, w_down),
        (
            token_type,
            token_type,
            token_type,
            jax.ShapeDtypeStruct((extra_rows, share), F32),
            jax.ShapeDtypeStruct((8, 128), F32),
            jax.ShapeDtypeStruct(rows_shape, BF16),
            jax.ShapeDtypeStruct(rows_shape, BF16),
            jax.ShapeDtypeStruct((2, local_experts, slots, ff_here), BF16),
            jax.ShapeDtypeStruct((local_experts, slots, ff_here), BF16),
        ),
        "vvvvvaaaa",
        [
            pltpu.VMEM((tok_rows, share), BF16),
            pltpu.VMEM(gate_up_t.shape, BF16),
            pltpu.VMEM(w_down.shape, BF16),
            pltpu.VMEM(rows_shape, BF16),
            pltpu.VMEM(rows_shape, BF16),
            pltpu.VMEM(rows_shape, BF16),
            pltpu.VMEM((2, local_experts, slots, ff_here), F32),
            pltpu.VMEM((local_experts, slots, ff_here), BF16),
            pltpu.VMEM((2, local_experts, slots, ff_here), BF16),
            pltpu.VMEM((2, tok_rows, share), F32),
            pltpu.VMEM((2 * tok_rows, share), BF16),
            pltpu.SemaphoreType.DMA((3,)),
            pltpu.SemaphoreType.DMA((4, steps)),
            pltpu.VMEM((groups, 8, 128), jnp.int32),
            pltpu.SemaphoreType.DMA((2, groups)),
            pltpu.VMEM((2, shards, 8, tok_rows), F32),
            pltpu.SemaphoreType.DMA((2, 2, shards)),
        ]
        + mover_scratch(*sizes, share) * 2,
        60,
        1,
        "experts_both",
    )
    valid_total = info[0, 0]

    gate_up_grad, down_grad = pl.pallas_call(
        functools.partial(weight_grads, shards),
        grid=(local_experts, 3),
        out_shape=(
            jax.ShapeDtypeStruct(gate_up_t.shape, F32),
            jax.ShapeDtypeStruct(w_down.shape, F32),
        ),
        in_specs=[
            pl.BlockSpec((shards, None, slots, share), lambda e, j: (0, e, 0, 0)),
            pl.BlockSpec((shards, None, slots, share), lambda e, j: (0, e, 0, 0)),
            pl.BlockSpec((None, None, slots, ff_here), lambda e, j: (jnp.minimum(j, 1), e, 0, 0)),
            pl.BlockSpec((None, slots, ff_here), lambda e, j: (e, 0, 0)),
        ],
        out_specs=(
            pl.BlockSpec((None, None, ff_here, model_width), lambda e, j: (e, jnp.minimum(j, 1), 0, 0)),
            pl.BlockSpec((None, ff_here, model_width), lambda e, j: (e, 0, 0)),
        ),
        compiler_params=pltpu.CompilerParams(vmem_limit_bytes=48 * 1024 * 1024),
        name="weight_grads",
    )(expert_rows, expert_grad, pre_grads, hidden_low)
    gate_up_grad = jnp.swapaxes(gate_up_grad, 2, 3)

    y_size = 1 << ((groups.bit_length() - 1) // 2)
    z_size = groups // y_size
    pieces, piece_rows = 2 * (1 + 3), model_width // 2
    dense, out_proj, input_grad, extras = staged_call(
        functools.partial(dense_backward, groups, shards, heads_here, head_width, experts),
        "vvvvvvvv" + "aaaaaaa",
        (
            normed_two_grad,
            after_mine,
            out_grad,
            columns,
            gain_one,
            gain_two,
            extras,
            onehot_offsets.astype(BF16),
            inputs,
            attended,
            w_out,
            projected,
            probs,
            normed_low,
            w_qkv,
        ),
        (
            jax.ShapeDtypeStruct((pieces - 2, piece_rows, width_here), BF16),
            jax.ShapeDtypeStruct((width_here, model_width), BF16),
            jax.ShapeDtypeStruct((tok_rows, share), F32),
            jax.ShapeDtypeStruct((shards, extra_rows, share), F32),
        ),
        "aavv",
        [
            pltpu.VMEM((tok_rows, share), BF16),
            pltpu.VMEM(attended.shape, BF16),
            pltpu.VMEM(w_out.shape, BF16),
            pltpu.VMEM(projected.shape, BF16),
            pltpu.VMEM(probs.shape, F32),
            pltpu.VMEM(normed_low.shape, BF16),
            pltpu.VMEM(w_qkv.shape, BF16),
            pltpu.SemaphoreType.DMA((7,)),
            pltpu.VMEM((2, shards, 8, tok_rows), F32),
            pltpu.SemaphoreType.DMA((2, 2, shards)),
            pltpu.VMEM((shards, tok_rows, share), BF16),
            pltpu.SemaphoreType.DMA((2, 2, lines, blocks)),
            pltpu.VMEM((tok_rows, share), F32),
            pltpu.VMEM((heads_here, TILE, SPAN), F32),
            pltpu.VMEM((SEQ_LEN, width_here), F32),
            pltpu.VMEM((SEQ_LEN, width_here), F32),
            pltpu.VMEM((3, tok_rows, width_here), BF16),
            pltpu.VMEM((shards, tok_rows, share), BF16),
            pltpu.VMEM((lines, tok_rows, share), BF16),
            pltpu.VMEM((lines, tok_rows, share), BF16),
            pltpu.VMEM((lines, tok_rows, share), BF16),
            pltpu.SemaphoreType.DMA((2, 2, lines, 2)),
            pltpu.VMEM((pieces, piece_rows, width_here), BF16),
            pltpu.VMEM((pieces, piece_rows, width_here), BF16),
            pltpu.VMEM((pieces, y_size, piece_rows // y_size, width_here), BF16),
            pltpu.VMEM((pieces, piece_rows // y_size, width_here), BF16),
            pltpu.VMEM((pieces, piece_rows // y_size // 2, width_here), BF16),
            pltpu.VMEM((pieces, piece_rows // y_size // 2, width_here), BF16),
            pltpu.VMEM((pieces, piece_rows // groups, width_here), BF16),
            pltpu.SemaphoreType.DMA((2, 2, pieces, y_size)),
            pltpu.SemaphoreType.DMA((2, 2, pieces, 2)),
            pltpu.SemaphoreType.DMA((pieces, max(shards // 2, 1))),
            pltpu.VMEM((1, extra_rows, share), F32),
            pltpu.VMEM((groups, extra_rows, share), F32),
            pltpu.SemaphoreType.DMA((2, groups)),
            pltpu.SemaphoreType.DMA((2, shards)),
        ],
        60,
        3,
        "dense_backward",
    )
    loss = jnp.sum(extras[:, experts + 2]) / (2.0 * valid_total * model_width)
    whole = jnp.swapaxes(extras, 0, 1).reshape(extra_rows, model_width)
    table_rows = lax.dynamic_index_in_dim(extras, lax.axis_index("tensor"), 0, keepdims=False)
    table_sum = table_rows[experts + 4 : experts + 4 + heads_here, :BUCKETS].T
    return (
        block_out,
        loss,
        input_grad,
        whole[experts],
        dense.reshape(w_qkv.shape).astype(F32),
        out_proj.astype(F32),
        table_sum,
        whole[experts + 1],
        whole[:experts].T,
        gate_up_grad,
        down_grad,
    )


def solution(mesh):
    placed = (
        P("dp", None),
        P("dp", None),
        P("dp"),
        P("dp", None),
        P("dp", None),
        P(),
        P(None, None, "tensor"),
        P("tensor", None),
        P(None, "tensor"),
        P(),
        P(),
        P("dp", None, None, "tensor"),
        P("dp", "tensor", None),
    )
    return jax.shard_map(
        body,
        mesh=mesh,
        in_specs=placed,
        out_specs=(
            P("dp", "tensor"),
            P(),
            P("dp", "tensor"),
            P(),
            P(None, None, "tensor"),
            P("tensor", None),
            P(None, "tensor"),
            P(),
            P(),
            P("dp", None, None, "tensor"),
            P("dp", "tensor", None),
        ),
        check_vma=False,
    )
```

```python
import functools
import math

import jax
import jax.numpy as jnp
from jax import lax
from jax.experimental import pallas as pl
from jax.experimental.pallas import tpu as pltpu
from jax.sharding import PartitionSpec as P

BUCKETS = 32
SEQ_LEN = 512
TILE = 128
SPAN = 2 * SEQ_LEN

EPSILON = 1e-06
FAR_STEPS = (12, 16, 23, 32, 46, 64, 91)
MASKED = -1000000000.0
F32 = jnp.float32
BF16 = jnp.bfloat16


def offset_bucket(offset):
    direction = jnp.where(offset > 0, 16, 0).astype(jnp.int32)
    distance = jnp.abs(offset)
    farther = jnp.full(offset.shape, 8, jnp.int32)
    for threshold in FAR_STEPS:
        farther = farther + (distance >= threshold).astype(jnp.int32)
    return direction + jnp.where(distance < 8, distance, farther)


def bucket_onehot(offsets):
    bucket_range = jnp.arange(BUCKETS, dtype=jnp.int32)
    return (offset_bucket(offsets)[:, None] == bucket_range[None, :]).astype(F32)


def dot(a, b, dims=((1,), (0,))):
    return lax.dot_general(a, b, (dims, ((), ())), preferred_element_type=F32)


SMEM = pl.BlockSpec(memory_space=pltpu.SMEM)


def staged_call(body, kinds, arrays, out_types, out_kinds, scratch, limit, collective, name):
    staged_in = [n for n, kind in enumerate(kinds) if kind == "v"]
    staged_out = [n for n, kind in enumerate(out_kinds) if kind == "v"]

    def kernel(*refs):
        ins, outs = list(refs[: len(kinds)]), list(refs[len(kinds) : len(kinds) + len(out_kinds)])
        rest = list(refs[len(kinds) + len(out_kinds) :])
        in_sems, out_sems = rest[:2]
        in_bufs = rest[2 : 2 + len(staged_in)]
        out_bufs = rest[2 + len(staged_in) : 2 + len(staged_in) + len(staged_out)]
        rest = rest[2 + len(staged_in) + len(staged_out) :]
        loads = []
        for m, n in enumerate(staged_in):
            loads.append(pltpu.make_async_copy(ins[n], in_bufs[m], in_sems.at[m]))
            ins[n] = in_bufs[m]
        for load in loads:
            load.start()
        results = []
        for m, n in enumerate(staged_out):
            results.append((out_bufs[m], outs[n], out_sems.at[m]))
            outs[n] = out_bufs[m]

        def ready():
            for load in loads:
                load.wait()

        body(ready, *ins, *outs, *rest)
        copies = [pltpu.make_async_copy(*result) for result in results]
        for copy in copies:
            copy.start()
        for copy in copies:
            copy.wait()

    return pl.pallas_call(
        kernel,
        out_shape=tuple(out_types),
        in_specs=[SMEM if kind == "s" else ANY for kind in kinds],
        out_specs=tuple(ANY for _ in out_kinds),
        scratch_shapes=[
            pltpu.SemaphoreType.DMA((max(len(staged_in), 1),)),
            pltpu.SemaphoreType.DMA((max(len(staged_out), 1),)),
        ]
        + [pltpu.VMEM(arrays[n].shape, arrays[n].dtype) for n in staged_in]
        + [pltpu.VMEM(out_types[n].shape, out_types[n].dtype) for n in staged_out]
        + scratch,
        compiler_params=pltpu.CompilerParams(
            vmem_limit_bytes=limit * 1024 * 1024, collective_id=collective, has_side_effects=True
        ),
        name=name,
    )(*arrays)


MESH_ID = pl.DeviceIdType.MESH
ANY = pl.BlockSpec(memory_space=pltpu.HBM)


def weight_grads(
    shards, heads, experts,
    rows, grads, side, hidden, dense, out_proj, extras, info, block_in, input_in,
    gate_up_out, down_out, dense_out, out_proj_out, router_out, gain_one_out, gain_two_out, table_out, loss_out,
    block_out, input_out,
):
    step = pl.program_id(1)
    at = pl.program_id(0) * 3 + step
    share = rows.shape[-1]

    @pl.when(at == 0)
    def _():
        block_out[...] = block_in[...]
        input_out[...] = input_in[...]
        out_proj_out[...] = out_proj[...].astype(F32)
        for s in range(shards):
            cols = slice(s * share, (s + 1) * share)
            router_out[:, cols] = extras[s, :experts, :]
            gain_one_out[:, cols] = extras[s, experts : experts + 1, :]
            gain_two_out[:, cols] = extras[s, experts + 1 : experts + 2, :]
        table_out[...] = extras[lax.axis_index("tensor"), experts + 4 : experts + 4 + heads, :BUCKETS]
        squares = sum(extras[s, experts + 2 : experts + 3, :] for s in range(shards))
        model = share * shards
        loss_out[...] = jnp.sum(squares, axis=1, keepdims=True) / (2.0 * info[0:1, 0:1] * model)

    dense_out[...] = dense[...].astype(F32)

    @pl.when(step < 2)
    def _():
        for s in range(shards):
            gate_up_out[:, s * share : (s + 1) * share] = dot(side[...], rows[s], ((0,), (0,)))

    @pl.when(step == 2)
    def _():
        for s in range(shards):
            down_out[:, s * share : (s + 1) * share] = dot(hidden[...], grads[s], ((0,), (0,)))


def to_row(column):
    rows = column.shape[0]
    return jnp.transpose(jnp.broadcast_to(column, (rows, 128)))[:8]


def to_column(row):
    return jnp.transpose(jnp.broadcast_to(row[:1], (128, row.shape[1])))[:, :1]


def flip(value, mask, size):
    total, unit = 0, 1
    while unit < size:
        bit = lax.rem(lax.div(value, unit), 2)
        total = total + unit * ((1 - bit) if mask & unit else bit)
        unit *= 2
    return total


def plan(groups, chunk):
    kinds = ("spread", "relay", "products", "along", "give", "taken")
    steps = []
    for step in range(groups // chunk + len(kinds) - 1):
        for lag, kind in enumerate(kinds):
            k = step - lag
            if 0 <= k < groups // chunk:
                steps += [(kind, k)] if kind == "products" else [(kind, k * chunk + n) for n in range(chunk)]
    return steps


class Mover:
    def __init__(self, groups, shards, cap, chunk, rows, part, scratch):
        self.groups, self.lines, self.cap, self.chunk = groups, shards // 2, cap, chunk
        self.rows, self.part = rows, part
        (
            self.source, self.mate_in, self.line_out, self.line_in, self.back_out, self.back,
            self.dp_sems, self.row_sems, self.sum_sems,
        ) = scratch
        self.me, self.place = lax.axis_index("dp"), lax.axis_index("tensor")
        self.line, self.core = lax.div(self.place, 2), lax.rem(self.place, 2)
        self.steps = groups // chunk

    def peer(self, i):
        return flip(self.me, i, self.groups)

    def shard(self, offset, core):
        return lax.rem(self.line + offset, self.lines) * 2 + core

    def near(self, i):
        return lax.rem(self.place + i, 2 * self.lines)

    def remote(self, src, dst, sems, index, device):
        return pltpu.make_async_remote_copy(
            src_ref=src, dst_ref=dst, send_sem=sems.at[(0, *index)], recv_sem=sems.at[(1, *index)],
            device_id=device, device_id_type=MESH_ID,
        )

    def mate(self):
        return {"tensor": self.shard(0, 1 - self.core)}

    def landed(self, where, sems, index):
        self.remote(where, where, sems, index, self.mate()).wait_recv()

    def here(self, shard, i):
        return self.rows.at[shard, :, pl.ds(i * self.cap, self.cap), :]

    def send(self, i, block):
        block = block.reshape(-1, self.cap, block.shape[-1])
        if i == 0:
            self.rows[self.place, :, : self.cap, :] = block
        else:
            self.source[i] = block
            self.out_copy(i).start()

    def out_copy(self, i):
        return self.remote(
            self.source.at[i], self.here(self.place, i), self.dp_sems.at[0], (i,), {"dp": self.peer(i)}
        )

    def line_copy(self, d, i):
        return self.remote(
            self.here(self.place, i), self.here(self.place, i), self.row_sems.at[0], (d, i),
            {"tensor": self.shard(d, self.core)},
        )

    def mate_copy(self, d, i):
        shard = self.shard(self.lines - d, self.core)
        return self.remote(self.here(shard, i), self.here(shard, i), self.row_sems.at[1], (d, i), self.mate())

    def places(self, k):
        return range(k * self.chunk, (k + 1) * self.chunk)

    def spread(self, i):
        if i:
            self.landed(self.here(self.place, i), self.dp_sems.at[0], (i,))
        for d in range(1, self.lines):
            self.line_copy(d, i).start()
        self.mate_copy(0, i).start()

    def relay(self, i):
        for d in range(1, self.lines):
            shard = self.shard(self.lines - d, self.core)
            self.landed(self.here(shard, i), self.row_sems.at[0], (d, i))
            self.mate_copy(d, i).start()

    def collect(self, i):
        for d in range(self.lines):
            shard = self.shard(self.lines - d, 1 - self.core)
            self.landed(self.here(shard, i), self.row_sems.at[1], (d, i))

    def span(self, k):
        return pl.ds(k * self.chunk * self.cap, self.chunk * self.cap)

    def block(self, i):
        return pl.ds(i * self.cap, self.cap)

    def pair_copy(self, d, i):
        shard = self.shard(d, 1 - self.core)
        return self.remote(
            self.part.at[shard, :, self.block(i), :], self.mate_in.at[d, :, self.block(i), :], self.sum_sems.at[0], (d, i),
            self.mate(),
        )

    def sum_copy(self, d, i):
        return self.remote(
            self.line_out.at[d - 1, :, self.block(i), :], self.line_in.at[d - 1, :, self.block(i), :],
            self.sum_sems.at[1], (d, i), {"tensor": self.shard(d, self.core)},
        )

    def back_copy(self, i):
        return self.remote(
            self.back_out.at[:, self.block(i), :], self.back.at[i], self.dp_sems.at[1], (i,), {"dp": self.peer(i)}
        )

    def pair(self, k):
        for i in self.places(k):
            for d in range(self.lines):
                self.pair_copy(d, i).start()

    def pair_sum(self, d, i):
        shard = self.shard(d, self.core)
        return self.part[shard, :, self.block(i), :].astype(F32) + self.mate_in[d, :, self.block(i), :].astype(F32)

    def along(self, i):
        for d in range(self.lines):
            self.landed(self.mate_in.at[d, :, self.block(i), :], self.sum_sems.at[0], (d, i))
        for d in range(1, self.lines):
            self.line_out[d - 1, :, self.block(i), :] = self.pair_sum(d, i).astype(BF16)
            self.sum_copy(d, i).start()

    def give(self, i):
        total = self.pair_sum(0, i)
        for d in range(1, self.lines):
            self.landed(self.line_in.at[d - 1, :, self.block(i), :], self.sum_sems.at[1], (d, i))
            total = total + self.line_in[d - 1, :, self.block(i), :].astype(F32)
        total = total.astype(BF16)
        if i == 0:
            self.back[0] = total
        else:
            self.back_out[:, self.block(i), :] = total
            self.back_copy(i).start()

    def arrived(self, i):
        if i:
            self.landed(self.back.at[i], self.dp_sems.at[1], (i,))
        return self.back[i].reshape(-1, self.back.shape[-1])

    def run(self, compute, take):
        def products(k):
            for i in self.places(k):
                self.collect(i)
            compute(k)
            self.pair(k)

        def taken(i):
            take(i, self.arrived(i))

        works = dict(
            spread=self.spread, relay=self.relay, products=products, along=self.along, give=self.give, taken=taken
        )
        for work, index in plan(self.groups, self.chunk):
            works[work](index)

    def finish(self):
        for i in range(1, self.groups):
            self.out_copy(i).wait_send()
            self.back_copy(i).wait_send()
        for i in range(self.groups):
            for d in range(self.lines):
                if d:
                    self.line_copy(d, i).wait_send()
                    self.sum_copy(d, i).wait_send()
                self.mate_copy(d, i).wait_send()
                self.pair_copy(d, i).wait_send()


def mover_scratch(groups, shards, local, cap, share):
    lines, slots = shards // 2, groups * cap
    return [
        pltpu.VMEM((groups, local, cap, share), BF16),
        pltpu.VMEM((lines, local, slots, share), BF16),
        pltpu.VMEM((lines - 1, local, slots, share), BF16),
        pltpu.VMEM((lines - 1, local, slots, share), BF16),
        pltpu.VMEM((local, slots, share), BF16),
        pltpu.VMEM((groups, local, cap, share), BF16),
        pltpu.SemaphoreType.DMA((2, 2, groups)),
        pltpu.SemaphoreType.DMA((2, 2, lines, groups)),
        pltpu.SemaphoreType.DMA((2, 2, lines, groups)),
    ]


MOVER_REFS = 9
ROOT = math.sqrt(2.0 / math.pi)


def gelu_parts(v):
    inner = jnp.tanh(ROOT * (v + 0.044715 * (v * v * v)))
    half = 0.5 * (1.0 + inner)
    slope = half + 0.5 * v * (1.0 - inner * inner) * (ROOT * (1.0 + 3.0 * 0.044715 * v * v))
    return v * half, slope


def experts_both(
    groups, shards, local, cap, chunk, experts,
    ready, len_ref, normed, after, columns, target_ref, ids_ref, router,
    teacher_hbm, gate_up_hbm, down_hbm,
    block_out, out_grad, norm_grad, extras, info,
    rows_hbm, grads_hbm, side_hbm, hidden_hbm,
    teacher, gate_up, down, rows, grads, part, pre, hidden, side, routed, gated, load_sems, save_sems,
    counts, count_sems, dots, dot_sems, *scratch,
):
    ahead = Mover(groups, shards, cap, chunk, rows, part, scratch[:MOVER_REFS])
    behind = Mover(groups, shards, cap, chunk, grads, part, scratch[MOVER_REFS:])
    tokens, share = normed.shape
    width = local * cap
    place = ahead.place
    mine = pl.ds(pl.multiple_of(place * share, 128), share)
    loads = [
        pltpu.make_async_copy(gate_up_hbm, gate_up, load_sems.at[0]),
        pltpu.make_async_copy(down_hbm, down, load_sems.at[1]),
        pltpu.make_async_copy(teacher_hbm.at[:, mine], teacher, load_sems.at[2]),
    ]
    for load in loads:
        load.start()

    barrier = pltpu.get_barrier_semaphore()
    for i in range(1, groups):
        pl.semaphore_signal(barrier, inc=1, device_id={"dp": ahead.peer(i)}, device_id_type=MESH_ID)
    for i in range(1, shards):
        pl.semaphore_signal(barrier, inc=1, device_id={"tensor": ahead.near(i)}, device_id_type=MESH_ID)
    counts[0] = jnp.full((8, 128), len_ref[0], jnp.int32)
    slot_lines = lax.broadcasted_iota(jnp.int32, (width, tokens), 0)
    slot_lanes = lax.broadcasted_iota(jnp.int32, (tokens, width), 1)
    ready()
    row_targets = [target_ref[n : n + 1, :] for n in range(2)]
    column_targets = [to_column(target_ref[n : n + 1, :].astype(F32)).astype(jnp.int32) for n in range(2)]

    def by_slot(i, n):
        return slot_lines + ahead.peer(i) * width == row_targets[n]

    def by_token(i, n):
        return slot_lanes + ahead.peer(i) * width == column_targets[n]

    def ones(mask):
        return jnp.where(mask, 1.0, 0.0).astype(BF16)

    pl.semaphore_wait(barrier, groups + shards - 2)

    def count_copy(i):
        return ahead.remote(counts.at[0], counts.at[i], count_sems, (i,), {"dp": ahead.peer(i)})

    order = [*range(1, groups), 0]
    for i in order:
        ahead.send(i, dot(ones(by_slot(i, 0) | by_slot(i, 1)), normed[...]).astype(BF16))
    for i in range(1, groups):
        count_copy(i).start()

    def forward_saves(k):
        span = ahead.span(k)
        return [
            pltpu.make_async_copy(rows.at[:, :, span, :], rows_hbm.at[:, :, span, :], save_sems.at[0, k]),
            pltpu.make_async_copy(hidden.at[:, span, :], hidden_hbm.at[:, span, :], save_sems.at[1, k]),
        ]

    def backward_saves(k):
        span = ahead.span(k)
        return [
            pltpu.make_async_copy(grads.at[:, :, span, :], grads_hbm.at[:, :, span, :], save_sems.at[2, k]),
            pltpu.make_async_copy(side.at[:, :, span, :], side_hbm.at[:, :, span, :], save_sems.at[3, k]),
        ]

    def put(e, span, result):
        result = result.astype(BF16)
        for s in range(shards):
            part[s, e, span, :] = result[:, s * share : (s + 1) * share]

    def forward(k):
        span = ahead.span(k)
        if k == 0:
            loads[0].wait()
            loads[1].wait()
        for e in range(local):
            lhs = jnp.concatenate([rows[s, e, span, :] for s in range(shards)], axis=1)
            gate = dot(lhs, gate_up[e, 0], ((1,), (1,)))
            up = dot(lhs, gate_up[e, 1], ((1,), (1,)))
            pre[0, e, span, :] = gate
            pre[1, e, span, :] = up
            low = (gelu_parts(gate)[0] * up).astype(BF16)
            hidden[e, span, :] = low
            put(e, span, dot(low, down[e]))
        for save in forward_saves(k):
            save.start()

    def take(i, block):
        for n in range(2):
            value = dot(ones(by_token(i, n)), block)
            if i == 0:
                routed[n] = value
            else:
                routed[n] += value

    ahead.run(forward, take)

    tally = counts[0]
    for i in range(1, groups):
        count_copy(i).wait()
        tally = tally + counts[i]
    valid = tally.astype(F32)
    loads[2].wait()
    gates = [columns[:, 2:3], columns[:, 3:4]]
    output = after[...] + gates[0] * routed[0] + gates[1] * routed[1]
    block_out[...] = output
    alive = lax.broadcasted_iota(jnp.int32, (tokens, share), 0) < len_ref[0]
    deviation = jnp.where(alive, output - teacher[...].astype(F32), 0.0)
    scaled = deviation * (groups * tokens / valid[0:1, 0:1])
    out_grad[...] = scaled
    for n in range(2):
        gated[n * tokens : (n + 1) * tokens, :] = (gates[n] * scaled).astype(BF16)
    for i in order:
        both = jnp.concatenate([ones(by_slot(i, 0)), ones(by_slot(i, 1))], axis=1)
        behind.send(i, dot(both, gated[...]).astype(BF16))
    for n in range(2):
        dots[n, 0] = to_row(jnp.sum(routed[n] * scaled, axis=1, keepdims=True))

    def dot_copy(n, i):
        return ahead.remote(dots.at[n, 0], dots.at[n, i], dot_sems, (n, i), {"tensor": ahead.near(i)})

    for n in range(2):
        for i in range(1, shards):
            dot_copy(n, i).start()
    info[...] = valid
    extras[...] = jnp.zeros_like(extras)
    extras[experts + 2 : experts + 3, :] = jnp.sum(deviation * deviation, axis=0, keepdims=True)
    ahead.finish()

    def route_grads():
        parts = []
        for n in range(2):
            total = dots[n, 0]
            for i in range(1, shards):
                dot_copy(n, i).wait()
                total = total + dots[n, i]
            parts.append(to_column(total))
        expert_probs = columns[:, 16 : 16 + experts]
        lanes = lax.broadcasted_iota(jnp.int32, (tokens, experts), 1)
        picks = [
            jnp.where(lanes == to_column(ids_ref[n : n + 1, :].astype(F32)).astype(jnp.int32), 1.0, 0.0)
            for n in range(2)
        ]
        chosen_total = jnp.sum(expert_probs * (picks[0] + picks[1]), axis=1, keepdims=True)
        along = parts[0] * gates[0] + parts[1] * gates[1]
        probs_grad = sum(picks[n] * ((parts[n] - along) / chosen_total) for n in range(2))
        logit_grad = expert_probs * (probs_grad - jnp.sum(probs_grad * expert_probs, axis=1, keepdims=True))
        logit_grad = logit_grad.astype(BF16)
        extras[0:experts, :] = dot(logit_grad, normed[...], ((0,), (0,)))
        norm_grad[...] = dot(logit_grad, router[:, mine])

    def backward(k):
        span = ahead.span(k)
        for e in range(local):
            lhs = jnp.concatenate([grads[s, e, span, :] for s in range(shards)], axis=1)
            hidden_grad = dot(lhs, down[e], ((1,), (1,)))
            activated, slope = gelu_parts(pre[0, e, span, :])
            gate_side = (hidden_grad * pre[1, e, span, :] * slope).astype(BF16)
            up_side = (hidden_grad * activated).astype(BF16)
            side[0, e, span, :] = gate_side
            side[1, e, span, :] = up_side
            put(e, span, dot(gate_side, gate_up[e, 0]) + dot(up_side, gate_up[e, 1]))
        for save in backward_saves(k):
            save.start()
        if k == 0:
            route_grads()

    def take_back(i, block):
        norm_grad[...] += dot(ones(by_token(i, 0) | by_token(i, 1)), block)

    behind.run(backward, take_back)
    behind.finish()
    for k in range(ahead.steps):
        for save in forward_saves(k) + backward_saves(k):
            save.wait()


def gate_columns(logits, first, second):
    lanes = lax.broadcasted_iota(jnp.int32, logits.shape, 1)
    exponent = jnp.exp(logits - jnp.max(logits, axis=1, keepdims=True))
    expert_probs = exponent / jnp.sum(exponent, axis=1, keepdims=True)
    chosen = [jnp.sum(jnp.where(lanes == pick, expert_probs, 0.0), axis=1, keepdims=True) for pick in (first, second)]
    total = chosen[0] + chosen[1]
    return expert_probs, chosen[0] / total, chosen[1] / total


def dense_forward(
    groups, shards, heads, width, experts,
    ready, len_ref, bias_ref, ids_ref, gain_one, gain_two, router_ref,
    inputs_hbm, w_qkv_hbm, w_out_hbm,
    normed_out, proj_out, probs_out, attended_out, after_out, normed_two_out, columns_out,
    inputs, w_qkv, load_sems, w_out, w_sems, attended, attended_sems, skew, normed, proj, probs, after, normed_two, save_sems,
):
    tokens, model = inputs.shape
    here = heads * width
    share = model // shards
    lines = shards // 2
    blocks = tokens // TILE
    place = lax.axis_index("tensor")
    line, core = lax.div(place, 2), lax.rem(place, 2)
    mate = {"tensor": line * 2 + 1 - core}

    def shard(d, c):
        return lax.rem(line + d, lines) * 2 + c

    def remote(src, dst, sems, index, device):
        return pltpu.make_async_remote_copy(
            src_ref=src, dst_ref=dst, send_sem=sems.at[(0, *index)], recv_sem=sems.at[(1, *index)],
            device_id=device, device_id_type=MESH_ID,
        )

    def landed(where, sems, index):
        remote(where, where, sems, index, mate).wait_recv()

    loads = [
        pltpu.make_async_copy(inputs_hbm, inputs, load_sems.at[0]),
        pltpu.make_async_copy(w_qkv_hbm, w_qkv, load_sems.at[1]),
        pltpu.make_async_copy(w_out_hbm, w_out.at[place], load_sems.at[2]),
    ]
    for load in loads:
        load.start()
    barrier = pltpu.get_barrier_semaphore()
    for d in range(1, lines):
        pl.semaphore_signal(barrier, inc=1, device_id={"tensor": shard(d, core)}, device_id_type=MESH_ID)
    pl.semaphore_signal(barrier, inc=1, device_id=mate, device_id_type=MESH_ID)
    pl.semaphore_wait(barrier, lines)

    def w_line(d):
        return remote(w_out.at[place], w_out.at[place], w_sems.at[0], (d,), {"tensor": shard(d, core)})

    def w_mate(d):
        where = w_out.at[shard(lines - d, core)]
        return remote(where, where, w_sems.at[1], (d,), mate)

    def row_block(j):
        return pl.ds(j * TILE, TILE)

    def rows_line(d, j):
        where = attended.at[place, row_block(j), :]
        return remote(where, where, attended_sems.at[0], (d, j), {"tensor": shard(d, core)})

    def rows_mate(d, j):
        where = attended.at[shard(lines - d, core), row_block(j), :]
        return remote(where, where, attended_sems.at[1], (d, j), mate)

    ready()
    loads[2].wait()
    for d in range(1, lines):
        w_line(d).start()
    w_mate(0).start()

    loads[0].wait()
    for j in range(blocks):
        rows = slice(j * TILE, (j + 1) * TILE)
        values = inputs[rows, :].astype(F32)
        scale = lax.rsqrt(jnp.mean(values * values, axis=1, keepdims=True) + EPSILON)
        columns_out[rows, 0:1] = scale
        normed[rows, :] = (values * scale * gain_one[...]).astype(BF16)
    loads[1].wait()
    for n in range(3):
        proj[n] = dot(normed[...], w_qkv[n]).astype(BF16)
    saves = [
        pltpu.make_async_copy(normed, normed_out, save_sems.at[0]),
        pltpu.make_async_copy(proj, proj_out, save_sems.at[1]),
    ]
    for h in range(heads):
        skew[h] = pltpu.roll(
            jnp.broadcast_to(bias_ref[h : h + 1, :], (TILE, SPAN)), 0, 1, stride=1, stride_axis=0
        )
    for item in saves:
        item.start()

    alive = lax.broadcasted_iota(jnp.int32, (TILE, SEQ_LEN), 1) < len_ref[0]
    for j in range(blocks):
        rows = slice(j * TILE, (j + 1) * TILE)
        start = SEQ_LEN - j * TILE
        for h in range(heads):
            cols = slice(h * width, (h + 1) * width)
            scores = dot(proj[0, rows, cols], proj[1, :, cols], ((1,), (1,)))
            scores = jnp.where(alive, scores + skew[h, :, start : start + SEQ_LEN], MASKED)
            exponent = jnp.exp(scores - jnp.max(scores, axis=1, keepdims=True))
            weights = exponent * (1.0 / jnp.sum(exponent, axis=1, keepdims=True))
            probs[h, rows, :] = weights
            attended[place, rows, cols] = dot(weights.astype(BF16), proj[2, :, cols]).astype(BF16)
        for d in range(1, lines):
            rows_line(d, j).start()
        rows_mate(0, j).start()
        if j == blocks - 2:
            for d in range(1, lines):
                landed(w_out.at[shard(lines - d, core)], w_sems.at[0], (d,))
                w_mate(d).start()
    saves += [
        pltpu.make_async_copy(probs, probs_out, save_sems.at[2]),
        pltpu.make_async_copy(attended.at[place], attended_out, save_sems.at[3]),
    ]
    for item in saves[2:]:
        item.start()

    ids = ids_ref[...].astype(F32)
    picks = [to_column(ids[n : n + 1]).astype(jnp.int32) for n in range(2)]

    def relay(j):
        for d in range(1, lines):
            landed(attended.at[shard(lines - d, core), row_block(j), :], attended_sems.at[0], (d, j))
            rows_mate(d, j).start()

    relay(0)
    for d in range(lines):
        landed(w_out.at[shard(lines - d, 1 - core)], w_sems.at[1], (d,))
    for j in range(blocks):
        rows = slice(j * TILE, (j + 1) * TILE)
        if j + 1 < blocks:
            relay(j + 1)
        for d in range(lines):
            landed(attended.at[shard(lines - d, 1 - core), row_block(j), :], attended_sems.at[1], (d, j))
        total = inputs[rows, :].astype(F32)
        for s in range(shards):
            total = total + dot(attended[s, rows, :], w_out[s])
        scale = lax.rsqrt(jnp.mean(total * total, axis=1, keepdims=True) + EPSILON)
        low = (total * scale * gain_two[...]).astype(BF16)
        after[...] = total
        normed_two[...] = low
        mine = pl.ds(pl.multiple_of(place * share, 128), share)
        after_out[rows, :] = after[:, mine]
        normed_two_out[rows, :] = normed_two[:, mine]
        expert_probs, first, second = gate_columns(
            dot(low, router_ref[...], ((1,), (1,))), picks[0][rows], picks[1][rows]
        )
        columns_out[rows, 1:2] = scale
        columns_out[rows, 2:3] = first
        columns_out[rows, 3:4] = second
        columns_out[rows, 16 : 16 + experts] = expert_probs
    for d in range(lines):
        if d:
            w_line(d).wait_send()
        w_mate(d).wait_send()
        for j in range(blocks):
            if d:
                rows_line(d, j).wait_send()
            rows_mate(d, j).wait_send()
    for item in saves:
        item.wait()


def dense_backward(
    groups, shards, heads, width, experts,
    ready, norm_grad, after, out_grad, scales, gain_one, gain_two, extras_in, onehot,
    inputs_hbm, attended_hbm, w_out_hbm, proj_hbm, probs_hbm, normed_hbm, w_qkv_hbm,
    dense_out, out_proj_out, input_grad, extras_out,
    residual, attended, w_out, proj, probs, normed, w_qkv, load_sems,
    dots, dot_sems, branch, branch_sems, grad_here, diag, key_acc, value_acc, proj_grad,
    part, mate_in, line_out, line_in, part_sems,
    dense, result, y_in, y_sum, half_in, half_sum, block_in, dense_sems, z_sems, save_sems,
    extras, extras_in_dp, extras_sems, extras_ring_sems,
):
    model = normed.shape[1]
    share = branch.shape[-1]
    tokens = branch.shape[1]
    here = heads * width
    lines = shards // 2
    y_size = 1 << ((groups.bit_length() - 1) // 2)
    z_size = groups // y_size
    pieces = dense.shape[0]
    me, place = lax.axis_index("dp"), lax.axis_index("tensor")
    line, core = lax.div(place, 2), lax.rem(place, 2)
    z, y = lax.div(me, y_size), lax.rem(me, y_size)
    mate = {"tensor": line * 2 + 1 - core}
    inverse = 1.0 / model
    mine = pl.ds(pl.multiple_of(place * share, 128), share)

    def group(i):
        return lax.rem(me + i, groups)

    def shard(d, c):
        return lax.rem(line + d, lines) * 2 + c

    def near(i):
        return lax.rem(place + i, shards)

    def remote(src, dst, sems, index, device):
        return pltpu.make_async_remote_copy(
            src_ref=src, dst_ref=dst, send_sem=sems.at[(0, *index)], recv_sem=sems.at[(1, *index)],
            device_id=device, device_id_type=MESH_ID,
        )

    def landed(where, sems, index):
        remote(where, where, sems, index, mate).wait_recv()

    loads = [
        pltpu.make_async_copy(src, dst, load_sems.at[n])
        for n, (src, dst) in enumerate(
            (
                (w_out_hbm, w_out), (attended_hbm, attended), (proj_hbm, proj), (probs_hbm, probs),
                (w_qkv_hbm, w_qkv), (normed_hbm, normed), (inputs_hbm.at[:, mine], residual),
            )
        )
    ]
    for load in loads:
        load.start()

    barrier = pltpu.get_barrier_semaphore()
    for i in range(1, groups):
        pl.semaphore_signal(barrier, inc=1, device_id={"dp": group(i)}, device_id_type=MESH_ID)
    for i in range(1, shards):
        pl.semaphore_signal(barrier, inc=1, device_id={"tensor": near(i)}, device_id_type=MESH_ID)
    def dot_copy(n, i):
        return remote(dots.at[n, 0], dots.at[n, i], dot_sems, (n, i), {"tensor": near(i)})

    def dot_send(n, column):
        dots[n, 0] = to_row(column)
        if n == 0:
            pl.semaphore_wait(barrier, groups + shards - 2)
        for i in range(1, shards):
            dot_copy(n, i).start()

    def dot_sum(n):
        total = dots[n, 0]
        for i in range(1, shards):
            dot_copy(n, i).wait()
            total = total + dots[n, i]
        return to_column(total)

    ready()
    scale_two = scales[:, 1:2]
    weighted = norm_grad[...] * gain_two[:, mine]
    dot_send(0, jnp.sum(weighted * after[...], axis=1, keepdims=True))
    extras[0] = extras_in[...]
    extras[0, experts + 1 : experts + 2, :] = jnp.sum(norm_grad[...] * after[...] * scale_two, axis=0, keepdims=True)
    along = dot_sum(0)
    after_grad = out_grad[...] + scale_two * (weighted - after[...] * (scale_two * scale_two * along * inverse))
    grad_here[...] = after_grad
    branch[place] = after_grad.astype(BF16)

    blocks = tokens // TILE

    def row_block(j):
        return pl.ds(j * TILE, TILE)

    def branch_line(d, j):
        where = branch.at[place, row_block(j), :]
        return remote(where, where, branch_sems.at[0], (d, j), {"tensor": shard(d, core)})

    def branch_mate(d, j):
        where = branch.at[shard(lines - d, core), row_block(j), :]
        return remote(where, where, branch_sems.at[1], (d, j), mate)

    for j in range(blocks):
        for d in range(1, lines):
            branch_line(d, j).start()
        branch_mate(0, j).start()
    for j in range(blocks):
        for d in range(1, lines):
            landed(branch.at[shard(lines - d, core), row_block(j), :], branch_sems.at[0], (d, j))
            branch_mate(d, j).start()
    def branch_landed(j):
        for d in range(lines):
            landed(branch.at[shard(lines - d, 1 - core), row_block(j), :], branch_sems.at[1], (d, j))

    rows_here = dense.shape[1]
    y_rows, z_rows = rows_here // y_size, rows_here // groups

    def y_copy(p, a):
        to = lax.rem(y + a, y_size)
        return remote(
            dense.at[p, pl.ds(to * y_rows, y_rows), :], y_in.at[p, a], dense_sems.at[0], (p, a), {"dp": z * y_size + to}
        )

    z_low, z_high = lax.rem(z, 2), lax.div(z, 2)
    half_rows = y_rows // 2
    kept_half, kept_block = y * y_rows + z_low * half_rows, y * y_rows + z_low * half_rows + z_high * z_rows
    near_z = {"dp": (z_high * 2 + 1 - z_low) * y_size + y}
    far_z = {"dp": ((1 - z_high) * 2 + z_low) * y_size + y}

    def half_copy(p):
        return remote(
            y_sum.at[p, pl.ds((1 - z_low) * half_rows, half_rows), :], half_in.at[p], z_sems.at[0], (p, 0), near_z
        )

    def block_copy(p):
        return remote(
            half_sum.at[p, pl.ds((1 - z_high) * z_rows, z_rows), :], block_in.at[p], z_sems.at[0], (p, 1), far_z
        )

    def block_spread(p):
        where = result.at[p, pl.ds(kept_block, z_rows), :]
        return remote(where, where, z_sems.at[1], (p, 1), far_z)

    def half_spread(p):
        where = result.at[p, pl.ds(kept_half, half_rows), :]
        return remote(where, where, z_sems.at[1], (p, 0), near_z)

    def y_spread(p, a):
        to = lax.rem(y + a, y_size)
        where = result.at[p, pl.ds(y * y_rows, y_rows), :]
        return remote(where, where, dense_sems.at[1], (p, a), {"dp": z * y_size + to})

    def reduce_start(p):
        for a in range(1, y_size):
            y_copy(p, a).start()

    def reduce_y(p):
        total = dense[p, pl.ds(y * y_rows, y_rows), :].astype(F32)
        for a in range(1, y_size):
            landed(y_in.at[p, a], dense_sems.at[0], (p, a))
            total = total + y_in[p, a].astype(F32)
        y_sum[p] = total.astype(BF16)
        half_copy(p).start()

    def reduce_half(p):
        for a in range(1, y_size):
            y_copy(p, a).wait_send()
        landed(half_in.at[p], z_sems.at[0], (p, 0))
        mine_half = y_sum[p, pl.ds(z_low * half_rows, half_rows), :].astype(F32)
        half_sum[p] = (mine_half + half_in[p].astype(F32)).astype(BF16)
        block_copy(p).start()

    def reduce_block(p):
        landed(block_in.at[p], z_sems.at[0], (p, 1))
        mine_block = half_sum[p, pl.ds(z_high * z_rows, z_rows), :].astype(F32)
        result[p, pl.ds(kept_block, z_rows), :] = (mine_block + block_in[p].astype(F32)).astype(BF16)
        block_spread(p).start()

    def spread_block(p):
        landed(result.at[p, pl.ds(kept_half + (1 - z_high) * z_rows, z_rows), :], z_sems.at[1], (p, 1))
        half_spread(p).start()

    def spread_half(p):
        landed(result.at[p, pl.ds(y * y_rows + (1 - z_low) * half_rows, half_rows), :], z_sems.at[1], (p, 0))
        for a in range(1, y_size):
            y_spread(p, a).start()

    per_piece = shards // 2

    def save(p):
        if p >= 2:
            return [pltpu.make_async_copy(result.at[p], dense_out.at[p - 2], save_sems.at[p, 0])]
        return [
            pltpu.make_async_copy(
                result.at[p, pl.ds(n * here, here), :],
                out_proj_out.at[:, pl.ds((p * per_piece + n) * here, here)],
                save_sems.at[p, n],
            )
            for n in range(per_piece)
        ]

    def spread_y(p):
        for a in range(1, y_size):
            origin = lax.rem(y + y_size - a, y_size)
            landed(result.at[p, pl.ds(origin * y_rows, y_rows), :], dense_sems.at[1], (p, a))
        for copy in save(p):
            copy.start()

    def out_projection():
        loads[1].wait()
        for s in range(shards):
            n = s % per_piece
            dense[s // per_piece, n * here : (n + 1) * here, :] = dot(
                attended[...], branch[s], ((0,), (0,))
            ).astype(BF16)
        for p in range(2):
            reduce_start(p)

    loads[0].wait()
    loads[2].wait()
    loads[3].wait()
    diag[...] = jnp.zeros_like(diag)
    for j in range(blocks):
        rows = slice(j * TILE, (j + 1) * TILE)
        start = SEQ_LEN - j * TILE
        branch_landed(j)
        if j == blocks - 1:
            out_projection()
        wide = jnp.concatenate([branch[s, rows, :] for s in range(shards)], axis=1)
        grads = dot(wide, w_out[...], ((1,), (1,))).astype(BF16)
        for h in range(heads):
            cols = slice(h * width, (h + 1) * width)
            p = probs[h, rows, :]
            grad = grads[:, cols]
            prob_grad = dot(grad, proj[2, :, cols], ((1,), (1,)))
            score_grad = p * (prob_grad - jnp.sum(p * prob_grad, axis=1, keepdims=True))
            diag[h, :, start : start + SEQ_LEN] += score_grad
            low = score_grad.astype(BF16)
            proj_grad[0, rows, cols] = dot(low, proj[1, :, cols]).astype(BF16)
            key_part = dot(low, proj[0, rows, cols], ((0,), (0,)))
            value_part = dot(p.astype(BF16), grad, ((0,), (0,)))
            if j == 0:
                key_acc[:, cols] = key_part
                value_acc[:, cols] = value_part
            else:
                key_acc[:, cols] += key_part
                value_acc[:, cols] += value_part
    proj_grad[1] = key_acc[...].astype(BF16)
    proj_grad[2] = value_acc[...].astype(BF16)
    loads[4].wait()
    loads[5].wait()
    for p in range(2, pieces):
        half = slice((p % 2) * rows_here, (p % 2 + 1) * rows_here)
        dense[p] = dot(normed[:, half], proj_grad[p // 2 - 1], ((0,), (0,))).astype(BF16)
        reduce_start(p)
    half = tokens // 2

    def part_rows(k):
        return pl.ds(k * half, half)

    def pair_copy(d, k):
        return remote(
            part.at[shard(d, 1 - core), part_rows(k), :], mate_in.at[d, part_rows(k), :], part_sems.at[0], (d, k), mate
        )

    def line_copy(d, k):
        return remote(
            line_out.at[d, part_rows(k), :], line_in.at[d, part_rows(k), :], part_sems.at[1], (d, k),
            {"tensor": shard(d, core)},
        )

    for k in range(2):
        rows = slice(k * half, (k + 1) * half)
        total = dot(proj_grad[0, rows, :], w_qkv[0], ((1,), (1,)))
        for n in range(1, 3):
            total = total + dot(proj_grad[n, rows, :], w_qkv[n], ((1,), (1,)))
        low = total.astype(BF16)
        for s in range(shards):
            part[s, rows, :] = low[:, s * share : (s + 1) * share]
        for d in range(lines):
            pair_copy(d, k).start()
    def advance(step):
        for lag, work in enumerate((reduce_y, reduce_half, reduce_block, spread_block, spread_half)):
            if 0 <= step - lag < pieces:
                work(step - lag)

    advance(0)

    def pair_sum(d, rows):
        return part[shard(d, core), rows, :].astype(F32) + mate_in[d, rows, :].astype(F32)

    for k in range(2):
        rows = part_rows(k)
        for d in range(lines):
            landed(mate_in.at[d, rows, :], part_sems.at[0], (d, k))
        for d in range(1, lines):
            line_out[d, rows, :] = pair_sum(d, rows).astype(BF16)
            line_copy(d, k).start()
    for h in range(heads):
        total = diag[h]
        size = TILE // 2
        while size >= 1:
            total = total[:size] + pltpu.roll(total[size : 2 * size], SPAN - size, 1)
            size //= 2
        row = jnp.broadcast_to(total, (8, SPAN))
        high = row.astype(BF16)
        middle = (row - high.astype(F32)).astype(BF16)
        low = (row - high.astype(F32) - middle.astype(F32)).astype(BF16)
        table = dot(high, onehot[...]) + dot(middle, onehot[...]) + dot(low, onehot[...])
        extras[0, experts + 4 + h : experts + 5 + h, : onehot.shape[1]] = table[:1]
    for step in range(1, 4):
        advance(step)

    total = pair_sum(0, pl.ds(0, tokens))
    for k in range(2):
        for d in range(1, lines):
            landed(line_in.at[d, part_rows(k), :], part_sems.at[1], (d, k))
    for d in range(1, lines):
        total = total + line_in[d].astype(F32)
    scale_one = scales[:, 0:1]
    loads[6].wait()
    values = residual[...].astype(F32)
    weighted = total * gain_one[:, mine]
    dot_send(1, jnp.sum(weighted * values, axis=1, keepdims=True))
    extras[0, experts : experts + 1, :] = jnp.sum(total * values * scale_one, axis=0, keepdims=True)

    def extras_copy(i):
        return remote(extras.at[0], extras_in_dp.at[i], extras_sems, (i,), {"dp": group(i)})

    for i in range(1, groups):
        extras_copy(i).start()
    advance(4)
    along = dot_sum(1)
    input_grad[...] = grad_here[...] + scale_one * (weighted - values * (scale_one * scale_one * along * inverse))
    for step in range(5, pieces + 4):
        advance(step)

    summed = extras[0]
    for i in range(1, groups):
        extras_copy(i).wait()
        summed = summed + extras_in_dp[i]
    extras_out[place] = summed

    def ring_copy(i):
        return remote(extras_out.at[place], extras_out.at[place], extras_ring_sems, (i,), {"tensor": near(i)})

    for i in range(1, shards):
        ring_copy(i).start()
    for p in range(pieces):
        spread_y(p)
    for i in range(1, shards):
        landed(extras_out.at[near(shards - i)], extras_ring_sems, (i,))
        ring_copy(i).wait_send()
    for j in range(blocks):
        for d in range(lines):
            if d:
                branch_line(d, j).wait_send()
            branch_mate(d, j).wait_send()
    for k in range(2):
        for d in range(lines):
            if d:
                line_copy(d, k).wait_send()
            pair_copy(d, k).wait_send()
    for p in range(pieces):
        for copy in (half_copy(p), block_copy(p), block_spread(p), half_spread(p)):
            copy.wait_send()
        for a in range(1, y_size):
            y_spread(p, a).wait_send()
        for copy in save(p):
            copy.wait()


def body(
    inputs,
    teacher,
    lengths,
    expert_ids,
    route_slots,
    gain_attn,
    w_qkv,
    w_out,
    rel_table,
    gain_moe,
    w_router,
    w_gate_up,
    w_down,
):
    highest = lax.Precision.HIGHEST
    tok_rows, model_width = inputs.shape
    groups = lax.axis_size("dp")
    shards = lax.axis_size("tensor")
    experts = w_router.shape[1]
    local_experts = w_gate_up.shape[0]
    capacity = 10 * tok_rows // (4 * experts)
    padded_cap = (capacity + 15) // 16 * 16
    slot_count = experts * padded_cap
    heads_here = rel_table.shape[1]
    width_here = w_qkv.shape[2]
    head_width = width_here // heads_here
    share = model_width // shards

    offsets = jnp.arange(SPAN, dtype=jnp.int32) - SEQ_LEN
    onehot_offsets = bucket_onehot(offsets)
    offset_bias = jnp.dot(onehot_offsets, rel_table, precision=highest).T
    lines = shards // 2
    blocks = tok_rows // TILE
    ids = expert_ids.T
    gain_one, gain_two = gain_attn.reshape(1, model_width), gain_moe.reshape(1, model_width)
    router_t = w_router.T
    normed_low, projected, probs, attended, after_mine, normed_mine, columns = staged_call(
        functools.partial(dense_forward, groups, shards, heads_here, head_width, experts),
        "svvvvvaaa",
        (lengths, offset_bias, ids, gain_one, gain_two, router_t, inputs, w_qkv, w_out),
        (
            jax.ShapeDtypeStruct((tok_rows, model_width), BF16),
            jax.ShapeDtypeStruct((3, tok_rows, width_here), BF16),
            jax.ShapeDtypeStruct((heads_here, SEQ_LEN, SEQ_LEN), F32),
            jax.ShapeDtypeStruct((tok_rows, width_here), BF16),
            jax.ShapeDtypeStruct((tok_rows, share), F32),
            jax.ShapeDtypeStruct((tok_rows, share), BF16),
            jax.ShapeDtypeStruct((tok_rows, 128), F32),
        ),
        "aaaavvv",
        [
            pltpu.VMEM((tok_rows, model_width), BF16),
            pltpu.VMEM(w_qkv.shape, BF16),
            pltpu.SemaphoreType.DMA((3,)),
            pltpu.VMEM((shards, width_here, model_width), BF16),
            pltpu.SemaphoreType.DMA((2, 2, lines)),
            pltpu.VMEM((shards, tok_rows, width_here), BF16),
            pltpu.SemaphoreType.DMA((2, 2, lines, blocks)),
            pltpu.VMEM((heads_here, TILE, SPAN), F32),
            pltpu.VMEM((tok_rows, model_width), BF16),
            pltpu.VMEM((3, tok_rows, width_here), BF16),
            pltpu.VMEM((heads_here, SEQ_LEN, SEQ_LEN), F32),
            pltpu.VMEM((TILE, model_width), F32),
            pltpu.VMEM((TILE, model_width), BF16),
            pltpu.SemaphoreType.DMA((4,)),
        ],
        60,
        4,
        "dense_forward",
    )
    kept_route = route_slots < capacity
    target = jnp.where(kept_route, expert_ids * padded_cap + route_slots, -1).T
    gate_up_t = jnp.swapaxes(w_gate_up, 2, 3)
    chunk = max(groups // 4, 1)
    steps = groups // chunk
    slots = groups * padded_cap
    ff_here = w_down.shape[1]
    sizes = (groups, shards, local_experts, padded_cap)
    rows_shape = (shards, local_experts, slots, share)
    extra_rows = experts + 8
    token_type = jax.ShapeDtypeStruct((tok_rows, share), F32)
    block_part, out_grad, normed_two_grad, extras, info, expert_rows, expert_grad, pre_grads, hidden_low = staged_call(
        functools.partial(experts_both, *sizes, chunk, experts),
        "svvvvvvaaa",
        (lengths, normed_mine, after_mine, columns, target, ids, router_t, teacher, gate_up_t, w_down),
        (
            token_type,
            token_type,
            token_type,
            jax.ShapeDtypeStruct((extra_rows, share), F32),
            jax.ShapeDtypeStruct((8, 128), F32),
            jax.ShapeDtypeStruct(rows_shape, BF16),
            jax.ShapeDtypeStruct(rows_shape, BF16),
            jax.ShapeDtypeStruct((2, local_experts, slots, ff_here), BF16),
            jax.ShapeDtypeStruct((local_experts, slots, ff_here), BF16),
        ),
        "vvvvvaaaa",
        [
            pltpu.VMEM((tok_rows, share), BF16),
            pltpu.VMEM(gate_up_t.shape, BF16),
            pltpu.VMEM(w_down.shape, BF16),
            pltpu.VMEM(rows_shape, BF16),
            pltpu.VMEM(rows_shape, BF16),
            pltpu.VMEM(rows_shape, BF16),
            pltpu.VMEM((2, local_experts, slots, ff_here), F32),
            pltpu.VMEM((local_experts, slots, ff_here), BF16),
            pltpu.VMEM((2, local_experts, slots, ff_here), BF16),
            pltpu.VMEM((2, tok_rows, share), F32),
            pltpu.VMEM((2 * tok_rows, share), BF16),
            pltpu.SemaphoreType.DMA((3,)),
            pltpu.SemaphoreType.DMA((4, steps)),
            pltpu.VMEM((groups, 8, 128), jnp.int32),
            pltpu.SemaphoreType.DMA((2, groups)),
            pltpu.VMEM((2, shards, 8, tok_rows), F32),
            pltpu.SemaphoreType.DMA((2, 2, shards)),
        ]
        + mover_scratch(*sizes, share) * 2,
        60,
        1,
        "experts_both",
    )

    y_size = 1 << ((groups.bit_length() - 1) // 2)
    z_size = groups // y_size
    pieces, piece_rows = 2 * (1 + 3), model_width // 2
    dense, out_proj, input_part, extras = staged_call(
        functools.partial(dense_backward, groups, shards, heads_here, head_width, experts),
        "vvvvvvvv" + "aaaaaaa",
        (
            normed_two_grad,
            after_mine,
            out_grad,
            columns,
            gain_one,
            gain_two,
            extras,
            onehot_offsets.astype(BF16),
            inputs,
            attended,
            w_out,
            projected,
            probs,
            normed_low,
            w_qkv,
        ),
        (
            jax.ShapeDtypeStruct((pieces - 2, piece_rows, width_here), BF16),
            jax.ShapeDtypeStruct((width_here, model_width), BF16),
            jax.ShapeDtypeStruct((tok_rows, share), F32),
            jax.ShapeDtypeStruct((shards, extra_rows, share), F32),
        ),
        "aavv",
        [
            pltpu.VMEM((tok_rows, share), BF16),
            pltpu.VMEM(attended.shape, BF16),
            pltpu.VMEM(w_out.shape, BF16),
            pltpu.VMEM(projected.shape, BF16),
            pltpu.VMEM(probs.shape, F32),
            pltpu.VMEM(normed_low.shape, BF16),
            pltpu.VMEM(w_qkv.shape, BF16),
            pltpu.SemaphoreType.DMA((7,)),
            pltpu.VMEM((2, shards, 8, tok_rows), F32),
            pltpu.SemaphoreType.DMA((2, 2, shards)),
            pltpu.VMEM((shards, tok_rows, share), BF16),
            pltpu.SemaphoreType.DMA((2, 2, lines, blocks)),
            pltpu.VMEM((tok_rows, share), F32),
            pltpu.VMEM((heads_here, TILE, SPAN), F32),
            pltpu.VMEM((SEQ_LEN, width_here), F32),
            pltpu.VMEM((SEQ_LEN, width_here), F32),
            pltpu.VMEM((3, tok_rows, width_here), BF16),
            pltpu.VMEM((shards, tok_rows, share), BF16),
            pltpu.VMEM((lines, tok_rows, share), BF16),
            pltpu.VMEM((lines, tok_rows, share), BF16),
            pltpu.VMEM((lines, tok_rows, share), BF16),
            pltpu.SemaphoreType.DMA((2, 2, lines, 2)),
            pltpu.VMEM((pieces, piece_rows, width_here), BF16),
            pltpu.VMEM((pieces, piece_rows, width_here), BF16),
            pltpu.VMEM((pieces, y_size, piece_rows // y_size, width_here), BF16),
            pltpu.VMEM((pieces, piece_rows // y_size, width_here), BF16),
            pltpu.VMEM((pieces, piece_rows // y_size // 2, width_here), BF16),
            pltpu.VMEM((pieces, piece_rows // y_size // 2, width_here), BF16),
            pltpu.VMEM((pieces, piece_rows // groups, width_here), BF16),
            pltpu.SemaphoreType.DMA((2, 2, pieces, y_size)),
            pltpu.SemaphoreType.DMA((2, 2, pieces, 2)),
            pltpu.SemaphoreType.DMA((pieces, max(shards // 2, 1))),
            pltpu.VMEM((1, extra_rows, share), F32),
            pltpu.VMEM((groups, extra_rows, share), F32),
            pltpu.SemaphoreType.DMA((2, groups)),
            pltpu.SemaphoreType.DMA((2, shards)),
        ],
        60,
        3,
        "dense_backward",
    )
    def whole(shape):
        return pl.BlockSpec(shape, lambda e, j: (0,) * len(shape))

    row_type = jax.ShapeDtypeStruct((1, model_width), F32)
    piece = pl.BlockSpec((1, piece_rows, width_here), lambda e, j: (e * 3 + j, 0, 0))
    results = pl.pallas_call(
        functools.partial(weight_grads, shards, heads_here, experts),
        grid=(local_experts, 3),
        out_shape=(
            jax.ShapeDtypeStruct(gate_up_t.shape, F32),
            jax.ShapeDtypeStruct(w_down.shape, F32),
            jax.ShapeDtypeStruct(dense.shape, F32),
            jax.ShapeDtypeStruct(out_proj.shape, F32),
            jax.ShapeDtypeStruct((experts, model_width), F32),
            row_type,
            row_type,
            jax.ShapeDtypeStruct((heads_here, BUCKETS), F32),
            jax.ShapeDtypeStruct((1, 1), F32),
            token_type,
            token_type,
        ),
        in_specs=[
            pl.BlockSpec((shards, None, slots, share), lambda e, j: (0, e, 0, 0)),
            pl.BlockSpec((shards, None, slots, share), lambda e, j: (0, e, 0, 0)),
            pl.BlockSpec((None, None, slots, ff_here), lambda e, j: (jnp.minimum(j, 1), e, 0, 0)),
            pl.BlockSpec((None, slots, ff_here), lambda e, j: (e, 0, 0)),
            piece,
            whole(out_proj.shape),
            whole(extras.shape),
            whole(info.shape),
            whole(token_type.shape),
            whole(token_type.shape),
        ],
        out_specs=(
            pl.BlockSpec((None, None, ff_here, model_width), lambda e, j: (e, jnp.minimum(j, 1), 0, 0)),
            pl.BlockSpec((None, ff_here, model_width), lambda e, j: (e, 0, 0)),
            piece,
            whole(out_proj.shape),
            whole((experts, model_width)),
            whole((1, model_width)),
            whole((1, model_width)),
            whole((heads_here, BUCKETS)),
            whole((1, 1)),
            whole(token_type.shape),
            whole(token_type.shape),
        ),
        compiler_params=pltpu.CompilerParams(vmem_limit_bytes=56 * 1024 * 1024),
        name="weight_grads",
    )(expert_rows, expert_grad, pre_grads, hidden_low, dense, out_proj, extras, info, block_part, input_part)
    gate_up_grad, down_grad, dense_sum, out_proj_sum, router_sum, gain_one_sum, gain_two_sum, table_sum = results[:8]
    loss, block_out, input_grad = results[8:]
    return (
        block_out,
        loss.reshape(()),
        input_grad,
        gain_one_sum.reshape(model_width),
        dense_sum.reshape(w_qkv.shape),
        out_proj_sum,
        table_sum.T,
        gain_two_sum.reshape(model_width),
        router_sum.T,
        jnp.swapaxes(gate_up_grad, 2, 3),
        down_grad,
    )


def solution(mesh):
    placed = (
        P("dp", None),
        P("dp", None),
        P("dp"),
        P("dp", None),
        P("dp", None),
        P(),
        P(None, None, "tensor"),
        P("tensor", None),
        P(None, "tensor"),
        P(),
        P(),
        P("dp", None, None, "tensor"),
        P("dp", "tensor", None),
    )
    return jax.shard_map(
        body,
        mesh=mesh,
        in_specs=placed,
        out_specs=(
            P("dp", "tensor"),
            P(),
            P("dp", "tensor"),
            P(),
            P(None, None, "tensor"),
            P("tensor", None),
            P(None, "tensor"),
            P(),
            P(),
            P("dp", None, None, "tensor"),
            P("dp", "tensor", None),
        ),
        check_vma=False,
    )
```

```python
import functools
import math

import jax
import jax.numpy as jnp
from jax import lax
from jax.experimental import pallas as pl
from jax.experimental.pallas import tpu as pltpu
from jax.sharding import PartitionSpec as P

BUCKETS = 32
SEQ_LEN = 512
TILE = 128
SPAN = 2 * SEQ_LEN

EPSILON = 1e-06
FAR_STEPS = (12, 16, 23, 32, 46, 64, 91)
MASKED = -1000000000.0
F32 = jnp.float32
BF16 = jnp.bfloat16


def offset_bucket(offset):
    direction = jnp.where(offset > 0, 16, 0).astype(jnp.int32)
    distance = jnp.abs(offset)
    farther = jnp.full(offset.shape, 8, jnp.int32)
    for threshold in FAR_STEPS:
        farther = farther + (distance >= threshold).astype(jnp.int32)
    return direction + jnp.where(distance < 8, distance, farther)


def bucket_onehot(offsets):
    bucket_range = jnp.arange(BUCKETS, dtype=jnp.int32)
    return (offset_bucket(offsets)[:, None] == bucket_range[None, :]).astype(F32)


def dot(a, b, dims=((1,), (0,))):
    return lax.dot_general(a, b, (dims, ((), ())), preferred_element_type=F32)


SMEM = pl.BlockSpec(memory_space=pltpu.SMEM)


def staged_call(body, kinds, arrays, out_types, out_kinds, scratch, limit, collective, name):
    staged_in = [n for n, kind in enumerate(kinds) if kind == "v"]
    staged_out = [n for n, kind in enumerate(out_kinds) if kind == "v"]

    def kernel(*refs):
        ins, outs = list(refs[: len(kinds)]), list(refs[len(kinds) : len(kinds) + len(out_kinds)])
        rest = list(refs[len(kinds) + len(out_kinds) :])
        in_sems, out_sems = rest[:2]
        in_bufs = rest[2 : 2 + len(staged_in)]
        out_bufs = rest[2 + len(staged_in) : 2 + len(staged_in) + len(staged_out)]
        rest = rest[2 + len(staged_in) + len(staged_out) :]
        loads = []
        for m, n in enumerate(staged_in):
            loads.append(pltpu.make_async_copy(ins[n], in_bufs[m], in_sems.at[m]))
            ins[n] = in_bufs[m]
        for load in loads:
            load.start()
        results = []
        for m, n in enumerate(staged_out):
            results.append((out_bufs[m], outs[n], out_sems.at[m]))
            outs[n] = out_bufs[m]

        def ready():
            for load in loads:
                load.wait()

        body(ready, *ins, *outs, *rest)
        copies = [pltpu.make_async_copy(*result) for result in results]
        for copy in copies:
            copy.start()
        for copy in copies:
            copy.wait()

    return pl.pallas_call(
        kernel,
        out_shape=tuple(out_types),
        in_specs=[SMEM if kind == "s" else ANY for kind in kinds],
        out_specs=tuple(ANY for _ in out_kinds),
        scratch_shapes=[
            pltpu.SemaphoreType.DMA((max(len(staged_in), 1),)),
            pltpu.SemaphoreType.DMA((max(len(staged_out), 1),)),
        ]
        + [pltpu.VMEM(arrays[n].shape, arrays[n].dtype) for n in staged_in]
        + [pltpu.VMEM(out_types[n].shape, out_types[n].dtype) for n in staged_out]
        + scratch,
        compiler_params=pltpu.CompilerParams(
            vmem_limit_bytes=limit * 1024 * 1024, collective_id=collective, has_side_effects=True
        ),
        name=name,
    )(*arrays)


MESH_ID = pl.DeviceIdType.MESH
ANY = pl.BlockSpec(memory_space=pltpu.HBM)


def weight_grads(
    shards, heads, experts,
    rows, grads, side, hidden, dense, out_proj, extras, info, block_in, input_in,
    gate_up_out, down_out, dense_out, out_proj_out, router_out, gain_one_out, gain_two_out, table_out, loss_out,
    block_out, input_out,
):
    step = pl.program_id(1)
    at = pl.program_id(0) * 3 + step
    share = rows.shape[-1]

    @pl.when(at == 0)
    def _():
        block_out[...] = block_in[...]
        input_out[...] = input_in[...]
        out_proj_out[...] = out_proj[...].astype(F32)
        for s in range(shards):
            cols = slice(s * share, (s + 1) * share)
            router_out[:, cols] = extras[s, :experts, :]
            gain_one_out[:, cols] = extras[s, experts : experts + 1, :]
            gain_two_out[:, cols] = extras[s, experts + 1 : experts + 2, :]
        table_out[...] = extras[lax.axis_index("tensor"), experts + 4 : experts + 4 + heads, :BUCKETS]
        squares = sum(extras[s, experts + 2 : experts + 3, :] for s in range(shards))
        model = share * shards
        loss_out[...] = jnp.sum(squares, axis=1, keepdims=True) / (2.0 * info[0:1, 0:1] * model)

    dense_out[...] = dense[...].astype(F32)

    @pl.when(step < 2)
    def _():
        for s in range(shards):
            gate_up_out[:, s * share : (s + 1) * share] = dot(side[...], rows[s], ((0,), (0,)))

    @pl.when(step == 2)
    def _():
        for s in range(shards):
            down_out[:, s * share : (s + 1) * share] = dot(hidden[...], grads[s], ((0,), (0,)))


def to_row(column):
    rows = column.shape[0]
    return jnp.transpose(jnp.broadcast_to(column, (rows, 128)))[:8]


def to_column(row):
    return jnp.transpose(jnp.broadcast_to(row[:1], (128, row.shape[1])))[:, :1]


def flip(value, mask, size):
    total, unit = 0, 1
    while unit < size:
        bit = lax.rem(lax.div(value, unit), 2)
        total = total + unit * ((1 - bit) if mask & unit else bit)
        unit *= 2
    return total


def plan(groups, chunk):
    kinds = ("spread", "relay", "products", "along", "give", "taken")
    steps = []
    for step in range(groups // chunk + len(kinds) - 1):
        for lag, kind in enumerate(kinds):
            k = step - lag
            if 0 <= k < groups // chunk:
                steps += [(kind, k)] if kind == "products" else [(kind, k * chunk + n) for n in range(chunk)]
    return steps


class Mover:
    def __init__(self, groups, shards, cap, chunk, rows, part, scratch):
        self.groups, self.lines, self.cap, self.chunk = groups, shards // 2, cap, chunk
        self.rows, self.part = rows, part
        (
            self.source, self.mate_in, self.line_out, self.line_in, self.back_out, self.back,
            self.dp_sems, self.row_sems, self.sum_sems,
        ) = scratch
        self.me, self.place = lax.axis_index("dp"), lax.axis_index("tensor")
        self.line, self.core = lax.div(self.place, 2), lax.rem(self.place, 2)
        self.steps = groups // chunk

    def peer(self, i):
        return flip(self.me, i, self.groups)

    def shard(self, offset, core):
        return lax.rem(self.line + offset, self.lines) * 2 + core

    def near(self, i):
        return lax.rem(self.place + i, 2 * self.lines)

    def remote(self, src, dst, sems, index, device):
        return pltpu.make_async_remote_copy(
            src_ref=src, dst_ref=dst, send_sem=sems.at[(0, *index)], recv_sem=sems.at[(1, *index)],
            device_id=device, device_id_type=MESH_ID,
        )

    def mate(self):
        return {"tensor": self.shard(0, 1 - self.core)}

    def landed(self, where, sems, index):
        self.remote(where, where, sems, index, self.mate()).wait_recv()

    def here(self, shard, i):
        return self.rows.at[shard, :, pl.ds(i * self.cap, self.cap), :]

    def send(self, i, block):
        block = block.reshape(-1, self.cap, block.shape[-1])
        if i == 0:
            self.rows[self.place, :, : self.cap, :] = block
        else:
            self.source[i] = block
            self.out_copy(i).start()

    def out_copy(self, i):
        return self.remote(
            self.source.at[i], self.here(self.place, i), self.dp_sems.at[0], (i,), {"dp": self.peer(i)}
        )

    def line_copy(self, d, i):
        return self.remote(
            self.here(self.place, i), self.here(self.place, i), self.row_sems.at[0], (d, i),
            {"tensor": self.shard(d, self.core)},
        )

    def mate_copy(self, d, i):
        shard = self.shard(self.lines - d, self.core)
        return self.remote(self.here(shard, i), self.here(shard, i), self.row_sems.at[1], (d, i), self.mate())

    def places(self, k):
        return range(k * self.chunk, (k + 1) * self.chunk)

    def spread(self, i):
        if i:
            self.landed(self.here(self.place, i), self.dp_sems.at[0], (i,))
        for d in range(1, self.lines):
            self.line_copy(d, i).start()
        self.mate_copy(0, i).start()

    def relay(self, i):
        for d in range(1, self.lines):
            shard = self.shard(self.lines - d, self.core)
            self.landed(self.here(shard, i), self.row_sems.at[0], (d, i))
            self.mate_copy(d, i).start()

    def collect(self, i):
        for d in range(self.lines):
            shard = self.shard(self.lines - d, 1 - self.core)
            self.landed(self.here(shard, i), self.row_sems.at[1], (d, i))

    def span(self, k):
        return pl.ds(k * self.chunk * self.cap, self.chunk * self.cap)

    def block(self, i):
        return pl.ds(i * self.cap, self.cap)

    def pair_copy(self, d, i):
        shard = self.shard(d, 1 - self.core)
        return self.remote(
            self.part.at[shard, :, self.block(i), :], self.mate_in.at[d, :, self.block(i), :], self.sum_sems.at[0], (d, i),
            self.mate(),
        )

    def sum_copy(self, d, i):
        return self.remote(
            self.line_out.at[d - 1, :, self.block(i), :], self.line_in.at[d - 1, :, self.block(i), :],
            self.sum_sems.at[1], (d, i), {"tensor": self.shard(d, self.core)},
        )

    def back_copy(self, i):
        return self.remote(
            self.back_out.at[:, self.block(i), :], self.back.at[i], self.dp_sems.at[1], (i,), {"dp": self.peer(i)}
        )

    def pair(self, k):
        for i in self.places(k):
            for d in range(self.lines):
                self.pair_copy(d, i).start()

    def pair_sum(self, d, i):
        shard = self.shard(d, self.core)
        return self.part[shard, :, self.block(i), :].astype(F32) + self.mate_in[d, :, self.block(i), :].astype(F32)

    def along(self, i):
        for d in range(self.lines):
            self.landed(self.mate_in.at[d, :, self.block(i), :], self.sum_sems.at[0], (d, i))
        for d in range(1, self.lines):
            self.line_out[d - 1, :, self.block(i), :] = self.pair_sum(d, i).astype(BF16)
            self.sum_copy(d, i).start()

    def give(self, i):
        total = self.pair_sum(0, i)
        for d in range(1, self.lines):
            self.landed(self.line_in.at[d - 1, :, self.block(i), :], self.sum_sems.at[1], (d, i))
            total = total + self.line_in[d - 1, :, self.block(i), :].astype(F32)
        total = total.astype(BF16)
        if i == 0:
            self.back[0] = total
        else:
            self.back_out[:, self.block(i), :] = total
            self.back_copy(i).start()

    def arrived(self, i):
        if i:
            self.landed(self.back.at[i], self.dp_sems.at[1], (i,))
        return self.back[i].reshape(-1, self.back.shape[-1])

    def run(self, compute, take):
        def products(k):
            for i in self.places(k):
                self.collect(i)
            compute(k)
            self.pair(k)

        def taken(i):
            take(i, self.arrived(i))

        works = dict(
            spread=self.spread, relay=self.relay, products=products, along=self.along, give=self.give, taken=taken
        )
        for work, index in plan(self.groups, self.chunk):
            works[work](index)

    def finish(self):
        for i in range(1, self.groups):
            self.out_copy(i).wait_send()
            self.back_copy(i).wait_send()
        for i in range(self.groups):
            for d in range(self.lines):
                if d:
                    self.line_copy(d, i).wait_send()
                    self.sum_copy(d, i).wait_send()
                self.mate_copy(d, i).wait_send()
                self.pair_copy(d, i).wait_send()


def mover_scratch(groups, shards, local, cap, share):
    lines, slots = shards // 2, groups * cap
    return [
        pltpu.VMEM((groups, local, cap, share), BF16),
        pltpu.VMEM((lines, local, slots, share), BF16),
        pltpu.VMEM((lines - 1, local, slots, share), BF16),
        pltpu.VMEM((lines - 1, local, slots, share), BF16),
        pltpu.VMEM((local, slots, share), BF16),
        pltpu.VMEM((groups, local, cap, share), BF16),
        pltpu.SemaphoreType.DMA((2, 2, groups)),
        pltpu.SemaphoreType.DMA((2, 2, lines, groups)),
        pltpu.SemaphoreType.DMA((2, 2, lines, groups)),
    ]


MOVER_REFS = 9
ROOT = math.sqrt(2.0 / math.pi)


def gelu_parts(v):
    inner = jnp.tanh(ROOT * (v + 0.044715 * (v * v * v)))
    half = 0.5 * (1.0 + inner)
    slope = half + 0.5 * v * (1.0 - inner * inner) * (ROOT * (1.0 + 3.0 * 0.044715 * v * v))
    return v * half, slope


def experts_both(
    groups, shards, local, cap, chunk, experts, kept,
    ready, len_ref, normed, after, columns, slots_ref, ids_ref, router,
    teacher_hbm, gate_up_hbm, down_hbm,
    block_out, out_grad, norm_grad, extras, info,
    rows_hbm, grads_hbm, side_hbm, hidden_hbm,
    teacher, gate_up, down, rows, grads, part, pre, hidden, side, routed, gated, load_sems, save_sems,
    counts, count_sems, dots, dot_sems, *scratch,
):
    ahead = Mover(groups, shards, cap, chunk, rows, part, scratch[:MOVER_REFS])
    behind = Mover(groups, shards, cap, chunk, grads, part, scratch[MOVER_REFS:])
    tokens, share = normed.shape
    width = local * cap
    place = ahead.place
    mine = pl.ds(pl.multiple_of(place * share, 128), share)
    loads = [
        pltpu.make_async_copy(gate_up_hbm, gate_up, load_sems.at[0]),
        pltpu.make_async_copy(down_hbm, down, load_sems.at[1]),
        pltpu.make_async_copy(teacher_hbm.at[:, mine], teacher, load_sems.at[2]),
    ]
    for load in loads:
        load.start()

    barrier = pltpu.get_barrier_semaphore()
    for i in range(1, groups):
        pl.semaphore_signal(barrier, inc=1, device_id={"dp": ahead.peer(i)}, device_id_type=MESH_ID)
    for i in range(1, shards):
        pl.semaphore_signal(barrier, inc=1, device_id={"tensor": ahead.near(i)}, device_id_type=MESH_ID)
    counts[0] = jnp.full((8, 128), len_ref[0], jnp.int32)
    slot_lines = lax.broadcasted_iota(jnp.int32, (width, tokens), 0)
    slot_lanes = lax.broadcasted_iota(jnp.int32, (tokens, width), 1)
    ready()
    targets = jnp.where(slots_ref[...] < kept, ids_ref[...] * cap + slots_ref[...], -1)
    row_targets = [targets[n : n + 1, :] for n in range(2)]
    column_targets = [to_column(target.astype(F32)).astype(jnp.int32) for target in row_targets]

    def by_slot(i, n):
        return slot_lines + ahead.peer(i) * width == row_targets[n]

    def by_token(i, n):
        return slot_lanes + ahead.peer(i) * width == column_targets[n]

    def ones(mask):
        return jnp.where(mask, 1.0, 0.0).astype(BF16)

    pl.semaphore_wait(barrier, groups + shards - 2)

    def count_copy(i):
        return ahead.remote(counts.at[0], counts.at[i], count_sems, (i,), {"dp": ahead.peer(i)})

    order = [*range(1, groups), 0]
    for i in order:
        ahead.send(i, dot(ones(by_slot(i, 0) | by_slot(i, 1)), normed[...]).astype(BF16))
    for i in range(1, groups):
        count_copy(i).start()

    def forward_saves(k):
        span = ahead.span(k)
        return [
            pltpu.make_async_copy(rows.at[:, :, span, :], rows_hbm.at[:, :, span, :], save_sems.at[0, k]),
            pltpu.make_async_copy(hidden.at[:, span, :], hidden_hbm.at[:, span, :], save_sems.at[1, k]),
        ]

    def backward_saves(k):
        span = ahead.span(k)
        return [
            pltpu.make_async_copy(grads.at[:, :, span, :], grads_hbm.at[:, :, span, :], save_sems.at[2, k]),
            pltpu.make_async_copy(side.at[:, :, span, :], side_hbm.at[:, :, span, :], save_sems.at[3, k]),
        ]

    def put(e, span, result):
        result = result.astype(BF16)
        for s in range(shards):
            part[s, e, span, :] = result[:, s * share : (s + 1) * share]

    def forward(k):
        span = ahead.span(k)
        if k == 0:
            loads[0].wait()
            loads[1].wait()
        for e in range(local):
            lhs = jnp.concatenate([rows[s, e, span, :] for s in range(shards)], axis=1)
            gate = dot(lhs, gate_up[e, 0], ((1,), (1,)))
            up = dot(lhs, gate_up[e, 1], ((1,), (1,)))
            pre[0, e, span, :] = gate
            pre[1, e, span, :] = up
            low = (gelu_parts(gate)[0] * up).astype(BF16)
            hidden[e, span, :] = low
            put(e, span, dot(low, down[e]))
        for save in forward_saves(k):
            save.start()

    def take(i, block):
        for n in range(2):
            value = dot(ones(by_token(i, n)), block)
            if i == 0:
                routed[n] = value
            else:
                routed[n] += value

    ahead.run(forward, take)

    tally = counts[0]
    for i in range(1, groups):
        count_copy(i).wait()
        tally = tally + counts[i]
    valid = tally.astype(F32)
    loads[2].wait()
    gates = [columns[:, 2:3], columns[:, 3:4]]
    output = after[...] + gates[0] * routed[0] + gates[1] * routed[1]
    block_out[...] = output
    alive = lax.broadcasted_iota(jnp.int32, (tokens, share), 0) < len_ref[0]
    deviation = jnp.where(alive, output - teacher[...].astype(F32), 0.0)
    scaled = deviation * (groups * tokens / valid[0:1, 0:1])
    out_grad[...] = scaled
    for n in range(2):
        gated[n * tokens : (n + 1) * tokens, :] = (gates[n] * scaled).astype(BF16)
    for i in order:
        both = jnp.concatenate([ones(by_slot(i, 0)), ones(by_slot(i, 1))], axis=1)
        behind.send(i, dot(both, gated[...]).astype(BF16))
    for n in range(2):
        dots[n, 0] = to_row(jnp.sum(routed[n] * scaled, axis=1, keepdims=True))

    def dot_copy(n, i):
        return ahead.remote(dots.at[n, 0], dots.at[n, i], dot_sems, (n, i), {"tensor": ahead.near(i)})

    for n in range(2):
        for i in range(1, shards):
            dot_copy(n, i).start()
    info[...] = valid
    extras[...] = jnp.zeros_like(extras)
    extras[experts + 2 : experts + 3, :] = jnp.sum(deviation * deviation, axis=0, keepdims=True)
    ahead.finish()

    def route_grads():
        parts = []
        for n in range(2):
            total = dots[n, 0]
            for i in range(1, shards):
                dot_copy(n, i).wait()
                total = total + dots[n, i]
            parts.append(to_column(total))
        expert_probs = columns[:, 16 : 16 + experts]
        lanes = lax.broadcasted_iota(jnp.int32, (tokens, experts), 1)
        picks = [
            jnp.where(lanes == to_column(ids_ref[n : n + 1, :].astype(F32)).astype(jnp.int32), 1.0, 0.0)
            for n in range(2)
        ]
        chosen_total = jnp.sum(expert_probs * (picks[0] + picks[1]), axis=1, keepdims=True)
        along = parts[0] * gates[0] + parts[1] * gates[1]
        probs_grad = sum(picks[n] * ((parts[n] - along) / chosen_total) for n in range(2))
        logit_grad = expert_probs * (probs_grad - jnp.sum(probs_grad * expert_probs, axis=1, keepdims=True))
        logit_grad = logit_grad.astype(BF16)
        extras[0:experts, :] = dot(logit_grad, normed[...], ((0,), (0,)))
        norm_grad[...] = dot(logit_grad, router[:, mine])

    def backward(k):
        span = ahead.span(k)
        for e in range(local):
            lhs = jnp.concatenate([grads[s, e, span, :] for s in range(shards)], axis=1)
            hidden_grad = dot(lhs, down[e], ((1,), (1,)))
            activated, slope = gelu_parts(pre[0, e, span, :])
            gate_side = (hidden_grad * pre[1, e, span, :] * slope).astype(BF16)
            up_side = (hidden_grad * activated).astype(BF16)
            side[0, e, span, :] = gate_side
            side[1, e, span, :] = up_side
            put(e, span, dot(gate_side, gate_up[e, 0]) + dot(up_side, gate_up[e, 1]))
        for save in backward_saves(k):
            save.start()
        if k == 0:
            route_grads()

    def take_back(i, block):
        norm_grad[...] += dot(ones(by_token(i, 0) | by_token(i, 1)), block)

    behind.run(backward, take_back)
    behind.finish()
    for k in range(ahead.steps):
        for save in forward_saves(k) + backward_saves(k):
            save.wait()


def gate_columns(logits, first, second):
    lanes = lax.broadcasted_iota(jnp.int32, logits.shape, 1)
    exponent = jnp.exp(logits - jnp.max(logits, axis=1, keepdims=True))
    expert_probs = exponent / jnp.sum(exponent, axis=1, keepdims=True)
    chosen = [jnp.sum(jnp.where(lanes == pick, expert_probs, 0.0), axis=1, keepdims=True) for pick in (first, second)]
    total = chosen[0] + chosen[1]
    return expert_probs, chosen[0] / total, chosen[1] / total


def dense_forward(
    groups, shards, heads, width, experts,
    ready, len_ref, bias_ref, ids_ref, gain_one, gain_two, router_ref,
    inputs_hbm, w_qkv_hbm, w_out_hbm,
    normed_out, proj_out, probs_out, attended_out, after_out, normed_two_out, columns_out,
    inputs, w_qkv, load_sems, w_out, w_sems, attended, attended_sems, skew, normed, proj, probs, after, normed_two, save_sems,
):
    tokens, model = inputs.shape
    here = heads * width
    share = model // shards
    lines = shards // 2
    blocks = tokens // TILE
    place = lax.axis_index("tensor")
    line, core = lax.div(place, 2), lax.rem(place, 2)
    mate = {"tensor": line * 2 + 1 - core}

    def shard(d, c):
        return lax.rem(line + d, lines) * 2 + c

    def remote(src, dst, sems, index, device):
        return pltpu.make_async_remote_copy(
            src_ref=src, dst_ref=dst, send_sem=sems.at[(0, *index)], recv_sem=sems.at[(1, *index)],
            device_id=device, device_id_type=MESH_ID,
        )

    def landed(where, sems, index):
        remote(where, where, sems, index, mate).wait_recv()

    loads = [
        pltpu.make_async_copy(inputs_hbm, inputs, load_sems.at[0]),
        pltpu.make_async_copy(w_qkv_hbm, w_qkv, load_sems.at[1]),
        pltpu.make_async_copy(w_out_hbm, w_out.at[place], load_sems.at[2]),
    ]
    for load in loads:
        load.start()
    barrier = pltpu.get_barrier_semaphore()
    for d in range(1, lines):
        pl.semaphore_signal(barrier, inc=1, device_id={"tensor": shard(d, core)}, device_id_type=MESH_ID)
    pl.semaphore_signal(barrier, inc=1, device_id=mate, device_id_type=MESH_ID)
    pl.semaphore_wait(barrier, lines)

    def w_line(d):
        return remote(w_out.at[place], w_out.at[place], w_sems.at[0], (d,), {"tensor": shard(d, core)})

    def w_mate(d):
        where = w_out.at[shard(lines - d, core)]
        return remote(where, where, w_sems.at[1], (d,), mate)

    def row_block(j):
        return pl.ds(j * TILE, TILE)

    def rows_line(d, j):
        where = attended.at[place, row_block(j), :]
        return remote(where, where, attended_sems.at[0], (d, j), {"tensor": shard(d, core)})

    def rows_mate(d, j):
        where = attended.at[shard(lines - d, core), row_block(j), :]
        return remote(where, where, attended_sems.at[1], (d, j), mate)

    ready()
    loads[2].wait()
    for d in range(1, lines):
        w_line(d).start()
    w_mate(0).start()

    loads[0].wait()
    for j in range(blocks):
        rows = slice(j * TILE, (j + 1) * TILE)
        values = inputs[rows, :].astype(F32)
        scale = lax.rsqrt(jnp.mean(values * values, axis=1, keepdims=True) + EPSILON)
        columns_out[rows, 0:1] = scale
        normed[rows, :] = (values * scale * gain_one[...]).astype(BF16)
    loads[1].wait()
    for n in range(3):
        proj[n] = dot(normed[...], w_qkv[n]).astype(BF16)
    saves = [
        pltpu.make_async_copy(normed, normed_out, save_sems.at[0]),
        pltpu.make_async_copy(proj, proj_out, save_sems.at[1]),
    ]
    for h in range(heads):
        skew[h] = pltpu.roll(
            jnp.broadcast_to(bias_ref[h : h + 1, :], (TILE, SPAN)), 0, 1, stride=1, stride_axis=0
        )
    for item in saves:
        item.start()

    alive = lax.broadcasted_iota(jnp.int32, (TILE, SEQ_LEN), 1) < len_ref[0]
    for j in range(blocks):
        rows = slice(j * TILE, (j + 1) * TILE)
        start = SEQ_LEN - j * TILE
        for h in range(heads):
            cols = slice(h * width, (h + 1) * width)
            scores = dot(proj[0, rows, cols], proj[1, :, cols], ((1,), (1,)))
            scores = jnp.where(alive, scores + skew[h, :, start : start + SEQ_LEN], MASKED)
            exponent = jnp.exp(scores - jnp.max(scores, axis=1, keepdims=True))
            weights = exponent * (1.0 / jnp.sum(exponent, axis=1, keepdims=True))
            probs[h, rows, :] = weights
            attended[place, rows, cols] = dot(weights.astype(BF16), proj[2, :, cols]).astype(BF16)
        for d in range(1, lines):
            rows_line(d, j).start()
        rows_mate(0, j).start()
        if j == blocks - 2:
            for d in range(1, lines):
                landed(w_out.at[shard(lines - d, core)], w_sems.at[0], (d,))
                w_mate(d).start()
    saves += [
        pltpu.make_async_copy(probs, probs_out, save_sems.at[2]),
        pltpu.make_async_copy(attended.at[place], attended_out, save_sems.at[3]),
    ]
    for item in saves[2:]:
        item.start()

    ids = ids_ref[...].astype(F32)
    picks = [to_column(ids[n : n + 1]).astype(jnp.int32) for n in range(2)]

    def relay(j):
        for d in range(1, lines):
            landed(attended.at[shard(lines - d, core), row_block(j), :], attended_sems.at[0], (d, j))
            rows_mate(d, j).start()

    relay(0)
    for d in range(lines):
        landed(w_out.at[shard(lines - d, 1 - core)], w_sems.at[1], (d,))
    for j in range(blocks):
        rows = slice(j * TILE, (j + 1) * TILE)
        if j + 1 < blocks:
            relay(j + 1)
        for d in range(lines):
            landed(attended.at[shard(lines - d, 1 - core), row_block(j), :], attended_sems.at[1], (d, j))
        total = inputs[rows, :].astype(F32)
        for s in range(shards):
            total = total + dot(attended[s, rows, :], w_out[s])
        scale = lax.rsqrt(jnp.mean(total * total, axis=1, keepdims=True) + EPSILON)
        low = (total * scale * gain_two[...]).astype(BF16)
        after[...] = total
        normed_two[...] = low
        mine = pl.ds(pl.multiple_of(place * share, 128), share)
        after_out[rows, :] = after[:, mine]
        normed_two_out[rows, :] = normed_two[:, mine]
        expert_probs, first, second = gate_columns(
            dot(low, router_ref[...], ((1,), (1,))), picks[0][rows], picks[1][rows]
        )
        columns_out[rows, 1:2] = scale
        columns_out[rows, 2:3] = first
        columns_out[rows, 3:4] = second
        columns_out[rows, 16 : 16 + experts] = expert_probs
    for d in range(lines):
        if d:
            w_line(d).wait_send()
        w_mate(d).wait_send()
        for j in range(blocks):
            if d:
                rows_line(d, j).wait_send()
            rows_mate(d, j).wait_send()
    for item in saves:
        item.wait()


def dense_backward(
    groups, shards, heads, width, experts,
    ready, norm_grad, after, out_grad, scales, gain_one, gain_two, extras_in, onehot,
    inputs_hbm, attended_hbm, w_out_hbm, proj_hbm, probs_hbm, normed_hbm, w_qkv_hbm,
    dense_out, out_proj_out, input_grad, extras_out,
    residual, attended, w_out, proj, probs, normed, w_qkv, load_sems,
    dots, dot_sems, branch, branch_sems, grad_here, diag, key_acc, value_acc, proj_grad,
    part, mate_in, line_out, line_in, part_sems,
    dense, result, y_in, y_sum, half_in, half_sum, block_in, dense_sems, z_sems, save_sems,
    extras, extras_in_dp, extras_sems, extras_ring_sems,
):
    model = normed.shape[1]
    share = branch.shape[-1]
    tokens = branch.shape[1]
    here = heads * width
    lines = shards // 2
    y_size = 1 << ((groups.bit_length() - 1) // 2)
    z_size = groups // y_size
    pieces = dense.shape[0]
    me, place = lax.axis_index("dp"), lax.axis_index("tensor")
    line, core = lax.div(place, 2), lax.rem(place, 2)
    z, y = lax.div(me, y_size), lax.rem(me, y_size)
    mate = {"tensor": line * 2 + 1 - core}
    inverse = 1.0 / model
    mine = pl.ds(pl.multiple_of(place * share, 128), share)

    def group(i):
        return lax.rem(me + i, groups)

    def shard(d, c):
        return lax.rem(line + d, lines) * 2 + c

    def near(i):
        return lax.rem(place + i, shards)

    def remote(src, dst, sems, index, device):
        return pltpu.make_async_remote_copy(
            src_ref=src, dst_ref=dst, send_sem=sems.at[(0, *index)], recv_sem=sems.at[(1, *index)],
            device_id=device, device_id_type=MESH_ID,
        )

    def landed(where, sems, index):
        remote(where, where, sems, index, mate).wait_recv()

    loads = [
        pltpu.make_async_copy(src, dst, load_sems.at[n])
        for n, (src, dst) in enumerate(
            (
                (w_out_hbm, w_out), (attended_hbm, attended), (proj_hbm, proj), (probs_hbm, probs),
                (w_qkv_hbm, w_qkv), (normed_hbm, normed), (inputs_hbm.at[:, mine], residual),
            )
        )
    ]
    for load in loads:
        load.start()

    barrier = pltpu.get_barrier_semaphore()
    for i in range(1, groups):
        pl.semaphore_signal(barrier, inc=1, device_id={"dp": group(i)}, device_id_type=MESH_ID)
    for i in range(1, shards):
        pl.semaphore_signal(barrier, inc=1, device_id={"tensor": near(i)}, device_id_type=MESH_ID)
    def dot_copy(n, i):
        return remote(dots.at[n, 0], dots.at[n, i], dot_sems, (n, i), {"tensor": near(i)})

    def dot_send(n, column):
        dots[n, 0] = to_row(column)
        if n == 0:
            pl.semaphore_wait(barrier, groups + shards - 2)
        for i in range(1, shards):
            dot_copy(n, i).start()

    def dot_sum(n):
        total = dots[n, 0]
        for i in range(1, shards):
            dot_copy(n, i).wait()
            total = total + dots[n, i]
        return to_column(total)

    ready()
    scale_two = scales[:, 1:2]
    weighted = norm_grad[...] * gain_two[:, mine]
    dot_send(0, jnp.sum(weighted * after[...], axis=1, keepdims=True))
    extras[0] = extras_in[...]
    extras[0, experts + 1 : experts + 2, :] = jnp.sum(norm_grad[...] * after[...] * scale_two, axis=0, keepdims=True)
    along = dot_sum(0)
    after_grad = out_grad[...] + scale_two * (weighted - after[...] * (scale_two * scale_two * along * inverse))
    grad_here[...] = after_grad
    branch[place] = after_grad.astype(BF16)

    blocks = tokens // TILE

    def row_block(j):
        return pl.ds(j * TILE, TILE)

    def branch_line(d, j):
        where = branch.at[place, row_block(j), :]
        return remote(where, where, branch_sems.at[0], (d, j), {"tensor": shard(d, core)})

    def branch_mate(d, j):
        where = branch.at[shard(lines - d, core), row_block(j), :]
        return remote(where, where, branch_sems.at[1], (d, j), mate)

    for j in range(blocks):
        for d in range(1, lines):
            branch_line(d, j).start()
        branch_mate(0, j).start()
    for j in range(blocks):
        for d in range(1, lines):
            landed(branch.at[shard(lines - d, core), row_block(j), :], branch_sems.at[0], (d, j))
            branch_mate(d, j).start()
    def branch_landed(j):
        for d in range(lines):
            landed(branch.at[shard(lines - d, 1 - core), row_block(j), :], branch_sems.at[1], (d, j))

    rows_here = dense.shape[1]
    y_rows, z_rows = rows_here // y_size, rows_here // groups

    def y_copy(p, a):
        to = lax.rem(y + a, y_size)
        return remote(
            dense.at[p, pl.ds(to * y_rows, y_rows), :], y_in.at[p, a], dense_sems.at[0], (p, a), {"dp": z * y_size + to}
        )

    z_low, z_high = lax.rem(z, 2), lax.div(z, 2)
    half_rows = y_rows // 2
    kept_half, kept_block = y * y_rows + z_low * half_rows, y * y_rows + z_low * half_rows + z_high * z_rows
    near_z = {"dp": (z_high * 2 + 1 - z_low) * y_size + y}
    far_z = {"dp": ((1 - z_high) * 2 + z_low) * y_size + y}

    def half_copy(p):
        return remote(
            y_sum.at[p, pl.ds((1 - z_low) * half_rows, half_rows), :], half_in.at[p], z_sems.at[0], (p, 0), near_z
        )

    def block_copy(p):
        return remote(
            half_sum.at[p, pl.ds((1 - z_high) * z_rows, z_rows), :], block_in.at[p], z_sems.at[0], (p, 1), far_z
        )

    def block_spread(p):
        where = result.at[p, pl.ds(kept_block, z_rows), :]
        return remote(where, where, z_sems.at[1], (p, 1), far_z)

    def half_spread(p):
        where = result.at[p, pl.ds(kept_half, half_rows), :]
        return remote(where, where, z_sems.at[1], (p, 0), near_z)

    def y_spread(p, a):
        to = lax.rem(y + a, y_size)
        where = result.at[p, pl.ds(y * y_rows, y_rows), :]
        return remote(where, where, dense_sems.at[1], (p, a), {"dp": z * y_size + to})

    def reduce_start(p):
        for a in range(1, y_size):
            y_copy(p, a).start()

    def reduce_y(p):
        total = dense[p, pl.ds(y * y_rows, y_rows), :].astype(F32)
        for a in range(1, y_size):
            landed(y_in.at[p, a], dense_sems.at[0], (p, a))
            total = total + y_in[p, a].astype(F32)
        y_sum[p] = total.astype(BF16)
        half_copy(p).start()

    def reduce_half(p):
        for a in range(1, y_size):
            y_copy(p, a).wait_send()
        landed(half_in.at[p], z_sems.at[0], (p, 0))
        mine_half = y_sum[p, pl.ds(z_low * half_rows, half_rows), :].astype(F32)
        half_sum[p] = (mine_half + half_in[p].astype(F32)).astype(BF16)
        block_copy(p).start()

    def reduce_block(p):
        landed(block_in.at[p], z_sems.at[0], (p, 1))
        mine_block = half_sum[p, pl.ds(z_high * z_rows, z_rows), :].astype(F32)
        result[p, pl.ds(kept_block, z_rows), :] = (mine_block + block_in[p].astype(F32)).astype(BF16)
        block_spread(p).start()

    def spread_block(p):
        landed(result.at[p, pl.ds(kept_half + (1 - z_high) * z_rows, z_rows), :], z_sems.at[1], (p, 1))
        half_spread(p).start()

    def spread_half(p):
        landed(result.at[p, pl.ds(y * y_rows + (1 - z_low) * half_rows, half_rows), :], z_sems.at[1], (p, 0))
        for a in range(1, y_size):
            y_spread(p, a).start()

    per_piece = shards // 2

    def save(p):
        if p >= 2:
            return [pltpu.make_async_copy(result.at[p], dense_out.at[p - 2], save_sems.at[p, 0])]
        return [
            pltpu.make_async_copy(
                result.at[p, pl.ds(n * here, here), :],
                out_proj_out.at[:, pl.ds((p * per_piece + n) * here, here)],
                save_sems.at[p, n],
            )
            for n in range(per_piece)
        ]

    def spread_y(p):
        for a in range(1, y_size):
            origin = lax.rem(y + y_size - a, y_size)
            landed(result.at[p, pl.ds(origin * y_rows, y_rows), :], dense_sems.at[1], (p, a))
        for copy in save(p):
            copy.start()

    def out_projection():
        loads[1].wait()
        for s in range(shards):
            n = s % per_piece
            dense[s // per_piece, n * here : (n + 1) * here, :] = dot(
                attended[...], branch[s], ((0,), (0,))
            ).astype(BF16)
        for p in range(2):
            reduce_start(p)

    loads[0].wait()
    loads[2].wait()
    loads[3].wait()
    diag[...] = jnp.zeros_like(diag)
    for j in range(blocks):
        rows = slice(j * TILE, (j + 1) * TILE)
        start = SEQ_LEN - j * TILE
        branch_landed(j)
        if j == blocks - 1:
            out_projection()
        wide = jnp.concatenate([branch[s, rows, :] for s in range(shards)], axis=1)
        grads = dot(wide, w_out[...], ((1,), (1,))).astype(BF16)
        for h in range(heads):
            cols = slice(h * width, (h + 1) * width)
            p = probs[h, rows, :]
            grad = grads[:, cols]
            prob_grad = dot(grad, proj[2, :, cols], ((1,), (1,)))
            score_grad = p * (prob_grad - jnp.sum(p * prob_grad, axis=1, keepdims=True))
            diag[h, :, start : start + SEQ_LEN] += score_grad
            low = score_grad.astype(BF16)
            proj_grad[0, rows, cols] = dot(low, proj[1, :, cols]).astype(BF16)
            key_part = dot(low, proj[0, rows, cols], ((0,), (0,)))
            value_part = dot(p.astype(BF16), grad, ((0,), (0,)))
            if j == 0:
                key_acc[:, cols] = key_part
                value_acc[:, cols] = value_part
            else:
                key_acc[:, cols] += key_part
                value_acc[:, cols] += value_part
    proj_grad[1] = key_acc[...].astype(BF16)
    proj_grad[2] = value_acc[...].astype(BF16)
    loads[4].wait()
    loads[5].wait()
    for p in range(2, pieces):
        half = slice((p % 2) * rows_here, (p % 2 + 1) * rows_here)
        dense[p] = dot(normed[:, half], proj_grad[p // 2 - 1], ((0,), (0,))).astype(BF16)
        reduce_start(p)
    half = tokens // 2

    def part_rows(k):
        return pl.ds(k * half, half)

    def pair_copy(d, k):
        return remote(
            part.at[shard(d, 1 - core), part_rows(k), :], mate_in.at[d, part_rows(k), :], part_sems.at[0], (d, k), mate
        )

    def line_copy(d, k):
        return remote(
            line_out.at[d, part_rows(k), :], line_in.at[d, part_rows(k), :], part_sems.at[1], (d, k),
            {"tensor": shard(d, core)},
        )

    for k in range(2):
        rows = slice(k * half, (k + 1) * half)
        total = dot(proj_grad[0, rows, :], w_qkv[0], ((1,), (1,)))
        for n in range(1, 3):
            total = total + dot(proj_grad[n, rows, :], w_qkv[n], ((1,), (1,)))
        low = total.astype(BF16)
        for s in range(shards):
            part[s, rows, :] = low[:, s * share : (s + 1) * share]
        for d in range(lines):
            pair_copy(d, k).start()
    def advance(step):
        for lag, work in enumerate((reduce_y, reduce_half, reduce_block, spread_block, spread_half)):
            if 0 <= step - lag < pieces:
                work(step - lag)

    advance(0)

    def pair_sum(d, rows):
        return part[shard(d, core), rows, :].astype(F32) + mate_in[d, rows, :].astype(F32)

    for k in range(2):
        rows = part_rows(k)
        for d in range(lines):
            landed(mate_in.at[d, rows, :], part_sems.at[0], (d, k))
        for d in range(1, lines):
            line_out[d, rows, :] = pair_sum(d, rows).astype(BF16)
            line_copy(d, k).start()
    for h in range(heads):
        total = diag[h]
        size = TILE // 2
        while size >= 1:
            total = total[:size] + pltpu.roll(total[size : 2 * size], SPAN - size, 1)
            size //= 2
        row = jnp.broadcast_to(total, (8, SPAN))
        high = row.astype(BF16)
        middle = (row - high.astype(F32)).astype(BF16)
        low = (row - high.astype(F32) - middle.astype(F32)).astype(BF16)
        table = dot(high, onehot[...]) + dot(middle, onehot[...]) + dot(low, onehot[...])
        extras[0, experts + 4 + h : experts + 5 + h, : onehot.shape[1]] = table[:1]
    for step in range(1, 4):
        advance(step)

    total = pair_sum(0, pl.ds(0, tokens))
    for k in range(2):
        for d in range(1, lines):
            landed(line_in.at[d, part_rows(k), :], part_sems.at[1], (d, k))
    for d in range(1, lines):
        total = total + line_in[d].astype(F32)
    scale_one = scales[:, 0:1]
    loads[6].wait()
    values = residual[...].astype(F32)
    weighted = total * gain_one[:, mine]
    dot_send(1, jnp.sum(weighted * values, axis=1, keepdims=True))
    extras[0, experts : experts + 1, :] = jnp.sum(total * values * scale_one, axis=0, keepdims=True)

    def extras_copy(i):
        return remote(extras.at[0], extras_in_dp.at[i], extras_sems, (i,), {"dp": group(i)})

    for i in range(1, groups):
        extras_copy(i).start()
    advance(4)
    along = dot_sum(1)
    input_grad[...] = grad_here[...] + scale_one * (weighted - values * (scale_one * scale_one * along * inverse))
    for step in range(5, pieces + 4):
        advance(step)

    summed = extras[0]
    for i in range(1, groups):
        extras_copy(i).wait()
        summed = summed + extras_in_dp[i]
    extras_out[place] = summed

    def ring_copy(i):
        return remote(extras_out.at[place], extras_out.at[place], extras_ring_sems, (i,), {"tensor": near(i)})

    for i in range(1, shards):
        ring_copy(i).start()
    for p in range(pieces):
        spread_y(p)
    for i in range(1, shards):
        landed(extras_out.at[near(shards - i)], extras_ring_sems, (i,))
        ring_copy(i).wait_send()
    for j in range(blocks):
        for d in range(lines):
            if d:
                branch_line(d, j).wait_send()
            branch_mate(d, j).wait_send()
    for k in range(2):
        for d in range(lines):
            if d:
                line_copy(d, k).wait_send()
            pair_copy(d, k).wait_send()
    for p in range(pieces):
        for copy in (half_copy(p), block_copy(p), block_spread(p), half_spread(p)):
            copy.wait_send()
        for a in range(1, y_size):
            y_spread(p, a).wait_send()
        for copy in save(p):
            copy.wait()


def body(
    inputs,
    teacher,
    lengths,
    expert_ids,
    route_slots,
    gain_attn,
    w_qkv,
    w_out,
    rel_table,
    gain_moe,
    w_router,
    w_gate_up,
    w_down,
):
    highest = lax.Precision.HIGHEST
    tok_rows, model_width = inputs.shape
    groups = lax.axis_size("dp")
    shards = lax.axis_size("tensor")
    experts = w_router.shape[1]
    local_experts = w_gate_up.shape[0]
    capacity = 10 * tok_rows // (4 * experts)
    padded_cap = (capacity + 15) // 16 * 16
    slot_count = experts * padded_cap
    heads_here = rel_table.shape[1]
    width_here = w_qkv.shape[2]
    head_width = width_here // heads_here
    share = model_width // shards

    offsets = jnp.arange(SPAN, dtype=jnp.int32) - SEQ_LEN
    onehot_offsets = bucket_onehot(offsets)
    offset_bias = jnp.dot(onehot_offsets, rel_table, precision=highest).T
    lines = shards // 2
    blocks = tok_rows // TILE
    ids = expert_ids.T
    gain_one, gain_two = gain_attn.reshape(1, model_width), gain_moe.reshape(1, model_width)
    router_t = w_router.T
    normed_low, projected, probs, attended, after_mine, normed_mine, columns = staged_call(
        functools.partial(dense_forward, groups, shards, heads_here, head_width, experts),
        "svvvvvaaa",
        (lengths, offset_bias, ids, gain_one, gain_two, router_t, inputs, w_qkv, w_out),
        (
            jax.ShapeDtypeStruct((tok_rows, model_width), BF16),
            jax.ShapeDtypeStruct((3, tok_rows, width_here), BF16),
            jax.ShapeDtypeStruct((heads_here, SEQ_LEN, SEQ_LEN), F32),
            jax.ShapeDtypeStruct((tok_rows, width_here), BF16),
            jax.ShapeDtypeStruct((tok_rows, share), F32),
            jax.ShapeDtypeStruct((tok_rows, share), BF16),
            jax.ShapeDtypeStruct((tok_rows, 128), F32),
        ),
        "aaaavvv",
        [
            pltpu.VMEM((tok_rows, model_width), BF16),
            pltpu.VMEM(w_qkv.shape, BF16),
            pltpu.SemaphoreType.DMA((3,)),
            pltpu.VMEM((shards, width_here, model_width), BF16),
            pltpu.SemaphoreType.DMA((2, 2, lines)),
            pltpu.VMEM((shards, tok_rows, width_here), BF16),
            pltpu.SemaphoreType.DMA((2, 2, lines, blocks)),
            pltpu.VMEM((heads_here, TILE, SPAN), F32),
            pltpu.VMEM((tok_rows, model_width), BF16),
            pltpu.VMEM((3, tok_rows, width_here), BF16),
            pltpu.VMEM((heads_here, SEQ_LEN, SEQ_LEN), F32),
            pltpu.VMEM((TILE, model_width), F32),
            pltpu.VMEM((TILE, model_width), BF16),
            pltpu.SemaphoreType.DMA((4,)),
        ],
        60,
        4,
        "dense_forward",
    )
    gate_up_t = jnp.swapaxes(w_gate_up, 2, 3)
    chunk = max(groups // 4, 1)
    steps = groups // chunk
    slots = groups * padded_cap
    ff_here = w_down.shape[1]
    sizes = (groups, shards, local_experts, padded_cap)
    rows_shape = (shards, local_experts, slots, share)
    extra_rows = experts + 8
    token_type = jax.ShapeDtypeStruct((tok_rows, share), F32)
    block_part, out_grad, normed_two_grad, extras, info, expert_rows, expert_grad, pre_grads, hidden_low = staged_call(
        functools.partial(experts_both, *sizes, chunk, experts, capacity),
        "svvvvvvaaa",
        (lengths, normed_mine, after_mine, columns, route_slots.T, ids, router_t, teacher, gate_up_t, w_down),
        (
            token_type,
            token_type,
            token_type,
            jax.ShapeDtypeStruct((extra_rows, share), F32),
            jax.ShapeDtypeStruct((8, 128), F32),
            jax.ShapeDtypeStruct(rows_shape, BF16),
            jax.ShapeDtypeStruct(rows_shape, BF16),
            jax.ShapeDtypeStruct((2, local_experts, slots, ff_here), BF16),
            jax.ShapeDtypeStruct((local_experts, slots, ff_here), BF16),
        ),
        "vvvvvaaaa",
        [
            pltpu.VMEM((tok_rows, share), BF16),
            pltpu.VMEM(gate_up_t.shape, BF16),
            pltpu.VMEM(w_down.shape, BF16),
            pltpu.VMEM(rows_shape, BF16),
            pltpu.VMEM(rows_shape, BF16),
            pltpu.VMEM(rows_shape, BF16),
            pltpu.VMEM((2, local_experts, slots, ff_here), F32),
            pltpu.VMEM((local_experts, slots, ff_here), BF16),
            pltpu.VMEM((2, local_experts, slots, ff_here), BF16),
            pltpu.VMEM((2, tok_rows, share), F32),
            pltpu.VMEM((2 * tok_rows, share), BF16),
            pltpu.SemaphoreType.DMA((3,)),
            pltpu.SemaphoreType.DMA((4, steps)),
            pltpu.VMEM((groups, 8, 128), jnp.int32),
            pltpu.SemaphoreType.DMA((2, groups)),
            pltpu.VMEM((2, shards, 8, tok_rows), F32),
            pltpu.SemaphoreType.DMA((2, 2, shards)),
        ]
        + mover_scratch(*sizes, share) * 2,
        60,
        1,
        "experts_both",
    )

    y_size = 1 << ((groups.bit_length() - 1) // 2)
    z_size = groups // y_size
    pieces, piece_rows = 2 * (1 + 3), model_width // 2
    dense, out_proj, input_part, extras = staged_call(
        functools.partial(dense_backward, groups, shards, heads_here, head_width, experts),
        "vvvvvvvv" + "aaaaaaa",
        (
            normed_two_grad,
            after_mine,
            out_grad,
            columns,
            gain_one,
            gain_two,
            extras,
            onehot_offsets.astype(BF16),
            inputs,
            attended,
            w_out,
            projected,
            probs,
            normed_low,
            w_qkv,
        ),
        (
            jax.ShapeDtypeStruct((pieces - 2, piece_rows, width_here), BF16),
            jax.ShapeDtypeStruct((width_here, model_width), BF16),
            jax.ShapeDtypeStruct((tok_rows, share), F32),
            jax.ShapeDtypeStruct((shards, extra_rows, share), F32),
        ),
        "aavv",
        [
            pltpu.VMEM((tok_rows, share), BF16),
            pltpu.VMEM(attended.shape, BF16),
            pltpu.VMEM(w_out.shape, BF16),
            pltpu.VMEM(projected.shape, BF16),
            pltpu.VMEM(probs.shape, F32),
            pltpu.VMEM(normed_low.shape, BF16),
            pltpu.VMEM(w_qkv.shape, BF16),
            pltpu.SemaphoreType.DMA((7,)),
            pltpu.VMEM((2, shards, 8, tok_rows), F32),
            pltpu.SemaphoreType.DMA((2, 2, shards)),
            pltpu.VMEM((shards, tok_rows, share), BF16),
            pltpu.SemaphoreType.DMA((2, 2, lines, blocks)),
            pltpu.VMEM((tok_rows, share), F32),
            pltpu.VMEM((heads_here, TILE, SPAN), F32),
            pltpu.VMEM((SEQ_LEN, width_here), F32),
            pltpu.VMEM((SEQ_LEN, width_here), F32),
            pltpu.VMEM((3, tok_rows, width_here), BF16),
            pltpu.VMEM((shards, tok_rows, share), BF16),
            pltpu.VMEM((lines, tok_rows, share), BF16),
            pltpu.VMEM((lines, tok_rows, share), BF16),
            pltpu.VMEM((lines, tok_rows, share), BF16),
            pltpu.SemaphoreType.DMA((2, 2, lines, 2)),
            pltpu.VMEM((pieces, piece_rows, width_here), BF16),
            pltpu.VMEM((pieces, piece_rows, width_here), BF16),
            pltpu.VMEM((pieces, y_size, piece_rows // y_size, width_here), BF16),
            pltpu.VMEM((pieces, piece_rows // y_size, width_here), BF16),
            pltpu.VMEM((pieces, piece_rows // y_size // 2, width_here), BF16),
            pltpu.VMEM((pieces, piece_rows // y_size // 2, width_here), BF16),
            pltpu.VMEM((pieces, piece_rows // groups, width_here), BF16),
            pltpu.SemaphoreType.DMA((2, 2, pieces, y_size)),
            pltpu.SemaphoreType.DMA((2, 2, pieces, 2)),
            pltpu.SemaphoreType.DMA((pieces, max(shards // 2, 1))),
            pltpu.VMEM((1, extra_rows, share), F32),
            pltpu.VMEM((groups, extra_rows, share), F32),
            pltpu.SemaphoreType.DMA((2, groups)),
            pltpu.SemaphoreType.DMA((2, shards)),
        ],
        60,
        3,
        "dense_backward",
    )
    def whole(shape):
        return pl.BlockSpec(shape, lambda e, j: (0,) * len(shape))

    row_type = jax.ShapeDtypeStruct((1, model_width), F32)
    piece = pl.BlockSpec((1, piece_rows, width_here), lambda e, j: (e * 3 + j, 0, 0))
    results = pl.pallas_call(
        functools.partial(weight_grads, shards, heads_here, experts),
        grid=(local_experts, 3),
        out_shape=(
            jax.ShapeDtypeStruct(gate_up_t.shape, F32),
            jax.ShapeDtypeStruct(w_down.shape, F32),
            jax.ShapeDtypeStruct(dense.shape, F32),
            jax.ShapeDtypeStruct(out_proj.shape, F32),
            jax.ShapeDtypeStruct((experts, model_width), F32),
            row_type,
            row_type,
            jax.ShapeDtypeStruct((heads_here, BUCKETS), F32),
            jax.ShapeDtypeStruct((1, 1), F32),
            token_type,
            token_type,
        ),
        in_specs=[
            pl.BlockSpec((shards, None, slots, share), lambda e, j: (0, e, 0, 0)),
            pl.BlockSpec((shards, None, slots, share), lambda e, j: (0, e, 0, 0)),
            pl.BlockSpec((None, None, slots, ff_here), lambda e, j: (jnp.minimum(j, 1), e, 0, 0)),
            pl.BlockSpec((None, slots, ff_here), lambda e, j: (e, 0, 0)),
            piece,
            whole(out_proj.shape),
            whole(extras.shape),
            whole(info.shape),
            whole(token_type.shape),
            whole(token_type.shape),
        ],
        out_specs=(
            pl.BlockSpec((None, None, ff_here, model_width), lambda e, j: (e, jnp.minimum(j, 1), 0, 0)),
            pl.BlockSpec((None, ff_here, model_width), lambda e, j: (e, 0, 0)),
            piece,
            whole(out_proj.shape),
            whole((experts, model_width)),
            whole((1, model_width)),
            whole((1, model_width)),
            whole((heads_here, BUCKETS)),
            whole((1, 1)),
            whole(token_type.shape),
            whole(token_type.shape),
        ),
        compiler_params=pltpu.CompilerParams(vmem_limit_bytes=56 * 1024 * 1024),
        name="weight_grads",
    )(expert_rows, expert_grad, pre_grads, hidden_low, dense, out_proj, extras, info, block_part, input_part)
    gate_up_grad, down_grad, dense_sum, out_proj_sum, router_sum, gain_one_sum, gain_two_sum, table_sum = results[:8]
    loss, block_out, input_grad = results[8:]
    return (
        block_out,
        loss.reshape(()),
        input_grad,
        gain_one_sum.reshape(model_width),
        dense_sum.reshape(w_qkv.shape),
        out_proj_sum,
        table_sum.T,
        gain_two_sum.reshape(model_width),
        router_sum.T,
        jnp.swapaxes(gate_up_grad, 2, 3),
        down_grad,
    )


def solution(mesh):
    placed = (
        P("dp", None),
        P("dp", None),
        P("dp"),
        P("dp", None),
        P("dp", None),
        P(),
        P(None, None, "tensor"),
        P("tensor", None),
        P(None, "tensor"),
        P(),
        P(),
        P("dp", None, None, "tensor"),
        P("dp", "tensor", None),
    )
    return jax.shard_map(
        body,
        mesh=mesh,
        in_specs=placed,
        out_specs=(
            P("dp", "tensor"),
            P(),
            P("dp", "tensor"),
            P(),
            P(None, None, "tensor"),
            P("tensor", None),
            P(None, "tensor"),
            P(),
            P(),
            P("dp", None, None, "tensor"),
            P("dp", "tensor", None),
        ),
        check_vma=False,
    )
```
